128 devices in a mesh: bx: 4 (over y_hi, core), by: 32 (over x, z, y_lo).
Axes of the slice: x: 4, y: 4 (y_hi: 2, y_lo: 2; y = y_hi * 2 + y_lo), z: 4, core: 2. Of those that a mesh axis runs over, the one named last changes fastest.
Arguments:
- features: bfloat16 [16384, 256], P(('bx', 'by')), may hold values from -6 to 6
- depth_logits: float32 [64, 16384], P(None, ('bx', 'by')), may hold values from -300 to 300
- ctx_weight: bfloat16 [256, 128], replicated, may hold values from -0.375 to 0.375
- point_pixel: int32 [524288], P(('bx', 'by')), may hold values from 0 to 127
- point_bin: int32 [524288], P(('bx', 'by')), may hold values from 0 to 63
- segment_count: int32 [128, 128], P(('bx', 'by')), may hold values from 0 to 64, as said below
- slot_cell: int32 [128, 128, 64], P(('bx', 'by')), may hold values from 0 to 8191
- conv_weight: bfloat16 [3, 3, 128, 128], replicated, may hold values from -0.1875 to 0.1875
- proj_weight: bfloat16 [128, 6], replicated, may hold values from -0.5 to 0.5
- level_count: int32 [6], replicated, may hold values from 3 to 8
- code_grad: float32 [6, 512, 2048], P(None, 'bx', 'by'), may hold values from -6 to 6
Outputs:
- fsq_codes: float32 [6, 512, 2048], P(None, 'bx', 'by')
- grad_logits: float32 [64, 16384], P(None, ('bx', 'by'))
- grad_features: bfloat16 [16384, 256], P(('bx', 'by'))
- grad_conv: float32 [3, 3, 128, 128], replicated
- grad_proj: float32 [128, 6], replicated
The draws below stay inside these ranges and needn't reach their ends.
Inputs may be any that keep to these rules, and one draw needn't show every extreme that they name: `segment_count`: entry [s, d] is the number of device s's points bound for tile d; each row sums to 4096; some tile receives 64 points from every device. `slot_cell`: entry [d, s, j] is the row-major cell within tile d of the j-th point that device s sends to tile d; entries with j at or beyond segment_count[s, d] are unused.
All inputs are finite; a program needn't handle non-finite values.
Results may differ from the reference program's by a relative error of at most 0.011.
Values may be sent and summed in bfloat16 or wider, within the bound.
A program may use at most 128 MiB of HBM per device.

```python
import jax
import jax.numpy as jnp
from jax import lax

CI = 256
DB = 64
C = 128
FQ = 6
TX = 128
TY = 64
PIX_DEV = 128
CAP = 64
PTS_DEV = 4096
PIX = 16384
GX = 512
GY = 2048
N_BX = 4
N_BY = 32
DEVICES = 128


def draw_depth_logits(key, part):
    key = jax.random.fold_in(key, 5)
    base_key = jax.random.fold_in(key, 0)
    logits = jnp.clip(jax.random.normal(base_key, (DB, PIX), jnp.float32) * 2.0, -8.0, 8.0)
    return logits


def draw_segment_count(key, part):
    key = jax.random.fold_in(key, 7)
    hot_key, noise_key, split_key = jax.random.split(key, 3)
    hot_tile = jax.random.randint(hot_key, (), 0, DEVICES)
    noise_bits = jax.random.randint(noise_key, (DEVICES, DEVICES), 0, 1 << 20)
    tile_ids = jnp.arange(DEVICES, dtype=jnp.int32)
    scores = noise_bits * DEVICES + tile_ids[None, :]
    scores = jnp.where(tile_ids[None, :] == hot_tile, jnp.int32(1 << 30), scores)
    ranked = jnp.argsort(-scores, axis=1, stable=True)
    pair_count = (DEVICES - 1) // 2
    spread_up = jax.random.randint(split_key, (DEVICES, pair_count), 0, CAP // 2)
    larger = CAP // 2 + spread_up
    smaller = CAP - larger
    paired = jnp.stack([larger, smaller], axis=2).reshape(DEVICES, 2 * pair_count)
    by_rank = jnp.concatenate([jnp.full((DEVICES, 1), CAP, jnp.int32), paired.astype(jnp.int32), jnp.zeros((DEVICES, DEVICES - 1 - 2 * pair_count), jnp.int32)], axis=1)
    rank_of = jnp.argsort(ranked, axis=1, stable=True)
    return jnp.take_along_axis(by_rank, rank_of, axis=1).astype(jnp.int32)


def set_ends(array, stream_key, low, top_value):
    longest = array.shape.index(max(array.shape))
    spots = []
    for shift in (0, 1):
        where = [jax.random.randint(jax.random.fold_in(stream_key, axis), (), 0, length) for axis, length in enumerate(array.shape)]
        where[longest] = (where[longest] + shift) % array.shape[longest]
        spots.append(tuple(where))
    return array.at[spots[0]].set(low).at[spots[1]].set(top_value)


def block_scale(rng, shape, pieces, smallest, top_value):
    factor_of = 1.0
    for dim, shards_of in pieces:
        steps = jax.random.uniform(jax.random.fold_in(jax.random.fold_in(rng, 6), dim), (shards_of,), jnp.float32, smallest / len(pieces), top_value / len(pieces))
        factor_of = factor_of * jnp.repeat(jnp.exp(steps), shape[dim] // shards_of).reshape((-1,) + (1,) * (len(shape) - 1 - dim))
    return factor_of


def bell_draw(stream_key, dims, scale, most, cuts=(), held_as=jnp.bfloat16):
    loudness = block_scale(stream_key, dims, cuts, -0.22, 0.18) if cuts else 1.0
    entries = jax.random.normal(stream_key, dims, jnp.float32) * scale * loudness
    return jnp.minimum(jnp.maximum(entries, -most), most).astype(held_as)


def setup_inputs(seed: int = 0) -> dict:
    key_of = jax.random.split(jax.random.key(seed), 12)
    features = bell_draw(key_of[0], (PIX, CI), 1.0, 6.0, ((0, 128),))
    depth_logits = draw_depth_logits(jax.random.fold_in(key_of[11], 71), 0)
    ctx_weight = bell_draw(key_of[2], (CI, C), CI ** -0.5, 0.375)
    point_pixel = set_ends(jax.random.randint(key_of[3], (DEVICES * PTS_DEV,), 0, PIX_DEV), jax.random.fold_in(key_of[3], 1), 0, PIX_DEV - 1).astype(jnp.int32)
    point_bin = set_ends(jax.random.randint(key_of[4], (DEVICES * PTS_DEV,), 0, DB), jax.random.fold_in(key_of[4], 1), 0, DB - 1).astype(jnp.int32)
    segment_count = draw_segment_count(jax.random.fold_in(key_of[11], 71), 0)
    slot_cell = set_ends(jax.random.randint(key_of[6], (DEVICES, DEVICES, CAP), 0, TX * TY), jax.random.fold_in(key_of[6], 1), 0, (TX * TY) - 1).astype(jnp.int32)
    conv_weight = bell_draw(key_of[7], (3, 3, C, C), (9 * C) ** -0.5, 0.1875)
    proj_weight = bell_draw(key_of[8], (C, FQ), C ** -0.5, 0.5)
    level_count = set_ends(jax.random.randint(key_of[9], (FQ,), 3, 9), jax.random.fold_in(key_of[9], 1), 3, 8).astype(jnp.int32)
    code_grad = bell_draw(key_of[10], (FQ, GX, GY), 1.0, 6.0, ((1, 4), (2, 32)), jnp.float32)
    return dict(features=features, depth_logits=depth_logits, ctx_weight=ctx_weight, point_pixel=point_pixel, point_bin=point_bin, segment_count=segment_count, slot_cell=slot_cell, conv_weight=conv_weight, proj_weight=proj_weight, level_count=level_count, code_grad=code_grad)


epsilon = 1e-05

def wide_dot(left, right):
    return jnp.dot(left.astype(jnp.float32), right.astype(jnp.float32), precision=lax.Precision.HIGHEST)

def plane_dot(window, weight):
    rows, cols, depth = window.shape
    flat = wide_dot(window.reshape(rows * cols, depth), weight)
    return flat.reshape(rows, cols, weight.shape[1])

def conv_taps(padded, weight, tile_rows, tile_cols):
    summed = jnp.zeros((tile_rows, tile_cols, weight.shape[3]), jnp.float32)
    for row_tap in range(3):
        for col_tap in range(3):
            window = padded[row_tap:row_tap + tile_rows, col_tap:col_tap + tile_cols, :]
            summed = summed + plane_dot(window, weight[row_tap, col_tap])
    return summed

def conv_back(padded_grad, weight, tile_rows, tile_cols):
    summed = jnp.zeros((tile_rows, tile_cols, weight.shape[2]), jnp.float32)
    for row_tap in range(3):
        for col_tap in range(3):
            window = padded_grad[2 - row_tap:2 - row_tap + tile_rows, 2 - col_tap:2 - col_tap + tile_cols, :]
            summed = summed + plane_dot(window, weight[row_tap, col_tap].T)
    return summed

def conv_weights_grad(padded, conv_grad, tile_rows, tile_cols):
    depth = padded.shape[2]
    grad_flat = conv_grad.reshape(tile_rows * tile_cols, conv_grad.shape[2]).astype(jnp.float32)
    stacked = []
    for row_tap in range(3):
        line = []
        for col_tap in range(3):
            window = padded[row_tap:row_tap + tile_rows, col_tap:col_tap + tile_cols, :].reshape(tile_rows * tile_cols, depth).astype(jnp.float32)
            line.append(lax.dot_general(window, grad_flat, (((0,), (0,)), ((), ())), precision=lax.Precision.HIGHEST))
        stacked.append(jnp.stack(line))
    return jnp.stack(stacked)

def encode_tile(padded, conv_weight, proj_weight, level_count, code_grad, tile_rows, tile_cols):
    conv_out = conv_taps(padded, conv_weight, tile_rows, tile_cols)
    inv_rms = lax.rsqrt(lax.optimization_barrier(jnp.mean(conv_out * conv_out, axis=-1, keepdims=True)) + epsilon)
    normed = conv_out * inv_rms
    hidden = jax.nn.silu(normed).astype(jnp.bfloat16)
    channels = hidden.shape[2]
    code_dims = proj_weight.shape[1]
    hidden_flat = hidden.reshape(tile_rows * tile_cols, channels)
    latent = wide_dot(hidden_flat, proj_weight).T.reshape(code_dims, tile_rows, tile_cols)
    half_levels = (level_count.astype(jnp.float32) - 1.0) * 0.5
    squash = jnp.tanh(latent)
    fsq_codes = half_levels[:, None, None] * squash
    code_slope = code_grad * half_levels[:, None, None] * (1.0 - squash * squash)
    slope_flat = code_slope.reshape(code_dims, tile_rows * tile_cols)
    proj_part = jnp.dot(hidden_flat.astype(jnp.float32).T, slope_flat.T, precision=lax.Precision.HIGHEST)
    hidden_grad = jnp.dot(slope_flat.T, proj_weight.astype(jnp.float32).T, precision=lax.Precision.HIGHEST).reshape(tile_rows, tile_cols, channels)
    gate_sig = jax.nn.sigmoid(normed)
    norm_grad = hidden_grad * gate_sig * (1.0 + normed * (1.0 - gate_sig))
    mixed_term = lax.optimization_barrier(jnp.mean(norm_grad * conv_out, axis=-1, keepdims=True))
    conv_grad = (inv_rms * norm_grad - conv_out * inv_rms * inv_rms * inv_rms * mixed_term).astype(jnp.bfloat16)
    return (fsq_codes, proj_part, conv_grad)

def point_values(counts, pixel_list, depth_list, depth_prob, context, capacity):
    starts = jnp.cumsum(counts) - counts
    slot_lane = jnp.arange(capacity, dtype=jnp.int32)
    slot_index = jnp.minimum(starts[:, None] + slot_lane[None, :], pixel_list.shape[0] - 1)
    usable = slot_lane[None, :] < counts[:, None]
    pixels = pixel_list[slot_index]
    depths = depth_list[slot_index]
    point_weight = jnp.where(usable, depth_prob[depths, pixels], 0.0)
    ctx_rows = context[pixels].astype(jnp.float32)
    return (pixels, depths, usable, point_weight, ctx_rows)

def point_grads(back_grads, pixels, depths, usable, point_weight, ctx_rows, depth_prob, ctx_weight):
    pix_count = depth_prob.shape[1]
    bin_count = depth_prob.shape[0]
    channels = ctx_rows.shape[2]
    grads_f = back_grads.astype(jnp.float32)
    pair_dot = jnp.where(usable, lax.optimization_barrier(jnp.sum(grads_f * ctx_rows, axis=-1)), 0.0)
    flat_pair = (depths * pix_count + pixels).reshape(-1)
    prob_grad = jax.ops.segment_sum(pair_dot.reshape(-1), flat_pair, num_segments=bin_count * pix_count).reshape(bin_count, pix_count)
    ctx_grad = jax.ops.segment_sum((point_weight[..., None] * grads_f).reshape(-1, channels), pixels.reshape(-1), num_segments=pix_count).astype(jnp.bfloat16)
    logit_grad = depth_prob * (prob_grad - lax.optimization_barrier(jnp.sum(depth_prob * prob_grad, axis=0, keepdims=True)))
    feature_grad = wide_dot(ctx_grad, ctx_weight.T).astype(jnp.bfloat16)
    return (logit_grad, feature_grad)

def tiles_to_grid(stacked):
    return stacked.reshape(N_BX, N_BY, TX, TY, -1).transpose(0, 2, 1, 3, 4).reshape(GX, GY, -1)

def reference(features, depth_logits, ctx_weight, point_pixel, point_bin, segment_count, slot_cell, conv_weight, proj_weight, level_count, code_grad):
    devices = N_BX * N_BY
    depth_prob = jax.nn.softmax(depth_logits, axis=0)
    context = wide_dot(features, ctx_weight).astype(jnp.bfloat16)
    prob_blocks = depth_prob.reshape(DB, devices, PIX_DEV).transpose(1, 0, 2)
    ctx_blocks = context.reshape(devices, PIX_DEV, C)
    pixel_lists = point_pixel.reshape(devices, PTS_DEV)
    depth_lists = point_bin.reshape(devices, PTS_DEV)
    tile_ids = jnp.arange(devices, dtype=jnp.int32)
    anchor = tile_ids // N_BY * (TX * GY) + tile_ids % N_BY * TY

    def to_global(targets):
        return anchor[:, None] + targets // TY * GY + targets % TY

    def lift_sender(bev_grid, sender):
        pixels, depths, usable, point_weight, ctx_rows = point_values(segment_count[sender], pixel_lists[sender], depth_lists[sender], prob_blocks[sender], ctx_blocks[sender], CAP)
        carried = (point_weight[..., None] * ctx_rows).astype(jnp.bfloat16)
        targets = to_global(slot_cell[:, sender, :]).reshape(-1)
        bev_grid = bev_grid.at[targets].add(carried.reshape(-1, C).astype(bev_grid.dtype))
        return (bev_grid, None)
    bev_grid, _ = lax.scan(lift_sender, jnp.zeros((GX * GY, C), jnp.float32), tile_ids)
    lifted = bev_grid.reshape(GX, GY, C).astype(jnp.bfloat16)
    padded = jnp.pad(lifted, ((1, 1), (1, 1), (0, 0)))
    zero_index = jnp.zeros((), jnp.int32)

    def tile_forward(tile):
        row_start = (tile // N_BY * TX).astype(jnp.int32)
        col_start = (tile % N_BY * TY).astype(jnp.int32)
        pad_tile = lax.dynamic_slice(padded, (row_start, col_start, zero_index), (TX + 2, TY + 2, C))
        code_tile = lax.dynamic_slice(code_grad, (zero_index, row_start, col_start), (FQ, TX, TY))
        fsq_tile, proj_part, conv_grad = encode_tile(pad_tile, conv_weight, proj_weight, level_count, code_tile, TX, TY)
        weight_part = conv_weights_grad(pad_tile, conv_grad, TX, TY)
        return (fsq_tile, proj_part, conv_grad, weight_part)
    fsq_tiles, proj_parts, conv_grads, weight_parts = lax.map(tile_forward, tile_ids)
    fsq_codes = fsq_tiles.reshape(N_BX, N_BY, FQ, TX, TY).transpose(2, 0, 3, 1, 4).reshape(FQ, GX, GY)
    grad_proj = lax.optimization_barrier(jnp.sum(proj_parts, axis=0))
    grad_conv = lax.optimization_barrier(jnp.sum(weight_parts, axis=0))
    conv_grad = tiles_to_grid(conv_grads)
    padded_grad = jnp.pad(conv_grad, ((1, 1), (1, 1), (0, 0)))

    def tile_back(tile):
        row_start = (tile // N_BY * TX).astype(jnp.int32)
        col_start = (tile % N_BY * TY).astype(jnp.int32)
        pad_tile = lax.dynamic_slice(padded_grad, (row_start, col_start, zero_index), (TX + 2, TY + 2, C))
        return conv_back(pad_tile, conv_weight, TX, TY).astype(jnp.bfloat16)
    lift_grad = tiles_to_grid(lax.map(tile_back, tile_ids)).reshape(GX * GY, C)

    def return_sender(sender):
        pixels, depths, usable, point_weight, ctx_rows = point_values(segment_count[sender], pixel_lists[sender], depth_lists[sender], prob_blocks[sender], ctx_blocks[sender], CAP)
        back_grads = lift_grad[to_global(slot_cell[:, sender, :])]
        return point_grads(back_grads, pixels, depths, usable, point_weight, ctx_rows, prob_blocks[sender], ctx_weight)
    logit_blocks, feature_blocks = lax.map(return_sender, tile_ids)
    grad_logits = logit_blocks.transpose(1, 0, 2).reshape(DB, PIX)
    grad_features = feature_blocks.reshape(PIX, CI)
    return (fsq_codes, grad_logits, grad_features, grad_conv, grad_proj)
```

```python
import functools

import jax
import jax.numpy as jnp
from jax import lax
from jax.experimental import pallas as pl
from jax.experimental.pallas import tpu as pltpu
from jax.sharding import PartitionSpec as P

epsilon = 1e-05
MESH = pl.DeviceIdType.MESH
F32 = jnp.float32
BF16 = jnp.bfloat16
VMEM_LIMIT = 60 * 2**20
NT = (((1,), (1,)), ((), ()))
TN = (((0,), (0,)), ((), ()))
PITCH = 80
DIRECTIONS = ((-1, 0), (1, 0), (0, -1), (0, 1), (-1, -1), (-1, 1), (1, -1), (1, 1))


def dot(left, right, dims=(((1,), (0,)), ((), ()))):
    return lax.dot_general(left, right, dims, preferred_element_type=F32)


def halves(value):
    high = value.astype(BF16)
    return high, (value - high.astype(F32)).astype(BF16)


def position():
    count = lax.axis_size("bx") * lax.axis_size("by")
    return lax.axis_index("bx") * lax.axis_size("by") + lax.axis_index("by"), count


def place(index):
    cols = lax.axis_size("by")
    return (lax.div(index, cols), lax.rem(index, cols))


def greet_all(me, count):
    barrier = pltpu.get_barrier_semaphore()

    def greet(step, carry):
        pl.semaphore_signal(
            barrier, inc=1, device_id=place(lax.rem(me + step, count)), device_id_type=MESH
        )
        return carry

    lax.fori_loop(1, count, greet, 0)
    return barrier


def lift_kernel(
    counts, features, logits, ctx_weight, pixels, bins,
    arrived, prob_out, ctx_out, weight_out,
    values, outgoing, starts, send_sem, recv_sem, own_sem,
):
    me, count = position()
    capacity = outgoing.shape[1]
    pix_count = ctx_out.shape[0]
    bin_count = prob_out.shape[0]
    barrier = greet_all(me, count)
    context = dot(features[...], ctx_weight[...]).astype(BF16)
    ctx_out[...] = context
    raw = logits[...]
    shifted = jnp.exp(raw - jnp.max(raw, axis=0, keepdims=True))
    prob = shifted / jnp.sum(shifted, axis=0, keepdims=True)
    prob_out[...] = prob
    prob_pair = jnp.concatenate(halves(prob), axis=1)
    ctx_pair = jnp.concatenate([context, context], axis=0)

    def start_of(tile, begin):
        starts[tile] = begin
        return begin + counts[0, tile]

    lax.fori_loop(0, count, start_of, 0)
    pix_lane = lax.broadcasted_iota(jnp.int32, (pix_count, 128), 0)
    bin_lane = lax.broadcasted_iota(jnp.int32, (bin_count, 128), 0)
    chunks = pixels.shape[0]
    group = 4

    def lift_chunk(step, carry):
        for part in range(group):
            chunk = step * group + part
            hot = pixels[pl.ds(chunk, 1), :] == pix_lane
            hot_b = jnp.where(hot, 1.0, 0.0).astype(BF16)
            picked = dot(prob_pair, jnp.concatenate([hot_b, hot_b], axis=0))
            weight = jnp.sum(
                jnp.where(bins[pl.ds(chunk, 1), :] == bin_lane, picked, 0.0), axis=0, keepdims=True
            )
            weight_out[pl.ds(chunk, 1), :] = weight
            spread = jnp.concatenate(halves(jnp.where(hot, weight, 0.0)), axis=0)
            values[pl.ds(pl.multiple_of(chunk * 128, 128), 128), :] = dot(spread, ctx_pair, TN)
        return carry

    lax.fori_loop(0, chunks // group, lift_chunk, 0)
    slot = lax.broadcasted_iota(jnp.int32, (capacity, 128), 0)
    values[pl.ds(chunks * 128, capacity), :] = jnp.zeros((capacity, 128), F32)

    def pack(tile):
        rows = values[pl.ds(starts[tile], capacity), :]
        outgoing[tile] = jnp.where(slot < counts[0, tile], rows, 0.0).astype(BF16)

    pl.semaphore_wait(barrier, count - 1)

    def send(step, carry):
        tile = lax.rem(me + step, count)
        pack(tile)
        pltpu.make_async_remote_copy(
            src_ref=outgoing.at[tile],
            dst_ref=arrived.at[me],
            send_sem=send_sem,
            recv_sem=recv_sem,
            device_id=place(tile),
            device_id_type=MESH,
        ).start()
        return carry

    lax.fori_loop(1, count, send, 0)
    pack(me)
    own = pltpu.make_async_copy(outgoing.at[me], arrived.at[me], own_sem)
    own.start()
    own.wait()
    others = pl.ds(0, count - 1)
    pltpu.make_async_copy(outgoing.at[others], outgoing.at[others], send_sem).wait()
    pltpu.make_async_copy(arrived.at[others], arrived.at[others], recv_sem).wait()


def lift(counts, features, logits, ctx_weight, pixels, bins, capacity):
    count = counts.shape[1]
    bin_count, pix_count = logits.shape
    channels = ctx_weight.shape[1]
    points = pixels.shape[0] * 128
    vmem = pl.BlockSpec(memory_space=pltpu.VMEM)
    return pl.pallas_call(
        lift_kernel,
        out_shape=(
            jax.ShapeDtypeStruct((count, capacity, channels), BF16),
            jax.ShapeDtypeStruct((bin_count, pix_count), F32),
            jax.ShapeDtypeStruct((pix_count, channels), BF16),
            jax.ShapeDtypeStruct(pixels.shape, F32),
        ),
        in_specs=[pl.BlockSpec(memory_space=pltpu.SMEM)] + [vmem] * 5,
        out_specs=(pl.BlockSpec(memory_space=pl.ANY), vmem, vmem, vmem),
        scratch_shapes=[
            pltpu.VMEM((points + capacity, channels), F32),
            pltpu.VMEM((count, capacity, channels), BF16),
            pltpu.SMEM((count,), jnp.int32),
            pltpu.SemaphoreType.DMA,
            pltpu.SemaphoreType.DMA,
            pltpu.SemaphoreType.DMA,
        ],
        compiler_params=pltpu.CompilerParams(
            collective_id=0, has_side_effects=True, vmem_limit_bytes=VMEM_LIMIT
        ),
        name="lift",
    )(counts, features, logits, ctx_weight, pixels, bins)


SUMS = 4


def pool_kernel(cells, arrived, lifted, *scratch):
    sums, stage = scratch[:SUMS], scratch[SUMS]
    count, capacity, channels = arrived.shape
    rows = lifted.shape[0]

    def clear(step, carry):
        at = pl.ds(pl.multiple_of(step * 128, 128), 128)
        for one in sums:
            one[at, :] = jnp.zeros((128, channels), F32)
        return carry

    lax.fori_loop(0, rows // 128, clear, 0)

    def add_block(sender, carry):
        stage[...] = arrived[sender].astype(F32)
        for slot in range(capacity):
            one = sums[slot % SUMS]
            cell = cells[sender, slot]
            one[pl.ds(cell, 1), :] = one[pl.ds(cell, 1), :] + stage[pl.ds(slot, 1), :]
        return carry

    lax.fori_loop(0, count, add_block, 0)

    def finish(step, carry):
        at = pl.ds(pl.multiple_of(step * 128, 128), 128)
        total = sums[0][at, :]
        for one in sums[1:]:
            total = total + one[at, :]
        lifted[at, :] = total.astype(BF16)
        return carry

    lax.fori_loop(0, rows // 128, finish, 0)


def pool(cells, arrived, rows):
    count, capacity, channels = arrived.shape
    vmem = pl.BlockSpec(memory_space=pltpu.VMEM)
    return pl.pallas_call(
        pool_kernel,
        out_shape=jax.ShapeDtypeStruct((rows, channels), BF16),
        in_specs=[pl.BlockSpec(memory_space=pltpu.SMEM), vmem],
        out_specs=vmem,
        scratch_shapes=[pltpu.VMEM((rows, channels), F32) for _ in range(SUMS)]
        + [pltpu.VMEM((capacity, channels), F32)],
        compiler_params=pltpu.CompilerParams(vmem_limit_bytes=VMEM_LIMIT),
        name="pool",
    )(cells, arrived)


def point_kernel(
    counts, back, prob, context, weights, pixels, bins, ctx_weight,
    logit_grad, feature_grad,
    grads,
):
    count, capacity, channels = back.shape
    pix_count = context.shape[0]
    bin_count = prob.shape[0]

    def unpack(tile, begin):
        grads[pl.ds(begin, capacity), :] = back[tile].astype(F32)
        return begin + counts[0, tile]

    lax.fori_loop(0, count, unpack, 0)
    pix_lane = lax.broadcasted_iota(jnp.int32, (pix_count, 128), 0)
    bin_lane = lax.broadcasted_iota(jnp.int32, (bin_count, 128), 0)
    chunks = pixels.shape[0]
    group = 4
    ctx = context[...]

    def chunk_grads(step, carry):
        prob_grad, ctx_grad = carry
        for part in range(group):
            chunk = step * group + part
            grad = grads[pl.ds(pl.multiple_of(chunk * 128, 128), 128), :].astype(BF16)
            hot = pixels[pl.ds(chunk, 1), :] == pix_lane
            hot_b = jnp.where(hot, 1.0, 0.0).astype(BF16)
            pair = jnp.sum(jnp.where(hot, dot(ctx, grad, NT), 0.0), axis=0, keepdims=True)
            by_bin = jnp.where(bins[pl.ds(chunk, 1), :] == bin_lane, pair, 0.0)
            prob_grad = prob_grad + dot(
                jnp.concatenate(halves(by_bin), axis=1), jnp.concatenate([hot_b, hot_b], axis=1), NT
            )
            spread = jnp.concatenate(
                halves(jnp.where(hot, weights[pl.ds(chunk, 1), :], 0.0)), axis=1
            )
            ctx_grad = ctx_grad + dot(spread, jnp.concatenate([grad, grad], axis=0))
        return prob_grad, ctx_grad

    prob_grad, ctx_grad = lax.fori_loop(
        0,
        chunks // group,
        chunk_grads,
        (jnp.zeros((bin_count, pix_count), F32), jnp.zeros((pix_count, channels), F32)),
    )
    chance = prob[...]
    logit_grad[...] = chance * (prob_grad - jnp.sum(chance * prob_grad, axis=0, keepdims=True))
    feature_grad[...] = dot(ctx_grad.astype(BF16), ctx_weight[...], NT).astype(BF16)


def point_grads(counts, back, prob, context, weights, pixels, bins, ctx_weight):
    vmem = pl.BlockSpec(memory_space=pltpu.VMEM)
    capacity, channels = back.shape[1:]
    return pl.pallas_call(
        point_kernel,
        out_shape=(
            jax.ShapeDtypeStruct(prob.shape, F32),
            jax.ShapeDtypeStruct((context.shape[0], ctx_weight.shape[0]), BF16),
        ),
        in_specs=[pl.BlockSpec(memory_space=pltpu.SMEM)] + [vmem] * 7,
        out_specs=(vmem, vmem),
        scratch_shapes=[pltpu.VMEM((pixels.shape[0] * 128 + capacity, channels), F32)],
        compiler_params=pltpu.CompilerParams(vmem_limit_bytes=VMEM_LIMIT),
        name="point_grads",
    )(counts, back, prob, context, weights, pixels, bins, ctx_weight)


def grid_place():
    return lax.axis_index("bx"), lax.axis_index("by"), lax.axis_size("bx"), lax.axis_size("by")


def inside(dx, dy):
    bx, by, nx, ny = grid_place()
    x, y = bx + dx, by + dy
    return (x >= 0) & (x < nx) & (y >= 0) & (y < ny)


def halo_copies(top, bottom, sides, landed, send_sems, recv_sems):
    bx, by, _, _ = grid_place()
    depth = sides.shape[1]
    pieces = (
        (top, landed.at[0, pl.ds(0, top.shape[0])]),
        (bottom, landed.at[1, pl.ds(0, bottom.shape[0])]),
        (sides.at[0], landed.at[2]),
        (sides.at[1], landed.at[3]),
        (sides.at[0, pl.ds(0, 16)], landed.at[4, pl.ds(0, 16)]),
        (sides.at[1, pl.ds(0, 16)], landed.at[5, pl.ds(0, 16)]),
        (sides.at[0, pl.ds(depth - 16, 16)], landed.at[6, pl.ds(0, 16)]),
        (sides.at[1, pl.ds(depth - 16, 16)], landed.at[7, pl.ds(0, 16)]),
    )
    return [
        pltpu.make_async_remote_copy(
            src_ref=source,
            dst_ref=target,
            send_sem=send_sems.at[way],
            recv_sem=recv_sems.at[way],
            device_id=(bx + dx, by + dy),
            device_id_type=MESH,
        )
        for way, ((dx, dy), (source, target)) in enumerate(zip(DIRECTIONS, pieces))
    ]


def start_halo(copies):
    for (dx, dy), copy in zip(DIRECTIONS, copies):
        pl.when(inside(dx, dy))(copy.start)


def finish_halo(copies, landed, field, rows, cols):
    low = (rows + 1) * PITCH

    def lay(way):
        if way == 0:
            field[pl.ds(low + 8, cols), :] = landed[0, 0:cols].astype(F32)
        elif way == 1:
            field[pl.ds(8, cols), :] = landed[1, 0:cols].astype(F32)
        elif way == 2:
            field[pl.ds(PITCH + 8 + cols, rows, stride=PITCH), :] = landed[2].astype(F32)
        elif way == 3:
            field[pl.ds(PITCH + 7, rows, stride=PITCH), :] = landed[3].astype(F32)
        elif way == 4:
            field[pl.ds(low + 8 + cols, 1), :] = landed[4, 0:16].astype(F32)[0:1]
        elif way == 5:
            field[pl.ds(low + 7, 1), :] = landed[5, 0:16].astype(F32)[0:1]
        elif way == 6:
            field[pl.ds(8 + cols, 1), :] = landed[6, 0:16].astype(F32)[15:16]
        else:
            field[pl.ds(7, 1), :] = landed[7, 0:16].astype(F32)[15:16]

    for way, ((dx, dy), copy) in enumerate(zip(DIRECTIONS, copies)):

        def arrive(way=way, copy=copy):
            copy.wait_recv()
            lay(way)

        pl.when(inside(-dx, -dy))(arrive)
        pl.when(inside(dx, dy))(copy.wait_send)


def spread_columns(field, wide, rows, cols):
    channels = field.shape[1]

    def row(x, carry):
        base = pl.multiple_of(x * PITCH, 8)
        at = pl.ds(pl.multiple_of(x * cols, cols), cols)
        for shift in range(3):
            wide[at, pl.ds(shift * channels, channels)] = field[
                pl.ds(base + 7 + shift, cols), :
            ].astype(BF16)
        return carry

    lax.fori_loop(0, rows + 2, row, 0)


def tile_kernel(
    cells, lifted, weight, back_weight, proj, levels, code_grad,
    codes, back, sums_out,
    field, wide, wide_grad, lift_grad, sides, edges, landed, stage, outgoing, parts, gathered,
    halo_send, halo_recv, send_sem, recv_sem, part_send, part_recv, sum_send, sum_recv, own_sem,
):
    me, count = position()
    channels = lifted.shape[1]
    capacity = outgoing.shape[1]
    cols = edges.shape[1]
    rows = lifted.shape[0] // cols
    owners = parts.shape[0]
    code_dims = code_grad.shape[0]
    barrier = greet_all(me, count)

    zeros = jnp.zeros((PITCH, channels), F32)
    field[pl.ds(0, PITCH), :] = zeros
    field[pl.ds((rows + 1) * PITCH, PITCH), :] = zeros
    for column in (7, 8 + cols):
        field[pl.ds(PITCH + column, rows, stride=PITCH), :] = jnp.zeros((rows, channels), F32)

    def load_row(x, carry):
        field[pl.ds(pl.multiple_of((x + 1) * PITCH + 8, 8), cols), :] = lifted[
            pl.ds(pl.multiple_of(x * cols, cols), cols), :
        ].astype(F32)
        return carry

    lax.fori_loop(0, rows, load_row, 0)

    def fill_borders():
        sides[0] = field[pl.ds(PITCH + 8, rows, stride=PITCH), :].astype(BF16)
        sides[1] = field[pl.ds(PITCH + 7 + cols, rows, stride=PITCH), :].astype(BF16)
        edges[0] = field[pl.ds(PITCH + 8, cols), :].astype(BF16)
        edges[1] = field[pl.ds(rows * PITCH + 8, cols), :].astype(BF16)

    fill_borders()
    pl.semaphore_wait(barrier, count - 1)
    first = halo_copies(
        edges.at[0], edges.at[1], sides, landed.at[0], halo_send.at[0], halo_recv.at[0]
    )
    start_halo(first)
    finish_halo(first, landed.at[0], field, rows, cols)
    spread_columns(field, wide, rows, cols)

    block_rows = 8
    block = block_rows * cols
    half_levels = (levels[...].astype(F32) - 1.0) * 0.5
    proj_pair = proj[...]
    depth = 3 * channels

    def encode(step, proj_sum):
        origin = pl.multiple_of(step * block, block)
        conv_out = jnp.zeros((block, channels), F32)
        for tap in range(3):
            window = wide[pl.ds(origin + tap * cols, block), :]
            conv_out = conv_out + dot(window, weight[pl.ds(tap * depth, depth), :])
        inv_rms = lax.rsqrt(jnp.mean(conv_out * conv_out, axis=-1, keepdims=True) + epsilon)
        normed = conv_out * inv_rms
        gate = 1.0 / (1.0 + jnp.exp(-normed))
        hidden = (normed * gate).astype(BF16)
        squash = jnp.tanh(dot(proj_pair, hidden, NT)[:code_dims])
        codes[:, pl.ds(origin, block)] = half_levels * squash
        slope = code_grad[:, pl.ds(origin, block)] * half_levels * (1.0 - squash * squash)
        slope_high = slope.astype(BF16).astype(F32)
        slope_pair = jnp.concatenate([slope_high, slope - slope_high], axis=0).astype(BF16)
        proj_two = dot(slope_pair, hidden)
        proj_sum = proj_sum + proj_two[:code_dims] + proj_two[code_dims:]
        hidden_grad = dot(slope_pair, proj_pair, TN)
        norm_grad = hidden_grad * (gate * (1.0 + normed * (1.0 - gate)))
        mixed = jnp.mean(norm_grad * normed, axis=-1, keepdims=True)
        conv_grad = inv_rms * (norm_grad - normed * mixed)
        for r in range(block_rows):
            at = pl.multiple_of((step * block_rows + r + 1) * PITCH + 8, 8)
            field[pl.ds(at, cols), :] = conv_grad[r * cols : (r + 1) * cols]
        wide_grad[pl.ds(origin + cols, block), pl.ds(channels, channels)] = conv_grad.astype(BF16)
        return proj_sum

    proj_sum = lax.fori_loop(
        0, rows // block_rows, encode, jnp.zeros((code_dims, channels), F32)
    )
    fill_borders()
    second = halo_copies(
        edges.at[0], edges.at[1], sides, landed.at[1], halo_send.at[1], halo_recv.at[1]
    )
    start_halo(second)

    for tap in range(3):
        for third in range(3):
            first_part = (tap * 3 + third) * (channels // 16)
            span = 2048

            def add(step, total, tap=tap, third=third):
                origin = pl.multiple_of(step * span, span)
                window = wide[
                    pl.ds(origin + tap * cols, span), pl.ds(third * channels, channels)
                ]
                grad = wide_grad[pl.ds(origin + cols, span), pl.ds(channels, channels)]
                return total + dot(window, grad, TN)

            total = lax.fori_loop(
                0, rows * cols // span, add, jnp.zeros((channels, channels), F32)
            )
            parts[pl.ds(first_part, channels // 16)] = total.reshape(channels // 16, 16, channels)
    parts[owners - 1] = jnp.concatenate(
        [proj_sum, jnp.zeros((16 - code_dims, channels), F32)], axis=0
    )

    def share_of(device):
        return lax.rem(device * 45, count)

    def send_part(step, carry):
        target = lax.rem(me + step, count)
        share = share_of(target)

        @pl.when(share < owners)
        def _():
            pltpu.make_async_remote_copy(
                src_ref=parts.at[share],
                dst_ref=gathered.at[me],
                send_sem=part_send,
                recv_sem=part_recv,
                device_id=place(target),
                device_id_type=MESH,
            ).start()

        return carry

    lax.fori_loop(1, count, send_part, 0)

    finish_halo(second, landed.at[1], field, rows, cols)
    spread_columns(field, wide_grad, rows, cols)

    def conv_back(step, carry):
        origin = pl.multiple_of(step * block, block)
        total = jnp.zeros((block, channels), F32)
        for tap in range(3):
            window = wide_grad[pl.ds(origin + tap * cols, block), :]
            total = total + dot(window, back_weight[pl.ds(tap * depth, depth), :])
        lift_grad[pl.ds(origin, block), :] = total
        return carry

    lax.fori_loop(0, rows // block_rows, conv_back, 0)

    def pick(sender):
        for slot in range(capacity):
            stage[pl.ds(slot, 1), :] = lift_grad[pl.ds(cells[sender, slot], 1), :]
        outgoing[sender] = stage[...].astype(BF16)

    def send_back(step, carry):
        sender = lax.rem(me + step, count)
        pick(sender)
        pltpu.make_async_remote_copy(
            src_ref=outgoing.at[sender],
            dst_ref=back.at[me],
            send_sem=send_sem,
            recv_sem=recv_sem,
            device_id=place(sender),
            device_id_type=MESH,
        ).start()
        return carry

    lax.fori_loop(1, count, send_back, 0)
    pick(me)
    own = pltpu.make_async_copy(outgoing.at[me], back.at[me], own_sem)
    own.start()

    mine = share_of(me)
    others = pl.ds(0, count - 1)

    @pl.when(mine < owners)
    def _():
        pltpu.make_async_copy(gathered.at[others], gathered.at[others], part_recv).wait()
        gathered[me] = parts[mine]

        def add(source, total):
            return total + gathered[source]

        sums_out[mine] = lax.fori_loop(0, count, add, jnp.zeros((16, channels), F32))

        def send_sum(step, carry):
            pltpu.make_async_remote_copy(
                src_ref=sums_out.at[mine],
                dst_ref=sums_out.at[mine],
                send_sem=sum_send,
                recv_sem=sum_recv,
                device_id=place(lax.rem(me + step, count)),
                device_id_type=MESH,
            ).start()
            return carry

        lax.fori_loop(1, count, send_sum, 0)
        pltpu.make_async_copy(gathered.at[others], gathered.at[others], sum_send).wait()
        rest = pl.ds(0, owners - 1)
        pltpu.make_async_copy(parts.at[rest], parts.at[rest], part_send).wait()
        pltpu.make_async_copy(sums_out.at[rest], sums_out.at[rest], sum_recv).wait()

    @pl.when(mine >= owners)
    def _():
        pltpu.make_async_copy(parts, parts, part_send).wait()
        pltpu.make_async_copy(sums_out, sums_out, sum_recv).wait()

    own.wait()
    pltpu.make_async_copy(outgoing.at[others], outgoing.at[others], send_sem).wait()
    pltpu.make_async_copy(back.at[others], back.at[others], recv_sem).wait()


def tile_step(cells, lifted, weight, back_weight, proj, levels, code_grad, cols):
    count, capacity = cells.shape
    cells_all, channels = lifted.shape
    rows = cells_all // cols
    owners = weight.shape[0] // 16 + 1
    code_dims = code_grad.shape[0]
    vmem = pl.BlockSpec(memory_space=pltpu.VMEM)
    wide = pltpu.VMEM(((rows + 2) * cols, 3 * channels), BF16)
    return pl.pallas_call(
        tile_kernel,
        out_shape=(
            jax.ShapeDtypeStruct((code_dims, cells_all), F32),
            jax.ShapeDtypeStruct((count, capacity, channels), BF16),
            jax.ShapeDtypeStruct((owners, 16, channels), F32),
        ),
        in_specs=[pl.BlockSpec(memory_space=pltpu.SMEM)] + [vmem] * 6,
        out_specs=(vmem, pl.BlockSpec(memory_space=pl.ANY), vmem),
        scratch_shapes=[
            pltpu.VMEM(((rows + 2) * PITCH, channels), F32),
            wide,
            wide,
            pltpu.VMEM((cells_all, channels), F32),
            pltpu.VMEM((2, rows, channels), BF16),
            pltpu.VMEM((2, cols, channels), BF16),
            pltpu.VMEM((2, 8, rows, channels), BF16),
            pltpu.VMEM((capacity, channels), F32),
            pltpu.VMEM((count, capacity, channels), BF16),
            pltpu.VMEM((owners, 16, channels), F32),
            pltpu.VMEM((count, 16, channels), F32),
            pltpu.SemaphoreType.DMA((2, 8)),
            pltpu.SemaphoreType.DMA((2, 8)),
        ]
        + [pltpu.SemaphoreType.DMA] * 7,
        compiler_params=pltpu.CompilerParams(
            collective_id=1, has_side_effects=True, vmem_limit_bytes=VMEM_LIMIT
        ),
        name="tile_step",
    )(cells, lifted, weight, back_weight, proj, levels, code_grad)


def per_device(
    features,
    depth_logits,
    ctx_weight,
    point_pixel,
    point_bin,
    segment_count,
    slot_cell,
    conv_weight,
    proj_weight,
    level_count,
    code_grad,
):
    capacity = slot_cell.shape[2]
    code_dims, tile_rows, tile_cols = code_grad.shape
    channels = ctx_weight.shape[1]
    pixels = point_pixel.reshape(-1, 128)
    bins = point_bin.reshape(-1, 128)
    arrived, prob, context, weights = lift(
        segment_count, features, depth_logits, ctx_weight, pixels, bins, capacity
    )
    cells = slot_cell[0]
    lifted = pool(cells, arrived, tile_rows * tile_cols)
    spare = 8 - code_dims
    weight = conv_weight.reshape(9 * channels, channels)
    back_weight = conv_weight[::-1, ::-1].transpose(0, 1, 3, 2).reshape(9 * channels, channels)
    proj = jnp.pad(proj_weight.T, ((0, spare), (0, 0)))
    levels = jnp.pad(level_count, (0, spare), constant_values=1).reshape(8, 1)
    slopes = jnp.pad(code_grad.reshape(code_dims, -1), ((0, spare), (0, 0)))
    codes, back, sums = tile_step(
        cells,
        lifted,
        weight,
        back_weight,
        jnp.concatenate([proj, proj], axis=0),
        levels,
        slopes,
        tile_cols,
    )
    grad_logits, grad_features = point_grads(
        segment_count, back, prob, context, weights, pixels, bins, ctx_weight
    )
    grad_conv = sums[:-1].reshape(conv_weight.shape)
    grad_proj = sums[-1, :code_dims].T
    fsq_codes = codes[:code_dims].reshape(code_dims, tile_rows, tile_cols)
    return (fsq_codes, grad_logits, grad_features, grad_conv, grad_proj)


def solution(mesh):
    return jax.shard_map(
        per_device,
        mesh=mesh,
        in_specs=(
            P(("bx", "by"), None),
            P(None, ("bx", "by")),
            P(),
            P(("bx", "by")),
            P(("bx", "by")),
            P(("bx", "by"), None),
            P(("bx", "by"), None, None),
            P(),
            P(),
            P(),
            P(None, "bx", "by"),
        ),
        out_specs=(P(None, "bx", "by"), P(None, ("bx", "by")), P(("bx", "by"), None), P(), P()),
        check_vma=False,
    )
```

```python
import jax
import jax.numpy as jnp
from jax import lax
from jax.experimental import pallas as pl
from jax.experimental.pallas import tpu as pltpu
from jax.sharding import PartitionSpec as P

epsilon = 1e-05
MESH = pl.DeviceIdType.MESH
F32 = jnp.float32
BF16 = jnp.bfloat16
I32 = jnp.int32
VMEM_LIMIT = 60 * 2**20
NT = (((1,), (1,)), ((), ()))
TN = (((0,), (0,)), ((), ()))
LANES = 128
PITCH = 80
STRIDE = 45
GROUP = 8
FOLD = 8
ENCODE_ROWS = 64
BACK_ROWS = 64
SPAN = 2048
SHARE = 16
SHARE_STRIDE = 45
DIRECTIONS = ((-1, 0), (1, 0), (0, -1), (0, 1), (-1, -1), (-1, 1), (1, -1), (1, 1))


def dot(left, right, dims=(((1,), (0,)), ((), ()))):
    return lax.dot_general(left, right, dims, preferred_element_type=F32)


def halves(value):
    high = value.astype(BF16)
    return high, (value - high.astype(F32)).astype(BF16)


def place(index):
    cols = lax.axis_size("by")
    return (lax.div(index, cols), lax.rem(index, cols))


def grid_place():
    return lax.axis_index("bx"), lax.axis_index("by"), lax.axis_size("bx"), lax.axis_size("by")


def inside(dx, dy):
    bx, by, nx, ny = grid_place()
    x, y = bx + dx, by + dy
    return (x >= 0) & (x < nx) & (y >= 0) & (y < ny)


def lane_iota(rows):
    return lax.broadcasted_iota(I32, (rows, LANES), 1)


def row_iota(rows):
    return lax.broadcasted_iota(I32, (rows, LANES), 0)


def halo_copies(edges, sides, landed, send_sems, recv_sems):
    bx, by, _, _ = grid_place()
    cols = edges.shape[1]
    depth = sides.shape[1]
    first, last = pl.ds(0, 16), pl.ds(depth - 16, 16)
    pieces = (
        (edges.at[0], landed.at[0, pl.ds(0, cols)]),
        (edges.at[1], landed.at[1, pl.ds(0, cols)]),
        (sides.at[0], landed.at[2]),
        (sides.at[1], landed.at[3]),
        (sides.at[0, first], landed.at[4, first]),
        (sides.at[1, first], landed.at[5, first]),
        (sides.at[0, last], landed.at[6, first]),
        (sides.at[1, last], landed.at[7, first]),
    )
    return [
        pltpu.make_async_remote_copy(
            src_ref=source,
            dst_ref=target,
            send_sem=send_sems.at[way],
            recv_sem=recv_sems.at[way],
            device_id=(bx + dx, by + dy),
            device_id_type=MESH,
        )
        for way, ((dx, dy), (source, target)) in enumerate(zip(DIRECTIONS, pieces))
    ]


def start_halo(copies):
    for (dx, dy), copy in zip(DIRECTIONS, copies):
        pl.when(inside(dx, dy))(copy.start)


def finish_halo(copies, landed, field, rows, cols):
    low = (rows + 1) * PITCH

    def lay(way):
        if way == 0:
            field[pl.ds(low + 8, cols), :] = landed[0, 0:cols].astype(F32)
        elif way == 1:
            field[pl.ds(8, cols), :] = landed[1, 0:cols].astype(F32)
        elif way == 2:
            field[pl.ds(PITCH + 8 + cols, rows, stride=PITCH), :] = landed[2].astype(F32)
        elif way == 3:
            field[pl.ds(PITCH + 7, rows, stride=PITCH), :] = landed[3].astype(F32)
        elif way == 4:
            field[pl.ds(low + 8 + cols, 1), :] = landed[4, 0:16].astype(F32)[0:1]
        elif way == 5:
            field[pl.ds(low + 7, 1), :] = landed[5, 0:16].astype(F32)[0:1]
        elif way == 6:
            field[pl.ds(8 + cols, 1), :] = landed[6, 0:16].astype(F32)[15:16]
        else:
            field[pl.ds(7, 1), :] = landed[7, 0:16].astype(F32)[15:16]

    for way, ((dx, dy), copy) in enumerate(zip(DIRECTIONS, copies)):

        def arrive(way=way, copy=copy):
            copy.wait_recv()
            lay(way)

        pl.when(inside(-dx, -dy))(arrive)
        pl.when(inside(dx, dy))(copy.wait_send)


def clear_border(field, rows, cols):
    channels = field.shape[1]
    zeros = jnp.zeros((PITCH, channels), F32)
    field[pl.ds(0, PITCH), :] = zeros
    field[pl.ds((rows + 1) * PITCH, PITCH), :] = zeros
    for column in (7, 8 + cols):
        field[pl.ds(PITCH + column, rows, stride=PITCH), :] = jnp.zeros((rows, channels), F32)


def fill_borders(field, edges, sides, rows, cols):
    sides[0] = field[pl.ds(PITCH + 8, rows, stride=PITCH), :].astype(BF16)
    sides[1] = field[pl.ds(PITCH + 7 + cols, rows, stride=PITCH), :].astype(BF16)
    edges[0] = field[pl.ds(PITCH + 8, cols), :].astype(BF16)
    edges[1] = field[pl.ds(rows * PITCH + 8, cols), :].astype(BF16)


def spread_columns(field, wide, rows, cols):
    channels = field.shape[1]

    def row(x, carry):
        base = pl.multiple_of(x * PITCH, 8)
        at = pl.ds(pl.multiple_of(x * cols, cols), cols)
        for shift in range(3):
            wide[at, pl.ds(shift * channels, channels)] = field[
                pl.ds(base + 7 + shift, cols), :
            ].astype(BF16)
        return carry

    lax.fori_loop(0, rows + 2, row, 0)


def conv_rows(wide, weight, step, rows, cols):
    channels = weight.shape[1] // 2
    window = jnp.concatenate(
        [
            jnp.concatenate(
                [
                    wide[pl.ds(pl.multiple_of((step * rows + r + tap) * cols, cols), cols), :]
                    for r in range(0, rows, 2)
                ],
                axis=0,
            )
            for tap in range(4)
        ],
        axis=1,
    )
    both = dot(window, weight[...])
    return [
        both[(r // 2) * cols : (r // 2 + 1) * cols, (r % 2) * channels : (r % 2 + 1) * channels]
        for r in range(rows)
    ]


def double_weight(target, tap_weight, depth, channels):
    for tap in range(4):
        at = pl.ds(tap * depth, depth)
        for half in range(2):
            inner = tap - half
            lane = pl.ds(half * channels, channels)
            if 0 <= inner < 3:
                for third in range(3):
                    target[pl.ds(tap * depth + third * channels, channels), lane] = tap_weight(
                        inner, third
                    )
            else:
                target[at, lane] = jnp.zeros((depth, channels), BF16)


def position():
    count = lax.axis_size("bx") * lax.axis_size("by")
    return lax.axis_index("bx") * lax.axis_size("by") + lax.axis_index("by"), count


def greet_all(me, count):
    barrier = pltpu.get_barrier_semaphore()

    def greet(step, carry):
        pl.semaphore_signal(
            barrier, inc=1, device_id=place(lax.rem(me + step, count)), device_id_type=MESH
        )
        return carry

    lax.fori_loop(1, count, greet, 0)
    return barrier


def partner(me, pairs, step):
    return lax.rem(lax.div(me, 2) + lax.rem(step * STRIDE, pairs), pairs)


def source(me, pairs, step):
    return lax.rem(lax.div(me, 2) + pairs - lax.rem(step * STRIDE, pairs), pairs)


def send_pair(me, pairs, step, leaving, landing, sent, received):
    pair = partner(me, pairs, step)
    for side in range(2):
        tile = 2 * pair + side

        @pl.when(tile != me)
        def _(side=side, tile=tile):
            pltpu.make_async_remote_copy(
                src_ref=leaving.at[2 * step + side],
                dst_ref=landing.at[2 * step + lax.rem(me, 2)],
                send_sem=sent,
                recv_sem=received.at[lax.div(step, GROUP)],
                device_id=place(tile),
                device_id_type=MESH,
            ).start()


def wait_group(group, landing, received):
    full = pl.ds(0, 2 * GROUP)
    less = pl.ds(0, 2 * GROUP - 1)

    @pl.when(group == 0)
    def _():
        pltpu.make_async_copy(landing.at[less], landing.at[less], received.at[0]).wait()

    @pl.when(group > 0)
    def _():
        pltpu.make_async_copy(landing.at[full], landing.at[full], received.at[group]).wait()


def wait_sent(leaving, sent):
    others = pl.ds(0, leaving.shape[0] - 1)
    pltpu.make_async_copy(leaving.at[others], leaving.at[others], sent).wait()


def lift_kernel(
    counts, features, logits, ctx_weight, pixels, bins, cells_in, weight, proj, code_grad,
    lifted, slot_code, slot_weight, prob_out, ctx_out, weight_two, back_two, proj_two, slopes_in,
    cells_two, starts, point_code, outgoing, arrived, pooled, hot_cells, folded,
    local_sem, send_sem, recv_sem,
):
    me, count = position()
    pairs = count // 2
    my_side = lax.rem(me, 2)
    capacity = cells_in.shape[1]
    channels = weight.shape[1]
    bin_count, pix_count = logits.shape
    code_dims = proj.shape[1]
    all_cells = lifted.shape[0]
    cols = code_grad.shape[1]
    rows = all_cells // cols
    depth = 3 * channels
    barrier = greet_all(me, count)

    context = dot(features[...], ctx_weight[...]).astype(BF16)
    ctx_pair = jnp.concatenate([context, context], axis=0)
    raw = logits[...]
    shifted = jnp.exp(raw - jnp.max(raw, axis=0, keepdims=True))
    prob = shifted / jnp.sum(shifted, axis=0, keepdims=True)
    prob_out[...] = prob
    ctx_out[...] = context
    prob_pair = jnp.concatenate(halves(prob), axis=1)
    point_code[...] = pixels[...] * bin_count + bins[...]
    last_row = pixels.shape[0] - 1

    def start_of(tile, begin):
        starts[tile] = begin
        return begin + counts[0, tile]

    lax.fori_loop(0, count, start_of, 0)
    lane = lane_iota(1)
    pix_row = row_iota(pix_count)
    bin_row = row_iota(bin_count)

    def codes_of(pair):
        sides_codes = []
        for side in range(2):
            tile = 2 * pair + side
            begin = starts[tile]
            offset = jnp.bitwise_and(begin, LANES - 1)
            row = jnp.right_shift(begin, 7)
            here = point_code[pl.ds(jnp.minimum(row, last_row), 1), :]
            after = point_code[pl.ds(jnp.minimum(row + 1, last_row), 1), :]
            turned = pltpu.roll(
                jnp.where(lane >= offset, here, after),
                jnp.bitwise_and(side * capacity + LANES - offset, LANES - 1),
                axis=1,
            )
            sides_codes.append(jnp.where(lane - side * capacity < counts[0, tile], turned, -1))
        return jnp.where(lane < capacity, sides_codes[0], sides_codes[1])

    pl.semaphore_wait(barrier, count - 1)
    unroll = 4

    def lift(step, carry):
        for part in range(unroll):
            turn = step * unroll + part
            code = codes_of(partner(me, pairs, turn))
            slot_code[pl.ds(turn, 1), :] = code
            hot = jnp.right_shift(code, 6) == pix_row
            hot_b = jnp.where(hot, 1.0, 0.0).astype(BF16)
            picked = dot(prob_pair, jnp.concatenate([hot_b, hot_b], axis=0))
            chosen = jnp.bitwise_and(code, bin_count - 1) == bin_row
            point_weight = jnp.sum(jnp.where(chosen, picked, 0.0), axis=0, keepdims=True)
            slot_weight[pl.ds(turn, 1), :] = point_weight
            spread = jnp.concatenate(halves(jnp.where(hot, point_weight, 0.0)), axis=0)
            value = dot(spread, ctx_pair, TN).astype(BF16)
            outgoing[pl.ds(2 * turn, 2)] = value.reshape(2, capacity, channels)
        for part in range(unroll):
            send_pair(me, pairs, step * unroll + part, outgoing, arrived, send_sem, recv_sem)
        return carry

    lax.fori_loop(0, pairs // unroll, lift, 0)
    own = pltpu.make_async_copy(outgoing.at[my_side], arrived.at[my_side], local_sem)
    own.start()

    double_weight(
        weight_two,
        lambda tap, third: weight[pl.ds(tap * depth + third * channels, channels), :],
        depth,
        channels,
    )
    double_weight(
        back_two,
        lambda tap, third: weight[pl.ds((2 - tap) * depth + (2 - third) * channels, channels), :]
        .astype(F32)
        .T.astype(BF16),
        depth,
        channels,
    )
    proj_rows = dot(
        proj[...], jnp.where(row_iota(channels) == lane_iota(channels), 1.0, 0.0).astype(BF16), TN
    )
    proj_two[...] = jnp.zeros(proj_two.shape, F32)
    proj_two[0:code_dims] = proj_rows
    proj_two[8 : 8 + code_dims] = proj_rows
    slopes_in[...] = jnp.zeros(slopes_in.shape, F32)

    def take_slopes(step, carry):
        two = [code_grad[pl.ds(2 * step + r, code_dims, stride=rows), :] for r in range(2)]
        at = pl.ds(pl.multiple_of(step * 2 * cols, 2 * cols), 2 * cols)
        slopes_in[0:code_dims, at] = jnp.concatenate(two, axis=1)
        return carry

    lax.fori_loop(0, rows // 2, take_slopes, 0)
    pooled[...] = jnp.zeros(pooled.shape, F32)
    cells_two[...] = jnp.concatenate(
        [cells_in[pl.ds(side, pairs, stride=2), :] for side in range(2)], axis=1
    )
    run = all_cells // FOLD
    run_shift = run.bit_length() - 1
    run_row = row_iota(run)
    own.wait()

    def pool(group, carry):
        wait_group(group, arrived, recv_sem)
        for part in range(GROUP):
            turn = group * GROUP + part
            cell = cells_two[pl.ds(source(me, pairs, turn), 1), :]
            at = pl.ds(part * LANES, LANES)
            hot_cells[:, at] = jnp.where(
                jnp.bitwise_and(cell, run - 1) == run_row, 1.0, 0.0
            ).astype(BF16)
            which = jnp.broadcast_to(jnp.right_shift(cell, run_shift), (LANES, LANES)).T
            value = arrived[pl.ds(2 * turn, 2)].reshape(2 * capacity, channels).astype(F32)
            for fold in range(FOLD):
                folded[at, pl.ds(fold * channels, channels)] = jnp.where(
                    which == fold, value, 0.0
                ).astype(BF16)
        pooled[...] += dot(hot_cells[...], folded[...])
        return carry

    lax.fori_loop(0, pairs // GROUP, pool, 0)
    for fold in range(FOLD):
        lifted[pl.ds(fold * run, run), :] = pooled[:, pl.ds(fold * channels, channels)].astype(BF16)
    wait_sent(outgoing, send_sem)


def tile_kernel(
    levels, lifted, slot_code, slot_weight, prob_in, ctx_in, weight_two, back_two, proj_two_in,
    slopes_in, ctx_weight, cells_in,
    codes_out, logit_out, feature_out, sums,
    cells, returning, back, field, wide, wide_grad, lift_grad, sides, edges, landed, stage,
    parts, gathered, codes, flipped, prob_sum, ctx_sum,
    local_sem, back_send, back_recv, halo_send, halo_recv,
    part_send, part_recv, sum_send, sum_recv,
):
    me, count = position()
    pairs = count // 2
    my_side = lax.rem(me, 2)
    capacity = cells.shape[1]
    channels = lifted.shape[1]
    bin_count, pix_count = prob_in.shape
    cols = edges.shape[1]
    rows = sides.shape[1]
    code_dims = codes_out.shape[0] // rows
    depth = 3 * channels
    owners = parts.shape[0]
    all_cells = rows * cols
    barrier = greet_all(me, count)
    to_smem = pltpu.make_async_copy(cells_in, cells, local_sem.at[0])
    to_smem.start()
    pix_row = row_iota(pix_count)
    bin_row = row_iota(bin_count)
    clear_border(field, rows, cols)

    def load_row(x, carry):
        field[pl.ds(pl.multiple_of((x + 1) * PITCH + 8, 8), cols), :] = lifted[
            pl.ds(pl.multiple_of(x * cols, cols), cols), :
        ].astype(F32)
        return carry

    lax.fori_loop(0, rows, load_row, 0)
    fill_borders(field, edges, sides, rows, cols)
    pl.semaphore_wait(barrier, count - 1)
    first = halo_copies(edges, sides, landed.at[0], halo_send.at[0], halo_recv.at[0])
    start_halo(first)
    finish_halo(first, landed.at[0], field, rows, cols)
    spread_columns(field, wide, rows, cols)

    half_levels = jnp.zeros((8, 1), F32)
    for q in range(code_dims):
        half_levels = half_levels + jnp.where(
            lax.broadcasted_iota(I32, (8, 1), 0) == q, (levels[q].astype(F32) - 1.0) * 0.5, 0.0
        )
    proj_two = proj_two_in[...].astype(BF16)
    block = ENCODE_ROWS * cols

    def encode(step, proj_sum):
        origin = pl.multiple_of(step * block, block)
        conv_out = jnp.concatenate(conv_rows(wide, weight_two, step, ENCODE_ROWS, cols), axis=0)
        inv_rms = lax.rsqrt(jnp.mean(conv_out * conv_out, axis=-1, keepdims=True) + epsilon)
        normed = conv_out * inv_rms
        gate = 0.5 + 0.5 * jnp.tanh(0.5 * normed)
        active = normed * gate
        hidden = active.astype(BF16)
        squash = jnp.tanh(dot(proj_two, hidden, NT)[:8])
        codes[:, pl.ds(origin, block)] = half_levels * squash
        slope = slopes_in[:, pl.ds(origin, block)] * half_levels * (1.0 - squash * squash)
        slope_high = slope.astype(BF16).astype(F32)
        slope_pair = jnp.concatenate([slope_high, slope - slope_high], axis=0).astype(BF16)
        proj_both = dot(slope_pair, hidden)
        hidden_grad = dot(slope_pair, proj_two, TN)
        norm_grad = hidden_grad * (gate + active * (1.0 - gate))
        mixed = jnp.mean(norm_grad * normed, axis=-1, keepdims=True)
        conv_grad = inv_rms * (norm_grad - normed * mixed)
        for r in range(ENCODE_ROWS):
            at = pl.multiple_of((step * ENCODE_ROWS + r + 1) * PITCH + 8, 8)
            field[pl.ds(at, cols), :] = conv_grad[r * cols : (r + 1) * cols]
        wide_grad[pl.ds(origin + cols, block), pl.ds(channels, channels)] = conv_grad.astype(BF16)
        return proj_sum + proj_both[:8] + proj_both[8:]

    proj_sum = lax.fori_loop(0, rows // ENCODE_ROWS, encode, jnp.zeros((8, channels), F32))
    fill_borders(field, edges, sides, rows, cols)
    second = halo_copies(edges, sides, landed.at[1], halo_send.at[1], halo_recv.at[1])
    start_halo(second)

    flipped[...] = jnp.zeros(flipped.shape, F32)

    def weight_grad(step, carry):
        origin = pl.multiple_of(step * SPAN, SPAN)
        grad_t = wide_grad[pl.ds(origin + cols, SPAN), pl.ds(channels, channels)].T
        for tap in range(3):
            flipped[:, pl.ds(tap * depth, depth)] += dot(
                grad_t, wide[pl.ds(origin + tap * cols, SPAN), :]
            )
        return carry

    lax.fori_loop(0, all_cells // SPAN, weight_grad, 0)
    for tap in range(9):
        parts[pl.ds(tap * (channels // SHARE), channels // SHARE)] = flipped[
            :, pl.ds(tap * channels, channels)
        ].T.reshape(channels // SHARE, SHARE, channels)
    parts[owners - 1] = jnp.concatenate([proj_sum, jnp.zeros((SHARE - 8, channels), F32)], axis=0)

    def share_of(device):
        return lax.rem(device * SHARE_STRIDE, count)

    def send_part(step, carry):
        target = lax.rem(me + step, count)
        share = share_of(target)

        @pl.when(share < owners)
        def _():
            pltpu.make_async_remote_copy(
                src_ref=parts.at[share],
                dst_ref=gathered.at[me],
                send_sem=part_send,
                recv_sem=part_recv,
                device_id=place(target),
                device_id_type=MESH,
            ).start()

        return carry

    lax.fori_loop(1, count, send_part, 0)

    finish_halo(second, landed.at[1], field, rows, cols)
    spread_columns(field, wide_grad, rows, cols)

    def conv_back(step, carry):
        for r, row in enumerate(conv_rows(wide_grad, back_two, step, BACK_ROWS, cols)):
            at = pl.multiple_of((step * BACK_ROWS + r) * cols, cols)
            lift_grad[pl.ds(at, cols), :] = row
        return carry

    lax.fori_loop(0, rows // BACK_ROWS, conv_back, 0)

    to_smem.wait()

    def send_back(turn, carry):
        pair = partner(me, pairs, turn)
        for side in range(2):
            for slot in range(capacity):
                stage[pl.ds(side * capacity + slot, 1), :] = lift_grad[
                    pl.ds(cells[2 * pair + side, slot], 1), :
                ]
        returning[pl.ds(2 * turn, 2)] = stage[...].astype(BF16).reshape(2, capacity, channels)
        send_pair(me, pairs, turn, returning, back, back_send, back_recv)
        return carry

    lax.fori_loop(0, pairs // 2, send_back, 0)
    own_back = pltpu.make_async_copy(returning.at[my_side], back.at[my_side], local_sem.at[1])
    own_back.start()

    mine = share_of(me)
    others = pl.ds(0, count - 1)
    rest = pl.ds(0, owners - 1)

    @pl.when(mine < owners)
    def _():
        pltpu.make_async_copy(gathered.at[others], gathered.at[others], part_recv).wait()
        gathered[me] = parts[mine]

        def add(sender, total):
            return total + gathered[sender]

        sums[mine] = lax.fori_loop(0, count, add, jnp.zeros((SHARE, channels), F32))

        def send_sum(step, carry):
            pltpu.make_async_remote_copy(
                src_ref=sums.at[mine],
                dst_ref=sums.at[mine],
                send_sem=sum_send,
                recv_sem=sum_recv,
                device_id=place(lax.rem(me + step, count)),
                device_id_type=MESH,
            ).start()
            return carry

        lax.fori_loop(1, count, send_sum, 0)

    lax.fori_loop(pairs // 2, pairs, send_back, 0)
    own_back.wait()

    context = ctx_in[...]
    prob = prob_in[...]
    prob_sum[...] = jnp.zeros(prob_sum.shape, F32)
    ctx_sum[...] = jnp.zeros(ctx_sum.shape, F32)

    def point_grads(group, carry):
        wait_group(group, back, back_recv)
        prob_grad, ctx_grad = prob_sum[...], ctx_sum[...]
        for part in range(GROUP):
            turn = group * GROUP + part
            met = lax.rem(pairs - turn, pairs)
            code = slot_code[pl.ds(met, 1), :]
            grad = back[pl.ds(2 * turn, 2)].reshape(2 * capacity, channels)
            hot = jnp.right_shift(code, 6) == pix_row
            hot_b = jnp.where(hot, 1.0, 0.0).astype(BF16)
            chosen = jnp.bitwise_and(code, bin_count - 1) == bin_row
            dots = jnp.sum(jnp.where(hot, dot(context, grad, NT), 0.0), axis=0, keepdims=True)
            by_bin = jnp.concatenate(halves(jnp.where(chosen, dots, 0.0)), axis=1)
            prob_grad = prob_grad + dot(by_bin, jnp.concatenate([hot_b, hot_b], axis=1), NT)
            spread = jnp.concatenate(
                halves(jnp.where(hot, slot_weight[pl.ds(met, 1), :], 0.0)), axis=1
            )
            ctx_grad = ctx_grad + dot(spread, jnp.concatenate([grad, grad], axis=0))
        prob_sum[...] = prob_grad
        ctx_sum[...] = ctx_grad
        return carry

    lax.fori_loop(0, pairs // GROUP, point_grads, 0)
    prob_grad, ctx_grad = prob_sum[...], ctx_sum[...]
    logit_out[...] = prob * (prob_grad - jnp.sum(prob * prob_grad, axis=0, keepdims=True))
    feature_out[...] = dot(ctx_grad.astype(BF16), ctx_weight[...], NT).astype(BF16)

    def put_codes(step, carry):
        two = codes[0:code_dims, pl.ds(pl.multiple_of(step * 2 * cols, 2 * cols), 2 * cols)]
        for r in range(2):
            codes_out[pl.ds(2 * step + r, code_dims, stride=rows), :] = two[
                :, r * cols : (r + 1) * cols
            ]
        return carry

    lax.fori_loop(0, rows // 2, put_codes, 0)

    @pl.when(mine < owners)
    def _():
        pltpu.make_async_copy(gathered.at[others], gathered.at[others], sum_send).wait()
        pltpu.make_async_copy(parts.at[rest], parts.at[rest], part_send).wait()
        pltpu.make_async_copy(sums.at[rest], sums.at[rest], sum_recv).wait()

    @pl.when(mine >= owners)
    def _():
        pltpu.make_async_copy(parts, parts, part_send).wait()
        pltpu.make_async_copy(sums, sums, sum_recv).wait()

    wait_sent(returning, back_send)


def per_device(
    features,
    depth_logits,
    ctx_weight,
    point_pixel,
    point_bin,
    segment_count,
    slot_cell,
    conv_weight,
    proj_weight,
    level_count,
    code_grad,
):
    _, count, capacity = slot_cell.shape
    code_dims, rows, cols = code_grad.shape
    bin_count, pix_count = depth_logits.shape
    feature_dims, channels = ctx_weight.shape
    pixels = point_pixel.reshape(-1, LANES)
    bins = point_bin.reshape(-1, LANES)
    all_cells = rows * cols
    owners = 9 * channels // SHARE + 1
    pairs = count // 2
    run = all_cells // FOLD
    vmem = pl.BlockSpec(memory_space=pltpu.VMEM)
    smem = pl.BlockSpec(memory_space=pltpu.SMEM)
    wide = pltpu.VMEM(((rows + 2) * cols, 3 * channels), BF16)
    blocks = pltpu.VMEM((count, capacity, channels), BF16)
    doubled = jax.ShapeDtypeStruct((12 * channels, 2 * channels), BF16)
    dma = pltpu.SemaphoreType.DMA
    cells = slot_cell[0]
    lifted, slot_code, slot_weight, prob, context, weight_two, back_two, proj_two, slopes = (
        pl.pallas_call(
            lift_kernel,
            out_shape=(
                jax.ShapeDtypeStruct((all_cells, channels), BF16),
                jax.ShapeDtypeStruct((pairs, LANES), I32),
                jax.ShapeDtypeStruct((pairs, LANES), F32),
                jax.ShapeDtypeStruct((bin_count, pix_count), F32),
                jax.ShapeDtypeStruct((pix_count, channels), BF16),
                doubled,
                doubled,
                jax.ShapeDtypeStruct((16, channels), F32),
                jax.ShapeDtypeStruct((8, all_cells), F32),
            ),
            in_specs=[smem] + [vmem] * 9,
            out_specs=(vmem,) * 9,
            scratch_shapes=[
                pltpu.VMEM((pairs, 2 * capacity), I32),
                pltpu.SMEM((count,), I32),
                pltpu.VMEM(pixels.shape, I32),
                blocks,
                blocks,
                pltpu.VMEM((run, FOLD * channels), F32),
                pltpu.VMEM((run, GROUP * LANES), BF16),
                pltpu.VMEM((GROUP * LANES, FOLD * channels), BF16),
                dma,
                dma,
                dma((pairs // GROUP,)),
            ],
            compiler_params=pltpu.CompilerParams(
                collective_id=0, has_side_effects=True, vmem_limit_bytes=VMEM_LIMIT
            ),
            name="lift",
        )(
            segment_count,
            features,
            depth_logits,
            ctx_weight,
            pixels,
            bins,
            cells,
            conv_weight.reshape(9 * channels, channels),
            proj_weight,
            code_grad.reshape(code_dims * rows, cols),
        )
    )
    codes, grad_logits, grad_features, sums = pl.pallas_call(
        tile_kernel,
        out_shape=(
            jax.ShapeDtypeStruct((code_dims * rows, cols), F32),
            jax.ShapeDtypeStruct((bin_count, pix_count), F32),
            jax.ShapeDtypeStruct((pix_count, feature_dims), BF16),
            jax.ShapeDtypeStruct((owners, SHARE, channels), F32),
        ),
        in_specs=[smem] + [vmem] * 10 + [pl.BlockSpec(memory_space=pl.ANY)],
        out_specs=(vmem,) * 4,
        scratch_shapes=[
            pltpu.SMEM((count, capacity), I32),
            blocks,
            blocks,
            pltpu.VMEM(((rows + 2) * PITCH, channels), F32),
            wide,
            wide,
            pltpu.VMEM((all_cells, channels), F32),
            pltpu.VMEM((2, rows, channels), BF16),
            pltpu.VMEM((2, cols, channels), BF16),
            pltpu.VMEM((2, 8, rows, channels), BF16),
            pltpu.VMEM((2 * capacity, channels), F32),
            pltpu.VMEM((owners, SHARE, channels), F32),
            pltpu.VMEM((count, SHARE, channels), F32),
            pltpu.VMEM((8, all_cells), F32),
            pltpu.VMEM((channels, 9 * channels), F32),
            pltpu.VMEM((bin_count, pix_count), F32),
            pltpu.VMEM((pix_count, channels), F32),
            dma((2,)),
            dma,
            dma((pairs // GROUP,)),
            dma((2, 8)),
            dma((2, 8)),
            dma,
            dma,
            dma,
            dma,
        ],
        compiler_params=pltpu.CompilerParams(
            collective_id=1, has_side_effects=True, vmem_limit_bytes=VMEM_LIMIT
        ),
        name="tile",
    )(
        level_count,
        lifted,
        slot_code,
        slot_weight,
        prob,
        context,
        weight_two,
        back_two,
        proj_two,
        slopes,
        ctx_weight,
        cells,
    )
    return (
        codes.reshape(code_grad.shape),
        grad_logits,
        grad_features,
        sums[:-1].reshape(conv_weight.shape),
        sums[-1, :code_dims].T,
    )


def solution(mesh):
    return jax.shard_map(
        per_device,
        mesh=mesh,
        in_specs=(
            P(("bx", "by"), None),
            P(None, ("bx", "by")),
            P(),
            P(("bx", "by")),
            P(("bx", "by")),
            P(("bx", "by"), None),
            P(("bx", "by"), None, None),
            P(),
            P(),
            P(),
            P(None, "bx", "by"),
        ),
        out_specs=(P(None, "bx", "by"), P(None, ("bx", "by")), P(("bx", "by"), None), P(), P()),
        check_vma=False,
    )
```

```python
import jax
import jax.numpy as jnp
from jax import lax
from jax.experimental import pallas as pl
from jax.experimental.pallas import tpu as pltpu
from jax.sharding import PartitionSpec as P

epsilon = 1e-05
MESH = pl.DeviceIdType.MESH
F32 = jnp.float32
BF16 = jnp.bfloat16
I32 = jnp.int32
VMEM_LIMIT = 60 * 2**20
NT = (((1,), (1,)), ((), ()))
TN = (((0,), (0,)), ((), ()))
LANES = 128
PITCH = 80
STRIDE = 45
GROUP = 8
FOLD = 8
ENCODE_ROWS = 64
BACK_ROWS = 64
SPAN = 2048
SHARE = 16
DIRECTIONS = ((-1, 0), (1, 0), (0, -1), (0, 1), (-1, -1), (-1, 1), (1, -1), (1, 1))


def dot(left, right, dims=(((1,), (0,)), ((), ()))):
    return lax.dot_general(left, right, dims, preferred_element_type=F32)


def halves(value):
    high = value.astype(BF16)
    return high, (value - high.astype(F32)).astype(BF16)


def place(index):
    cols = lax.axis_size("by")
    return (lax.div(index, cols), lax.rem(index, cols))


def grid_place():
    return lax.axis_index("bx"), lax.axis_index("by"), lax.axis_size("bx"), lax.axis_size("by")


def inside(dx, dy):
    bx, by, nx, ny = grid_place()
    x, y = bx + dx, by + dy
    return (x >= 0) & (x < nx) & (y >= 0) & (y < ny)


def lane_iota(rows):
    return lax.broadcasted_iota(I32, (rows, LANES), 1)


def row_iota(rows):
    return lax.broadcasted_iota(I32, (rows, LANES), 0)


def halo_copies(edges, sides, landed, send_sems, recv_sems):
    bx, by, _, _ = grid_place()
    cols = edges.shape[1]
    depth = sides.shape[1]
    first, last = pl.ds(0, 16), pl.ds(depth - 16, 16)
    pieces = (
        (edges.at[0], landed.at[0, pl.ds(0, cols)]),
        (edges.at[1], landed.at[1, pl.ds(0, cols)]),
        (sides.at[0], landed.at[2]),
        (sides.at[1], landed.at[3]),
        (sides.at[0, first], landed.at[4, first]),
        (sides.at[1, first], landed.at[5, first]),
        (sides.at[0, last], landed.at[6, first]),
        (sides.at[1, last], landed.at[7, first]),
    )
    return [
        pltpu.make_async_remote_copy(
            src_ref=source,
            dst_ref=target,
            send_sem=send_sems.at[way],
            recv_sem=recv_sems.at[way],
            device_id=(bx + dx, by + dy),
            device_id_type=MESH,
        )
        for way, ((dx, dy), (source, target)) in enumerate(zip(DIRECTIONS, pieces))
    ]


def start_halo(copies):
    for (dx, dy), copy in zip(DIRECTIONS, copies):
        pl.when(inside(dx, dy))(copy.start)


def finish_halo(copies, landed, field, rows, cols):
    low = (rows + 1) * PITCH

    def lay(way):
        if way == 0:
            field[pl.ds(low + 8, cols), :] = landed[0, 0:cols].astype(F32)
        elif way == 1:
            field[pl.ds(8, cols), :] = landed[1, 0:cols].astype(F32)
        elif way == 2:
            field[pl.ds(PITCH + 8 + cols, rows, stride=PITCH), :] = landed[2].astype(F32)
        elif way == 3:
            field[pl.ds(PITCH + 7, rows, stride=PITCH), :] = landed[3].astype(F32)
        elif way == 4:
            field[pl.ds(low + 8 + cols, 1), :] = landed[4, 0:16].astype(F32)[0:1]
        elif way == 5:
            field[pl.ds(low + 7, 1), :] = landed[5, 0:16].astype(F32)[0:1]
        elif way == 6:
            field[pl.ds(8 + cols, 1), :] = landed[6, 0:16].astype(F32)[15:16]
        else:
            field[pl.ds(7, 1), :] = landed[7, 0:16].astype(F32)[15:16]

    for way, ((dx, dy), copy) in enumerate(zip(DIRECTIONS, copies)):

        def arrive(way=way, copy=copy):
            copy.wait_recv()
            lay(way)

        pl.when(inside(-dx, -dy))(arrive)
        pl.when(inside(dx, dy))(copy.wait_send)


def clear_border(field, rows, cols):
    channels = field.shape[1]
    zeros = jnp.zeros((PITCH, channels), F32)
    field[pl.ds(0, PITCH), :] = zeros
    field[pl.ds((rows + 1) * PITCH, PITCH), :] = zeros
    for column in (7, 8 + cols):
        field[pl.ds(PITCH + column, rows, stride=PITCH), :] = jnp.zeros((rows, channels), F32)


def fill_borders(field, edges, sides, rows, cols):
    sides[0] = field[pl.ds(PITCH + 8, rows, stride=PITCH), :].astype(BF16)
    sides[1] = field[pl.ds(PITCH + 7 + cols, rows, stride=PITCH), :].astype(BF16)
    edges[0] = field[pl.ds(PITCH + 8, cols), :].astype(BF16)
    edges[1] = field[pl.ds(rows * PITCH + 8, cols), :].astype(BF16)


def spread_columns(field, wide, rows, cols):
    channels = field.shape[1]

    def row(x, carry):
        base = pl.multiple_of(x * PITCH, 8)
        at = pl.ds(pl.multiple_of(x * cols, cols), cols)
        for shift in range(3):
            wide[at, pl.ds(shift * channels, channels)] = field[
                pl.ds(base + 7 + shift, cols), :
            ].astype(BF16)
        return carry

    lax.fori_loop(0, rows + 2, row, 0)


def conv_rows(wide, weight, step, rows, cols):
    channels = weight.shape[1] // 2
    window = jnp.concatenate(
        [
            jnp.concatenate(
                [
                    wide[pl.ds(pl.multiple_of((step * rows + r + tap) * cols, cols), cols), :]
                    for r in range(0, rows, 2)
                ],
                axis=0,
            )
            for tap in range(4)
        ],
        axis=1,
    )
    both = dot(window, weight[...])
    return [
        both[(r // 2) * cols : (r // 2 + 1) * cols, (r % 2) * channels : (r % 2 + 1) * channels]
        for r in range(rows)
    ]


def double_weight(target, tap_weight, depth, channels):
    for tap in range(4):
        at = pl.ds(tap * depth, depth)
        for half in range(2):
            inner = tap - half
            lane = pl.ds(half * channels, channels)
            if 0 <= inner < 3:
                for third in range(3):
                    target[pl.ds(tap * depth + third * channels, channels), lane] = tap_weight(
                        inner, third
                    )
            else:
                target[at, lane] = jnp.zeros((depth, channels), BF16)


def position():
    count = lax.axis_size("bx") * lax.axis_size("by")
    return lax.axis_index("bx") * lax.axis_size("by") + lax.axis_index("by"), count


def greet_all(me, count):
    barrier = pltpu.get_barrier_semaphore()

    def greet(step, carry):
        pl.semaphore_signal(
            barrier, inc=1, device_id=place(lax.rem(me + step, count)), device_id_type=MESH
        )
        return carry

    lax.fori_loop(1, count, greet, 0)
    return barrier


def partner(me, pairs, step):
    return lax.rem(lax.div(me, 2) + lax.rem(step * STRIDE, pairs), pairs)


def source(me, pairs, step):
    return lax.rem(lax.div(me, 2) + pairs - lax.rem(step * STRIDE, pairs), pairs)


def send_pair(me, pairs, step, leaving, landing, sent, received):
    pair = partner(me, pairs, step)
    for side in range(2):
        tile = 2 * pair + side

        @pl.when(tile != me)
        def _(side=side, tile=tile):
            pltpu.make_async_remote_copy(
                src_ref=leaving.at[2 * step + side],
                dst_ref=landing.at[2 * step + lax.rem(me, 2)],
                send_sem=sent,
                recv_sem=received.at[lax.div(step, GROUP)],
                device_id=place(tile),
                device_id_type=MESH,
            ).start()


def wait_group(group, landing, received):
    full = pl.ds(0, 2 * GROUP)
    less = pl.ds(0, 2 * GROUP - 1)

    @pl.when(group == 0)
    def _():
        pltpu.make_async_copy(landing.at[less], landing.at[less], received.at[0]).wait()

    @pl.when(group > 0)
    def _():
        pltpu.make_async_copy(landing.at[full], landing.at[full], received.at[group]).wait()


def wait_sent(leaving, sent):
    others = pl.ds(0, leaving.shape[0] - 1)
    pltpu.make_async_copy(leaving.at[others], leaving.at[others], sent).wait()


def lift_kernel(
    counts, features, logits, ctx_weight, pixels, bins, cells_in, weight, proj, code_grad,
    lifted, slot_code, slot_weight, prob_out, ctx_out, weight_two, back_two, proj_two, slopes_in,
    cells_two, cells_v, slopes_v, starts, point_code, outgoing, arrived, pooled, hot_cells, folded,
    local_sem, send_sem, recv_sem,
):
    me, count = position()
    pairs = count // 2
    my_side = lax.rem(me, 2)
    capacity = cells_in.shape[0]
    channels = weight.shape[1]
    bin_count, pix_count = logits.shape
    code_dims = proj.shape[0]
    all_cells = lifted.shape[0]
    cols = code_grad.shape[1]
    rows = all_cells // cols
    depth = 3 * channels
    barrier = greet_all(me, count)

    context = dot(features[...], ctx_weight[...]).astype(BF16)
    raw = logits[...]
    shifted = jnp.exp(raw - jnp.max(raw, axis=0, keepdims=True))
    prob = shifted / jnp.sum(shifted, axis=0, keepdims=True)
    prob_out[...] = prob
    ctx_out[...] = context
    prob_pair = jnp.concatenate(halves(prob), axis=1)
    ctx_pair = jnp.concatenate([context, context], axis=0)
    point_code[...] = pixels[...] * bin_count + bins[...]
    last_row = pixels.shape[0] - 1

    def start_of(tile, begin):
        starts[tile] = begin
        return begin + counts[0, tile]

    lax.fori_loop(0, count, start_of, 0)
    lane = lane_iota(1)
    pix_row = row_iota(pix_count)
    bin_row = row_iota(bin_count)

    def codes_of(pair):
        sides_codes = []
        for side in range(2):
            tile = 2 * pair + side
            begin = starts[tile]
            offset = jnp.bitwise_and(begin, LANES - 1)
            row = jnp.right_shift(begin, 7)
            here = point_code[pl.ds(jnp.minimum(row, last_row), 1), :]
            after = point_code[pl.ds(jnp.minimum(row + 1, last_row), 1), :]
            turned = pltpu.roll(
                jnp.where(lane >= offset, here, after),
                jnp.bitwise_and(side * capacity + LANES - offset, LANES - 1),
                axis=1,
            )
            sides_codes.append(jnp.where(lane - side * capacity < counts[0, tile], turned, -1))
        return jnp.where(lane < capacity, sides_codes[0], sides_codes[1])

    def find_codes(step, carry):
        for part in range(GROUP):
            turn = step * GROUP + part
            slot_code[pl.ds(turn, 1), :] = codes_of(partner(me, pairs, turn))
        return carry

    lax.fori_loop(0, pairs // GROUP, find_codes, 0)

    pl.semaphore_wait(barrier, count - 1)

    def lift(step, carry):
        code = slot_code[pl.ds(pl.multiple_of(step * GROUP, GROUP), GROUP), :]
        code = jnp.concatenate([code[part : part + 1] for part in range(GROUP)], axis=1)
        wide_rows = lax.broadcasted_iota(I32, (pix_count, GROUP * LANES), 0)
        hot = jnp.right_shift(code, 6) == wide_rows
        hot_b = jnp.where(hot, 1.0, 0.0).astype(BF16)
        picked = dot(prob_pair, jnp.concatenate([hot_b, hot_b], axis=0))
        chosen = jnp.bitwise_and(code, bin_count - 1) == wide_rows[:bin_count]
        point_weight = jnp.sum(jnp.where(chosen, picked, 0.0), axis=0, keepdims=True)
        for part in range(GROUP):
            slot_weight[pl.ds(step * GROUP + part, 1), :] = point_weight[
                :, part * LANES : (part + 1) * LANES
            ]
        spread = jnp.concatenate(halves(jnp.where(hot, point_weight, 0.0)), axis=0)
        value = dot(spread, ctx_pair, TN).astype(BF16)
        outgoing[pl.ds(2 * GROUP * step, 2 * GROUP)] = value.reshape(
            2 * GROUP, capacity, channels
        )
        for part in range(GROUP):
            send_pair(me, pairs, step * GROUP + part, outgoing, arrived, send_sem, recv_sem)
        return carry

    lax.fori_loop(0, pairs // GROUP, lift, 0)
    own = pltpu.make_async_copy(outgoing.at[my_side], arrived.at[my_side], local_sem)
    own.start()

    double_weight(
        weight_two,
        lambda tap, third: weight[pl.ds(tap * depth + third * channels, channels), :],
        depth,
        channels,
    )
    double_weight(
        back_two,
        lambda tap, third: weight[pl.ds((2 - tap) * depth + (2 - third) * channels, channels), :]
        .astype(F32)
        .T.astype(BF16),
        depth,
        channels,
    )
    proj_rows = proj[...].astype(F32)
    proj_two[...] = jnp.zeros(proj_two.shape, F32)
    proj_two[0:code_dims] = proj_rows
    proj_two[8 : 8 + code_dims] = proj_rows
    slopes_in[...] = jnp.zeros(slopes_in.shape, F32)
    for q in range(code_dims):
        slopes_v[pl.ds(q * rows, rows), :] = code_grad[q].T

    def take_slopes(step, carry):
        two = [slopes_v[pl.ds(2 * step + r, code_dims, stride=rows), :] for r in range(2)]
        at = pl.ds(pl.multiple_of(step * 2 * cols, 2 * cols), 2 * cols)
        slopes_in[0:code_dims, at] = jnp.concatenate(two, axis=1)
        return carry

    lax.fori_loop(0, rows // 2, take_slopes, 0)
    pooled[...] = jnp.zeros(pooled.shape, F32)
    cells_v[...] = cells_in[...].T
    cells_two[...] = jnp.concatenate(
        [cells_v[pl.ds(side, pairs, stride=2), :] for side in range(2)], axis=1
    )
    run = all_cells // FOLD
    run_shift = run.bit_length() - 1
    run_row = row_iota(run)
    own.wait()

    def pool(group, carry):
        wait_group(group, arrived, recv_sem)
        for part in range(GROUP):
            turn = group * GROUP + part
            cell = cells_two[pl.ds(source(me, pairs, turn), 1), :]
            at = pl.ds(part * LANES, LANES)
            hot_cells[:, at] = jnp.where(
                jnp.bitwise_and(cell, run - 1) == run_row, 1.0, 0.0
            ).astype(BF16)
            which = jnp.broadcast_to(jnp.right_shift(cell, run_shift), (LANES, LANES)).T
            value = arrived[pl.ds(2 * turn, 2)].reshape(2 * capacity, channels).astype(F32)
            for fold in range(FOLD):
                folded[at, pl.ds(fold * channels, channels)] = jnp.where(
                    which == fold, value, 0.0
                ).astype(BF16)
        pooled[...] += dot(hot_cells[...], folded[...])
        return carry

    lax.fori_loop(0, pairs // GROUP, pool, 0)
    for fold in range(FOLD):
        lifted[pl.ds(fold * run, run), :] = pooled[:, pl.ds(fold * channels, channels)].astype(BF16)
    wait_sent(outgoing, send_sem)


def tile_kernel(
    levels, lifted, slot_code, slot_weight, prob_in, ctx_in, weight_two, back_two, proj_two_in,
    slopes_in, cells_in,
    codes, prob_sum, ctx_sum, sums,
    cells, returning, back, field, wide, wide_grad, lift_grad, sides, edges, landed, stage,
    parts, paired, chip_sums, gathered, sum_size, flipped,
    local_sem, back_send, back_recv, halo_send, halo_recv,
    pair_send, pair_recv, part_send, part_recv, sum_send, sum_recv,
):
    me, count = position()
    pairs = count // 2
    my_side = lax.rem(me, 2)
    capacity = cells.shape[0]
    channels = lifted.shape[1]
    bin_count, pix_count = prob_in.shape
    cols = edges.shape[1]
    rows = sides.shape[1]
    code_dims = levels.shape[0]
    depth = 3 * channels
    owners = parts.shape[0]
    full_shares = 9 * channels // SHARE
    all_cells = rows * cols
    barrier = greet_all(me, count)
    to_smem = pltpu.make_async_copy(cells_in, cells, local_sem.at[0])
    to_smem.start()
    pix_row = row_iota(pix_count)
    bin_row = row_iota(bin_count)
    clear_border(field, rows, cols)

    def load_row(x, carry):
        field[pl.ds(pl.multiple_of((x + 1) * PITCH + 8, 8), cols), :] = lifted[
            pl.ds(pl.multiple_of(x * cols, cols), cols), :
        ].astype(F32)
        return carry

    lax.fori_loop(0, rows, load_row, 0)
    fill_borders(field, edges, sides, rows, cols)
    pl.semaphore_wait(barrier, count - 1)
    first = halo_copies(edges, sides, landed.at[0], halo_send.at[0], halo_recv.at[0])
    start_halo(first)
    finish_halo(first, landed.at[0], field, rows, cols)
    spread_columns(field, wide, rows, cols)

    half_levels = jnp.zeros((8, 1), F32)
    for q in range(code_dims):
        half_levels = half_levels + jnp.where(
            lax.broadcasted_iota(I32, (8, 1), 0) == q, (levels[q].astype(F32) - 1.0) * 0.5, 0.0
        )
    proj_two = proj_two_in[...].astype(BF16)
    block = ENCODE_ROWS * cols

    def encode(step, proj_sum):
        origin = pl.multiple_of(step * block, block)
        conv_out = jnp.concatenate(conv_rows(wide, weight_two, step, ENCODE_ROWS, cols), axis=0)
        inv_rms = lax.rsqrt(jnp.mean(conv_out * conv_out, axis=-1, keepdims=True) + epsilon)
        normed = conv_out * inv_rms
        gate = 0.5 + 0.5 * jnp.tanh(0.5 * normed)
        active = normed * gate
        hidden = active.astype(BF16)
        squash = jnp.tanh(dot(proj_two, hidden, NT)[:8])
        codes[:, pl.ds(origin, block)] = half_levels * squash
        slope = slopes_in[:, pl.ds(origin, block)] * half_levels * (1.0 - squash * squash)
        slope_high = slope.astype(BF16).astype(F32)
        slope_pair = jnp.concatenate([slope_high, slope - slope_high], axis=0).astype(BF16)
        proj_both = dot(slope_pair, hidden)
        hidden_grad = dot(slope_pair, proj_two, TN)
        norm_grad = hidden_grad * (gate + active * (1.0 - gate))
        mixed = jnp.mean(norm_grad * normed, axis=-1, keepdims=True)
        conv_grad = inv_rms * (norm_grad - normed * mixed)
        for r in range(ENCODE_ROWS):
            at = pl.multiple_of((step * ENCODE_ROWS + r + 1) * PITCH + 8, 8)
            field[pl.ds(at, cols), :] = conv_grad[r * cols : (r + 1) * cols]
        wide_grad[pl.ds(origin + cols, block), pl.ds(channels, channels)] = conv_grad.astype(BF16)
        return proj_sum + proj_both[:8] + proj_both[8:]

    proj_sum = lax.fori_loop(0, rows // ENCODE_ROWS, encode, jnp.zeros((8, channels), F32))
    fill_borders(field, edges, sides, rows, cols)
    second = halo_copies(edges, sides, landed.at[1], halo_send.at[1], halo_recv.at[1])
    start_halo(second)

    flipped[...] = jnp.zeros(flipped.shape, F32)

    def weight_grad(step, carry):
        origin = pl.multiple_of(step * SPAN, SPAN)
        grad_t = wide_grad[pl.ds(origin + cols, SPAN), pl.ds(channels, channels)].T
        for tap in range(3):
            flipped[:, pl.ds(tap * depth, depth)] += dot(
                grad_t, wide[pl.ds(origin + tap * cols, SPAN), :]
            )
        return carry

    lax.fori_loop(0, all_cells // SPAN, weight_grad, 0)
    for tap in range(9):
        parts[pl.ds(tap * (channels // SHARE), channels // SHARE)] = flipped[
            :, pl.ds(tap * channels, channels)
        ].T.reshape(channels // SHARE, SHARE, channels)
    parts[full_shares] = jnp.concatenate(
        [proj_sum, jnp.zeros((SHARE - 8, channels), F32)], axis=0
    )
    for spare in range(full_shares + 1, owners):
        parts[spare] = jnp.zeros((SHARE, channels), F32)

    chips, half = count // 2, owners // 2
    bx, by, _, row_devices = grid_place()
    core = lax.rem(bx, 2)
    chip = lax.div(bx, 2) * row_devices + by
    to_sibling = pltpu.make_async_remote_copy(
        src_ref=parts.at[pl.ds((1 - core) * half, half)],
        dst_ref=paired,
        send_sem=pair_send,
        recv_sem=pair_recv,
        device_id=(bx + 1 - 2 * core, by),
        device_id_type=MESH,
    )
    to_sibling.start()

    def share_of(one):
        return lax.rem(one * STRIDE, chips)

    def send_part(step, carry):
        target = lax.rem(chip + step, chips)
        share = share_of(target)

        @pl.when(share < half)
        def _():
            pltpu.make_async_remote_copy(
                src_ref=chip_sums.at[share],
                dst_ref=gathered.at[chip],
                send_sem=part_send,
                recv_sem=part_recv,
                device_id=(2 * lax.div(target, row_devices) + core, lax.rem(target, row_devices)),
                device_id_type=MESH,
            ).start()

        return carry

    finish_halo(second, landed.at[1], field, rows, cols)
    spread_columns(field, wide_grad, rows, cols)
    to_sibling.wait()
    chip_sums[...] = (parts[pl.ds(core * half, half)] + paired[...]).astype(BF16)
    lax.fori_loop(1, chips, send_part, 0)

    def conv_back(step, carry):
        for r, row in enumerate(conv_rows(wide_grad, back_two, step, BACK_ROWS, cols)):
            at = pl.multiple_of((step * BACK_ROWS + r) * cols, cols)
            lift_grad[pl.ds(at, cols), :] = row
        return carry

    lax.fori_loop(0, rows // BACK_ROWS, conv_back, 0)

    to_smem.wait()

    def send_back(turn, carry):
        pair = partner(me, pairs, turn)
        for side in range(2):
            for slot in range(capacity):
                stage[pl.ds(side * capacity + slot, 1), :] = lift_grad[
                    pl.ds(cells[slot, 2 * pair + side], 1), :
                ]
        returning[pl.ds(2 * turn, 2)] = stage[...].astype(BF16).reshape(2, capacity, channels)
        send_pair(me, pairs, turn, returning, back, back_send, back_recv)
        return carry

    share = share_of(chip)
    mine = core * half + share
    others = pl.ds(0, chips - 1)
    rest = pl.ds(0, half - 1)

    def sum_parts():
        @pl.when(share < half)
        def _():
            pltpu.make_async_copy(gathered.at[others], gathered.at[others], part_recv).wait()
            gathered[chip] = chip_sums[share]

            def add(sender, total):
                return total + gathered[sender].astype(F32)

            sums[mine] = lax.fori_loop(0, chips, add, jnp.zeros((SHARE, channels), F32)).astype(
                BF16
            )

            def send_sum(step, carry):
                pltpu.make_async_remote_copy(
                    src_ref=sums.at[mine],
                    dst_ref=sums.at[mine],
                    send_sem=sum_send,
                    recv_sem=sum_recv,
                    device_id=place(lax.rem(me + step, count)),
                    device_id_type=MESH,
                ).start()
                return carry

            lax.fori_loop(1, count, send_sum, 0)

    early = pairs // 8
    lax.fori_loop(0, early, send_back, 0)
    sum_parts()
    lax.fori_loop(early, pairs, send_back, 0)
    own_back = pltpu.make_async_copy(returning.at[my_side], back.at[my_side], local_sem.at[1])
    own_back.start()
    own_back.wait()

    context = ctx_in[...]
    prob_sum[...] = jnp.zeros(prob_sum.shape, F32)
    ctx_sum[...] = jnp.zeros(ctx_sum.shape, F32)

    def point_grads(group, carry):
        wait_group(group, back, back_recv)
        prob_grad, ctx_grad = prob_sum[...], ctx_sum[...]
        for part in range(GROUP):
            turn = group * GROUP + part
            met = lax.rem(pairs - turn, pairs)
            code = slot_code[pl.ds(met, 1), :]
            grad = back[pl.ds(2 * turn, 2)].reshape(2 * capacity, channels)
            hot = jnp.right_shift(code, 6) == pix_row
            hot_b = jnp.where(hot, 1.0, 0.0).astype(BF16)
            chosen = jnp.bitwise_and(code, bin_count - 1) == bin_row
            dots = jnp.sum(jnp.where(hot, dot(context, grad, NT), 0.0), axis=0, keepdims=True)
            by_bin = jnp.concatenate(halves(jnp.where(chosen, dots, 0.0)), axis=1)
            prob_grad = prob_grad + dot(by_bin, jnp.concatenate([hot_b, hot_b], axis=1), NT)
            spread = jnp.where(hot, slot_weight[pl.ds(met, 1), :], 0.0).astype(BF16)
            ctx_grad = ctx_grad + dot(spread, grad)
        prob_sum[...] = prob_grad
        ctx_sum[...] = ctx_grad
        return carry

    lax.fori_loop(0, pairs // GROUP, point_grads, 0)
    @pl.when(share < half)
    def _():
        sent_sums = sum_size.at[pl.ds(0, count - 1)]
        pltpu.make_async_copy(sent_sums, sent_sums, sum_send).wait()
        pltpu.make_async_copy(chip_sums.at[rest], chip_sums.at[rest], part_send).wait()
        less = pl.ds(0, owners - 1)
        pltpu.make_async_copy(sums.at[less], sums.at[less], sum_recv).wait()

    @pl.when(share >= half)
    def _():
        pltpu.make_async_copy(chip_sums, chip_sums, part_send).wait()
        pltpu.make_async_copy(sums, sums, sum_recv).wait()

    wait_sent(returning, back_send)


def finish_kernel(
    codes, prob, prob_grad, ctx_grad, sums, ctx_weight,
    codes_out, logit_out, feature_out, conv_out, proj_out,
    by_row,
):
    code_dims, cols, rows = codes_out.shape

    def put_codes(step, carry):
        two = codes[0:code_dims, pl.ds(pl.multiple_of(step * 2 * cols, 2 * cols), 2 * cols)]
        for r in range(2):
            by_row[pl.ds(2 * step + r, code_dims, stride=rows), :] = two[
                :, r * cols : (r + 1) * cols
            ]
        return carry

    lax.fori_loop(0, rows // 2, put_codes, 0, unroll=4)
    for q in range(code_dims):
        codes_out[q] = by_row[pl.ds(q * rows, rows), :].T
    chance, grad = prob[...], prob_grad[...]
    logit_out[...] = chance * (grad - jnp.sum(chance * grad, axis=0, keepdims=True))
    feature_out[...] = dot(ctx_grad[...].astype(BF16), ctx_weight[...], NT).astype(BF16)
    for share in range(conv_out.shape[0] // SHARE):
        conv_out[pl.ds(share * SHARE, SHARE), :] = sums[share].astype(F32)
    proj_out[...] = sums[conv_out.shape[0] // SHARE].astype(F32)[0:code_dims]


def per_device(
    features,
    depth_logits,
    ctx_weight,
    point_pixel,
    point_bin,
    segment_count,
    slot_cell,
    conv_weight,
    proj_weight,
    level_count,
    code_grad,
):
    _, count, capacity = slot_cell.shape
    code_dims, rows, cols = code_grad.shape
    bin_count, pix_count = depth_logits.shape
    feature_dims, channels = ctx_weight.shape
    pixels = point_pixel.reshape(-1, LANES)
    bins = point_bin.reshape(-1, LANES)
    all_cells = rows * cols
    owners = (9 * channels // SHARE + 2) // 2 * 2
    pairs = count // 2
    run = all_cells // FOLD
    vmem = pl.BlockSpec(memory_space=pltpu.VMEM)
    smem = pl.BlockSpec(memory_space=pltpu.SMEM)
    wide = pltpu.VMEM(((rows + 2) * cols, 3 * channels), BF16)
    blocks = pltpu.VMEM((count, capacity, channels), BF16)
    doubled = jax.ShapeDtypeStruct((12 * channels, 2 * channels), BF16)
    dma = pltpu.SemaphoreType.DMA
    cells = slot_cell[0].T
    lifted, slot_code, slot_weight, prob, context, weight_two, back_two, proj_two, slopes = (
        pl.pallas_call(
            lift_kernel,
            out_shape=(
                jax.ShapeDtypeStruct((all_cells, channels), BF16),
                jax.ShapeDtypeStruct((pairs, LANES), I32),
                jax.ShapeDtypeStruct((pairs, LANES), F32),
                jax.ShapeDtypeStruct((bin_count, pix_count), F32),
                jax.ShapeDtypeStruct((pix_count, channels), BF16),
                doubled,
                doubled,
                jax.ShapeDtypeStruct((16, channels), F32),
                jax.ShapeDtypeStruct((8, all_cells), F32),
            ),
            in_specs=[smem] + [vmem] * 9,
            out_specs=(vmem,) * 9,
            scratch_shapes=[
                pltpu.VMEM((pairs, 2 * capacity), I32),
                pltpu.VMEM((count, capacity), I32),
                pltpu.VMEM((code_dims * rows, cols), F32),
                pltpu.SMEM((count,), I32),
                pltpu.VMEM(pixels.shape, I32),
                blocks,
                blocks,
                pltpu.VMEM((run, FOLD * channels), F32),
                pltpu.VMEM((run, GROUP * LANES), BF16),
                pltpu.VMEM((GROUP * LANES, FOLD * channels), BF16),
                dma,
                dma,
                dma((pairs // GROUP,)),
            ],
            compiler_params=pltpu.CompilerParams(
                collective_id=0, has_side_effects=True, vmem_limit_bytes=VMEM_LIMIT
            ),
            name="lift",
        )(
            segment_count,
            features,
            depth_logits,
            ctx_weight,
            pixels,
            bins,
            cells,
            conv_weight.reshape(9 * channels, channels),
            proj_weight.T,
            code_grad.transpose(0, 2, 1),
        )
    )
    codes, prob_grad, ctx_grad, sums = pl.pallas_call(
        tile_kernel,
        out_shape=(
            jax.ShapeDtypeStruct((8, all_cells), F32),
            jax.ShapeDtypeStruct((bin_count, pix_count), F32),
            jax.ShapeDtypeStruct((pix_count, channels), F32),
            jax.ShapeDtypeStruct((owners, SHARE, channels), BF16),
        ),
        in_specs=[smem] + [vmem] * 9 + [pl.BlockSpec(memory_space=pl.ANY)],
        out_specs=(vmem,) * 4,
        scratch_shapes=[
            pltpu.SMEM((capacity, count), I32),
            blocks,
            blocks,
            pltpu.VMEM(((rows + 2) * PITCH, channels), F32),
            wide,
            wide,
            pltpu.VMEM((all_cells, channels), F32),
            pltpu.VMEM((2, rows, channels), BF16),
            pltpu.VMEM((2, cols, channels), BF16),
            pltpu.VMEM((2, 8, rows, channels), BF16),
            pltpu.VMEM((2 * capacity, channels), F32),
            pltpu.VMEM((owners, SHARE, channels), F32),
            pltpu.VMEM((owners // 2, SHARE, channels), F32),
            pltpu.VMEM((owners // 2, SHARE, channels), BF16),
            pltpu.VMEM((count // 2, SHARE, channels), BF16),
            pltpu.VMEM((count, SHARE, channels), BF16),
            pltpu.VMEM((channels, 9 * channels), F32),
            dma((2,)),
            dma,
            dma((pairs // GROUP,)),
            dma((2, 8)),
            dma((2, 8)),
            dma,
            dma,
            dma,
            dma,
            dma,
            dma,
        ],
        compiler_params=pltpu.CompilerParams(
            collective_id=1, has_side_effects=True, vmem_limit_bytes=VMEM_LIMIT
        ),
        name="tile",
    )(
        level_count,
        lifted,
        slot_code,
        slot_weight,
        prob,
        context,
        weight_two,
        back_two,
        proj_two,
        slopes,
        cells,
    )
    codes_out, grad_logits, grad_features, grad_conv, grad_proj = pl.pallas_call(
        finish_kernel,
        out_shape=(
            jax.ShapeDtypeStruct((code_dims, cols, rows), F32),
            jax.ShapeDtypeStruct((bin_count, pix_count), F32),
            jax.ShapeDtypeStruct((pix_count, feature_dims), BF16),
            jax.ShapeDtypeStruct((9 * channels, channels), F32),
            jax.ShapeDtypeStruct((code_dims, channels), F32),
        ),
        in_specs=[vmem] * 6,
        out_specs=(vmem,) * 5,
        scratch_shapes=[pltpu.VMEM((code_dims * rows, cols), F32)],
        compiler_params=pltpu.CompilerParams(vmem_limit_bytes=VMEM_LIMIT),
        name="finish",
    )(codes, prob, prob_grad, ctx_grad, sums, ctx_weight)
    return (
        codes_out.transpose(0, 2, 1),
        grad_logits,
        grad_features,
        grad_conv.reshape(conv_weight.shape),
        grad_proj.T,
    )


def solution(mesh):
    return jax.shard_map(
        per_device,
        mesh=mesh,
        in_specs=(
            P(("bx", "by"), None),
            P(None, ("bx", "by")),
            P(),
            P(("bx", "by")),
            P(("bx", "by")),
            P(("bx", "by"), None),
            P(("bx", "by"), None, None),
            P(),
            P(),
            P(),
            P(None, "bx", "by"),
        ),
        out_specs=(P(None, "bx", "by"), P(None, ("bx", "by")), P(("bx", "by"), None), P(), P()),
        check_vma=False,
    )
```

```python
import jax
import jax.numpy as jnp
from jax import lax
from jax.experimental import pallas as pl
from jax.experimental.pallas import tpu as pltpu
from jax.sharding import PartitionSpec as P

epsilon = 1e-05
MESH = pl.DeviceIdType.MESH
F32 = jnp.float32
BF16 = jnp.bfloat16
I32 = jnp.int32
VMEM_LIMIT = 60 * 2**20
NT = (((1,), (1,)), ((), ()))
TN = (((0,), (0,)), ((), ()))
LANES = 128
PITCH = 80
STRIDE = 37
GROUP = 8
FOLD = 8
ENCODE_ROWS = 64
BACK_ROWS = 64
SPAN = 2048
SHARE = 16
DIRECTIONS = ((-1, 0), (1, 0), (0, -1), (0, 1), (-1, -1), (-1, 1), (1, -1), (1, 1))


def dot(left, right, dims=(((1,), (0,)), ((), ()))):
    return lax.dot_general(left, right, dims, preferred_element_type=F32)


def halves(value):
    high = value.astype(BF16)
    return high, (value - high.astype(F32)).astype(BF16)


def place(index):
    cols = lax.axis_size("by")
    return (lax.div(index, cols), lax.rem(index, cols))


def grid_place():
    return lax.axis_index("bx"), lax.axis_index("by"), lax.axis_size("bx"), lax.axis_size("by")


def inside(dx, dy):
    bx, by, nx, ny = grid_place()
    x, y = bx + dx, by + dy
    return (x >= 0) & (x < nx) & (y >= 0) & (y < ny)


def lane_iota(rows):
    return lax.broadcasted_iota(I32, (rows, LANES), 1)


def row_iota(rows):
    return lax.broadcasted_iota(I32, (rows, LANES), 0)


def halo_copies(edges, sides, landed, send_sems, recv_sems):
    bx, by, _, _ = grid_place()
    cols = edges.shape[1]
    depth = sides.shape[1]
    first, last = pl.ds(0, 16), pl.ds(depth - 16, 16)
    pieces = (
        (edges.at[0], landed.at[0, pl.ds(0, cols)]),
        (edges.at[1], landed.at[1, pl.ds(0, cols)]),
        (sides.at[0], landed.at[2]),
        (sides.at[1], landed.at[3]),
        (sides.at[0, first], landed.at[4, first]),
        (sides.at[1, first], landed.at[5, first]),
        (sides.at[0, last], landed.at[6, first]),
        (sides.at[1, last], landed.at[7, first]),
    )
    return [
        pltpu.make_async_remote_copy(
            src_ref=source,
            dst_ref=target,
            send_sem=send_sems.at[way],
            recv_sem=recv_sems.at[way],
            device_id=(bx + dx, by + dy),
            device_id_type=MESH,
        )
        for way, ((dx, dy), (source, target)) in enumerate(zip(DIRECTIONS, pieces))
    ]


def start_halo(copies):
    for (dx, dy), copy in zip(DIRECTIONS, copies):
        pl.when(inside(dx, dy))(copy.start)


def finish_halo(copies, landed, field, rows, cols):
    low = (rows + 1) * PITCH

    def lay(way):
        if way == 0:
            field[pl.ds(low + 8, cols), :] = landed[0, 0:cols].astype(F32)
        elif way == 1:
            field[pl.ds(8, cols), :] = landed[1, 0:cols].astype(F32)
        elif way == 2:
            field[pl.ds(PITCH + 8 + cols, rows, stride=PITCH), :] = landed[2].astype(F32)
        elif way == 3:
            field[pl.ds(PITCH + 7, rows, stride=PITCH), :] = landed[3].astype(F32)
        elif way == 4:
            field[pl.ds(low + 8 + cols, 1), :] = landed[4, 0:16].astype(F32)[0:1]
        elif way == 5:
            field[pl.ds(low + 7, 1), :] = landed[5, 0:16].astype(F32)[0:1]
        elif way == 6:
            field[pl.ds(8 + cols, 1), :] = landed[6, 0:16].astype(F32)[15:16]
        else:
            field[pl.ds(7, 1), :] = landed[7, 0:16].astype(F32)[15:16]

    for way, ((dx, dy), copy) in enumerate(zip(DIRECTIONS, copies)):

        def arrive(way=way, copy=copy):
            copy.wait_recv()
            lay(way)

        pl.when(inside(-dx, -dy))(arrive)
        pl.when(inside(dx, dy))(copy.wait_send)


def clear_border(field, rows, cols):
    channels = field.shape[1]
    zeros = jnp.zeros((PITCH, channels), F32)
    field[pl.ds(0, PITCH), :] = zeros
    field[pl.ds((rows + 1) * PITCH, PITCH), :] = zeros
    for column in (7, 8 + cols):
        field[pl.ds(PITCH + column, rows, stride=PITCH), :] = jnp.zeros((rows, channels), F32)


def fill_borders(field, edges, sides, rows, cols):
    sides[0] = field[pl.ds(PITCH + 8, rows, stride=PITCH), :].astype(BF16)
    sides[1] = field[pl.ds(PITCH + 7 + cols, rows, stride=PITCH), :].astype(BF16)
    edges[0] = field[pl.ds(PITCH + 8, cols), :].astype(BF16)
    edges[1] = field[pl.ds(rows * PITCH + 8, cols), :].astype(BF16)


def spread_columns(field, wide, rows, cols):
    channels = field.shape[1]

    def row(x, carry):
        base = pl.multiple_of(x * PITCH, 8)
        at = pl.ds(pl.multiple_of(x * cols, cols), cols)
        for shift in range(3):
            wide[at, pl.ds(shift * channels, channels)] = field[
                pl.ds(base + 7 + shift, cols), :
            ].astype(BF16)
        return carry

    lax.fori_loop(0, rows + 2, row, 0)


def conv_rows(wide, weight, step, rows, cols):
    channels = weight.shape[1] // 2
    window = jnp.concatenate(
        [
            jnp.concatenate(
                [
                    wide[pl.ds(pl.multiple_of((step * rows + r + tap) * cols, cols), cols), :]
                    for r in range(0, rows, 2)
                ],
                axis=0,
            )
            for tap in range(4)
        ],
        axis=1,
    )
    both = dot(window, weight[...])
    return [
        both[(r // 2) * cols : (r // 2 + 1) * cols, (r % 2) * channels : (r % 2 + 1) * channels]
        for r in range(rows)
    ]


def double_weight(target, tap_weight, depth, channels):
    for tap in range(4):
        at = pl.ds(tap * depth, depth)
        for half in range(2):
            inner = tap - half
            lane = pl.ds(half * channels, channels)
            if 0 <= inner < 3:
                for third in range(3):
                    target[pl.ds(tap * depth + third * channels, channels), lane] = tap_weight(
                        inner, third
                    )
            else:
                target[at, lane] = jnp.zeros((depth, channels), BF16)


def position():
    count = lax.axis_size("bx") * lax.axis_size("by")
    return lax.axis_index("bx") * lax.axis_size("by") + lax.axis_index("by"), count


def greet_all(me, count):
    barrier = pltpu.get_barrier_semaphore()

    def greet(step, carry):
        pl.semaphore_signal(
            barrier, inc=1, device_id=place(lax.rem(me + step, count)), device_id_type=MESH
        )
        return carry

    lax.fori_loop(1, count, greet, 0)
    return barrier


def partner(me, pairs, step):
    return lax.rem(lax.div(me, 2) + lax.rem(step * STRIDE, pairs), pairs)


def source(me, pairs, step):
    return lax.rem(lax.div(me, 2) + pairs - lax.rem(step * STRIDE, pairs), pairs)


def send_pair(me, pairs, step, leaving, landing, sent, received):
    pair = partner(me, pairs, step)
    for side in range(2):
        tile = 2 * pair + side

        @pl.when(tile != me)
        def _(side=side, tile=tile):
            pltpu.make_async_remote_copy(
                src_ref=leaving.at[2 * step + side],
                dst_ref=landing.at[2 * step + lax.rem(me, 2)],
                send_sem=sent,
                recv_sem=received.at[lax.div(step, GROUP)],
                device_id=place(tile),
                device_id_type=MESH,
            ).start()


def wait_group(group, landing, received):
    alone = isinstance(group, int) and group == 0
    blocks = landing.at[pl.ds(0, 2 * GROUP - alone)]
    pltpu.make_async_copy(blocks, blocks, received.at[group]).wait()


def wait_sent(leaving, sent):
    others = pl.ds(0, leaving.shape[0] - 1)
    pltpu.make_async_copy(leaving.at[others], leaving.at[others], sent).wait()


def lift_kernel(
    counts, features, logits, ctx_weight, pixels, bins, cells_in,
    lifted, slot_code, slot_weight, prob_out, ctx_out,
    cells_two, cells_v, starts, point_code, outgoing, arrived, pooled,
    local_sem, send_sem, recv_sem,
):
    me, count = position()
    pairs = count // 2
    my_side = lax.rem(me, 2)
    capacity = cells_in.shape[0]
    all_cells, channels = lifted.shape
    bin_count, pix_count = logits.shape
    barrier = greet_all(me, count)

    context = dot(features[...], ctx_weight[...]).astype(BF16)
    raw = logits[...]
    shifted = jnp.exp(raw - jnp.max(raw, axis=0, keepdims=True))
    prob = shifted / jnp.sum(shifted, axis=0, keepdims=True)
    prob_out[...] = prob
    ctx_out[...] = context
    prob_pair = jnp.concatenate(halves(prob), axis=1)
    ctx_pair = jnp.concatenate([context, context], axis=0)
    point_code[...] = pixels[...] * bin_count + bins[...]
    last_row = pixels.shape[0] - 1

    def start_of(tile, begin):
        starts[tile] = begin
        return begin + counts[0, tile]

    lax.fori_loop(0, count, start_of, 0)
    lane = lane_iota(1)
    pix_row = row_iota(pix_count)
    bin_row = row_iota(bin_count)

    def codes_of(pair):
        sides_codes = []
        for side in range(2):
            tile = 2 * pair + side
            begin = starts[tile]
            offset = jnp.bitwise_and(begin, LANES - 1)
            row = jnp.right_shift(begin, 7)
            here = point_code[pl.ds(jnp.minimum(row, last_row), 1), :]
            after = point_code[pl.ds(jnp.minimum(row + 1, last_row), 1), :]
            turned = pltpu.roll(
                jnp.where(lane >= offset, here, after),
                jnp.bitwise_and(side * capacity + LANES - offset, LANES - 1),
                axis=1,
            )
            sides_codes.append(jnp.where(lane - side * capacity < counts[0, tile], turned, -1))
        return jnp.where(lane < capacity, sides_codes[0], sides_codes[1])

    def find_codes(step, carry):
        for part in range(GROUP):
            turn = step * GROUP + part
            slot_code[pl.ds(turn, 1), :] = codes_of(partner(me, pairs, turn))
        return carry

    lax.fori_loop(0, pairs // GROUP, find_codes, 0)

    pl.semaphore_wait(barrier, count - 1)

    def lift(step, carry):
        code = slot_code[pl.ds(pl.multiple_of(step * GROUP, GROUP), GROUP), :]
        code = jnp.concatenate([code[part : part + 1] for part in range(GROUP)], axis=1)
        wide_rows = lax.broadcasted_iota(I32, (pix_count, GROUP * LANES), 0)
        hot = jnp.right_shift(code, 6) == wide_rows
        hot_b = jnp.where(hot, 1.0, 0.0).astype(BF16)
        picked = dot(prob_pair, jnp.concatenate([hot_b, hot_b], axis=0))
        chosen = jnp.bitwise_and(code, bin_count - 1) == wide_rows[:bin_count]
        point_weight = jnp.sum(jnp.where(chosen, picked, 0.0), axis=0, keepdims=True)
        for part in range(GROUP):
            slot_weight[pl.ds(step * GROUP + part, 1), :] = point_weight[
                :, part * LANES : (part + 1) * LANES
            ]
        spread = jnp.concatenate(halves(jnp.where(hot, point_weight, 0.0)), axis=0)
        value = dot(spread, ctx_pair, TN).astype(BF16)
        outgoing[pl.ds(2 * GROUP * step, 2 * GROUP)] = value.reshape(
            2 * GROUP, capacity, channels
        )
        for part in range(GROUP):
            send_pair(me, pairs, step * GROUP + part, outgoing, arrived, send_sem, recv_sem)
        return carry

    lax.fori_loop(0, pairs // GROUP, lift, 0)
    own = pltpu.make_async_copy(outgoing.at[my_side], arrived.at[my_side], local_sem)
    own.start()

    cells_v[...] = cells_in[...].T
    cells_two[...] = jnp.concatenate(
        [cells_v[pl.ds(side, pairs, stride=2), :] for side in range(2)], axis=1
    )
    run = all_cells // FOLD
    run_shift = run.bit_length() - 1
    run_row = row_iota(run)
    own.wait()

    pooled[...] = jnp.zeros(pooled.shape, F32)
    wait_group(0, arrived, recv_sem)

    def pool(group, carry):
        pl.when(group > 0)(lambda: wait_group(group, arrived, recv_sem))
        hot_cells, folded = [], []
        for part in range(GROUP):
            turn = group * GROUP + part
            cell = cells_two[pl.ds(source(me, pairs, turn), 1), :]
            hot_cells.append(
                jnp.where(jnp.bitwise_and(cell, run - 1) == run_row, 1.0, 0.0).astype(BF16)
            )
            which = jnp.broadcast_to(jnp.right_shift(cell, run_shift), (LANES, LANES)).T
            value = arrived[pl.ds(2 * turn, 2)].reshape(2 * capacity, channels).astype(F32)
            folded.append(
                jnp.concatenate(
                    [jnp.where(which == fold, value, 0.0).astype(BF16) for fold in range(FOLD)],
                    axis=1,
                )
            )
        pooled[...] += dot(
            jnp.concatenate(hot_cells, axis=1), jnp.concatenate(folded, axis=0)
        )
        return carry

    lax.fori_loop(0, pairs // GROUP, pool, 0)
    for fold in range(FOLD):
        lifted[pl.ds(fold * run, run), :] = pooled[:, pl.ds(fold * channels, channels)].astype(BF16)
    wait_sent(outgoing, send_sem)


def tile_kernel(
    levels, lifted, slot_code, slot_weight, ctx_in, weight, proj, code_grad, cells_in,
    codes_out, prob_sum, ctx_sum, sums,
    cells, returning, back, field, wide, wide_grad, lift_grad, sides, edges, landed, stage,
    parts, paired, chip_sums, gathered, flipped, weight_two, back_two, proj_two, slopes_in,
    by_row, codes,
    local_sem, back_send, back_recv, halo_send, halo_recv,
    pair_send, pair_recv, part_send, part_recv, sum_send, sum_recv, half_send, half_recv,
):
    me, count = position()
    pairs = count // 2
    my_side = lax.rem(me, 2)
    capacity = cells.shape[0]
    channels = lifted.shape[1]
    bin_count, pix_count = prob_sum.shape
    cols = edges.shape[1]
    rows = sides.shape[1]
    code_dims = levels.shape[0]
    depth = 3 * channels
    owners = parts.shape[0]
    full_shares = 9 * channels // SHARE
    all_cells = rows * cols
    barrier = greet_all(me, count)
    to_smem = pltpu.make_async_copy(cells_in, cells, local_sem.at[0])
    to_smem.start()
    pix_row = row_iota(pix_count)
    bin_row = row_iota(bin_count)
    clear_border(field, rows, cols)

    def load_row(x, carry):
        field[pl.ds(pl.multiple_of((x + 1) * PITCH + 8, 8), cols), :] = lifted[
            pl.ds(pl.multiple_of(x * cols, cols), cols), :
        ].astype(F32)
        return carry

    lax.fori_loop(0, rows, load_row, 0)
    fill_borders(field, edges, sides, rows, cols)
    pl.semaphore_wait(barrier, count - 1)
    first = halo_copies(edges, sides, landed.at[0], halo_send.at[0], halo_recv.at[0])
    start_halo(first)
    double_weight(
        weight_two,
        lambda tap, third: weight[pl.ds(tap * depth + third * channels, channels), :],
        depth,
        channels,
    )
    double_weight(
        back_two,
        lambda tap, third: weight[pl.ds((2 - tap) * depth + (2 - third) * channels, channels), :]
        .astype(F32)
        .T.astype(BF16),
        depth,
        channels,
    )
    proj_rows = proj[...].astype(F32)
    proj_two[...] = jnp.zeros(proj_two.shape, F32)
    proj_two[0:code_dims] = proj_rows
    proj_two[8 : 8 + code_dims] = proj_rows
    slopes_in[...] = jnp.zeros(slopes_in.shape, F32)
    for q in range(code_dims):
        by_row[pl.ds(q * rows, rows), :] = code_grad[q].T

    def take_slopes(step, carry):
        two = [by_row[pl.ds(2 * step + r, code_dims, stride=rows), :] for r in range(2)]
        at = pl.ds(pl.multiple_of(step * 2 * cols, 2 * cols), 2 * cols)
        slopes_in[0:code_dims, at] = jnp.concatenate(two, axis=1)
        return carry

    lax.fori_loop(0, rows // 2, take_slopes, 0)
    finish_halo(first, landed.at[0], field, rows, cols)
    spread_columns(field, wide, rows, cols)

    half_levels = jnp.zeros((8, 1), F32)
    for q in range(code_dims):
        half_levels = half_levels + jnp.where(
            lax.broadcasted_iota(I32, (8, 1), 0) == q, (levels[q].astype(F32) - 1.0) * 0.5, 0.0
        )
    proj_both_rows = proj_two[...].astype(BF16)
    block = ENCODE_ROWS * cols

    def encode(step, proj_sum):
        origin = pl.multiple_of(step * block, block)
        conv_out = jnp.concatenate(conv_rows(wide, weight_two, step, ENCODE_ROWS, cols), axis=0)
        inv_rms = lax.rsqrt(jnp.mean(conv_out * conv_out, axis=-1, keepdims=True) + epsilon)
        normed = conv_out * inv_rms
        gate = 0.5 + 0.5 * jnp.tanh(0.5 * normed)
        active = normed * gate
        hidden = active.astype(BF16)
        squash = jnp.tanh(dot(proj_both_rows, hidden, NT)[:8])
        codes[:, pl.ds(origin, block)] = half_levels * squash
        slope = slopes_in[:, pl.ds(origin, block)] * half_levels * (1.0 - squash * squash)
        slope_high = slope.astype(BF16).astype(F32)
        slope_pair = jnp.concatenate([slope_high, slope - slope_high], axis=0).astype(BF16)
        proj_both = dot(slope_pair, hidden)
        hidden_grad = dot(slope_pair, proj_both_rows, TN)
        norm_grad = hidden_grad * (gate + active * (1.0 - gate))
        mixed = jnp.mean(norm_grad * normed, axis=-1, keepdims=True)
        conv_grad = inv_rms * (norm_grad - normed * mixed)
        for r in range(ENCODE_ROWS):
            at = pl.multiple_of((step * ENCODE_ROWS + r + 1) * PITCH + 8, 8)
            field[pl.ds(at, cols), :] = conv_grad[r * cols : (r + 1) * cols]
        wide_grad[pl.ds(origin + cols, block), pl.ds(channels, channels)] = conv_grad.astype(BF16)
        return proj_sum + proj_both[:8] + proj_both[8:]

    proj_sum = lax.fori_loop(0, rows // ENCODE_ROWS, encode, jnp.zeros((8, channels), F32))
    fill_borders(field, edges, sides, rows, cols)
    second = halo_copies(edges, sides, landed.at[1], halo_send.at[1], halo_recv.at[1])
    start_halo(second)

    flipped[...] = jnp.zeros(flipped.shape, F32)

    def weight_grad(step, carry):
        origin = pl.multiple_of(step * SPAN, SPAN)
        grad_t = wide_grad[pl.ds(origin + cols, SPAN), pl.ds(channels, channels)].T
        for tap in range(3):
            flipped[:, pl.ds(tap * depth, depth)] += dot(
                grad_t, wide[pl.ds(origin + tap * cols, SPAN), :]
            )
        return carry

    lax.fori_loop(0, all_cells // SPAN, weight_grad, 0)
    for tap in range(9):
        parts[pl.ds(tap * (channels // SHARE), channels // SHARE)] = flipped[
            :, pl.ds(tap * channels, channels)
        ].T.reshape(channels // SHARE, SHARE, channels)
    parts[full_shares] = jnp.concatenate(
        [proj_sum, jnp.zeros((SHARE - 8, channels), F32)], axis=0
    )
    for spare in range(full_shares + 1, owners):
        parts[spare] = jnp.zeros((SHARE, channels), F32)

    chips, half = count // 2, owners // 2
    bx, by, _, row_devices = grid_place()
    core = lax.rem(bx, 2)
    chip = lax.div(bx, 2) * row_devices + by
    to_sibling = pltpu.make_async_remote_copy(
        src_ref=parts.at[pl.ds((1 - core) * half, half)],
        dst_ref=paired,
        send_sem=pair_send,
        recv_sem=pair_recv,
        device_id=(bx + 1 - 2 * core, by),
        device_id_type=MESH,
    )
    to_sibling.start()
    my_half = sums.at[pl.ds(core * half, half)]
    half_to_sibling = pltpu.make_async_remote_copy(
        src_ref=my_half,
        dst_ref=my_half,
        send_sem=half_send,
        recv_sem=half_recv,
        device_id=(bx + 1 - 2 * core, by),
        device_id_type=MESH,
    )

    def same_core(one):
        return (2 * lax.div(one, row_devices) + core, lax.rem(one, row_devices))

    def share_of(one):
        return lax.rem(one * STRIDE, chips)

    def send_part(step, carry):
        target = lax.rem(chip + step, chips)
        share = share_of(target)

        @pl.when(share < half)
        def _():
            pltpu.make_async_remote_copy(
                src_ref=chip_sums.at[share],
                dst_ref=gathered.at[chip],
                send_sem=part_send,
                recv_sem=part_recv,
                device_id=same_core(target),
                device_id_type=MESH,
            ).start()

        return carry

    finish_halo(second, landed.at[1], field, rows, cols)
    spread_columns(field, wide_grad, rows, cols)
    to_sibling.wait()
    chip_sums[...] = (parts[pl.ds(core * half, half)] + paired[...]).astype(BF16)
    lax.fori_loop(1, chips, send_part, 0)

    def conv_back(step, carry):
        for r, row in enumerate(conv_rows(wide_grad, back_two, step, BACK_ROWS, cols)):
            at = pl.multiple_of((step * BACK_ROWS + r) * cols, cols)
            lift_grad[pl.ds(at, cols), :] = row
        return carry

    lax.fori_loop(0, rows // BACK_ROWS, conv_back, 0)

    to_smem.wait()

    def send_back(turn, carry):
        pair = partner(me, pairs, turn)
        for side in range(2):
            for slot in range(capacity):
                stage[pl.ds(side * capacity + slot, 1), :] = lift_grad[
                    pl.ds(cells[slot, 2 * pair + side], 1), :
                ]
        returning[pl.ds(2 * turn, 2)] = stage[...].astype(BF16).reshape(2, capacity, channels)
        send_pair(me, pairs, turn, returning, back, back_send, back_recv)
        return carry

    share = share_of(chip)
    mine = core * half + share
    others = pl.ds(0, chips - 1)
    rest = pl.ds(0, half - 1)

    def sum_parts():
        @pl.when(share < half)
        def _():
            pltpu.make_async_copy(gathered.at[others], gathered.at[others], part_recv).wait()
            gathered[chip] = chip_sums[share]

            def add(sender, total):
                return total + gathered[sender].astype(F32)

            sums[mine] = lax.fori_loop(0, chips, add, jnp.zeros((SHARE, channels), F32)).astype(
                BF16
            )

            def send_sum(step, carry):
                pltpu.make_async_remote_copy(
                    src_ref=sums.at[mine],
                    dst_ref=sums.at[mine],
                    send_sem=sum_send,
                    recv_sem=sum_recv,
                    device_id=same_core(lax.rem(chip + step, chips)),
                    device_id_type=MESH,
                ).start()
                return carry

            lax.fori_loop(1, chips, send_sum, 0)

    early = pairs // 8
    lax.fori_loop(0, early, send_back, 0)
    sum_parts()
    lax.fori_loop(early, pairs, send_back, 0)
    own_back = pltpu.make_async_copy(returning.at[my_side], back.at[my_side], local_sem.at[1])
    own_back.start()
    own_back.wait()

    def put_codes(step, carry):
        two = codes[0:code_dims, pl.ds(pl.multiple_of(step * 2 * cols, 2 * cols), 2 * cols)]
        for r in range(2):
            by_row[pl.ds(2 * step + r, code_dims, stride=rows), :] = two[
                :, r * cols : (r + 1) * cols
            ]
        return carry

    lax.fori_loop(0, rows // 2, put_codes, 0)
    for q in range(code_dims):
        codes_out[q] = by_row[pl.ds(q * rows, rows), :].T

    context = ctx_in[...]
    prob_sum[...] = jnp.zeros(prob_sum.shape, F32)
    ctx_sum[...] = jnp.zeros(ctx_sum.shape, F32)

    def point_grads(group, carry):
        wait_group(group, back, back_recv)
        add_points(group)
        return carry

    def add_points(group):
        prob_grad, ctx_grad = prob_sum[...], ctx_sum[...]
        for part in range(GROUP):
            turn = group * GROUP + part
            met = lax.rem(pairs - turn, pairs)
            code = slot_code[pl.ds(met, 1), :]
            grad = back[pl.ds(2 * turn, 2)].reshape(2 * capacity, channels)
            hot = jnp.right_shift(code, 6) == pix_row
            hot_b = jnp.where(hot, 1.0, 0.0).astype(BF16)
            chosen = jnp.bitwise_and(code, bin_count - 1) == bin_row
            dots = jnp.sum(jnp.where(hot, dot(context, grad, NT), 0.0), axis=0, keepdims=True)
            by_bin = jnp.concatenate(halves(jnp.where(chosen, dots, 0.0)), axis=1)
            prob_grad = prob_grad + dot(by_bin, jnp.concatenate([hot_b, hot_b], axis=1), NT)
            spread = jnp.where(hot, slot_weight[pl.ds(met, 1), :], 0.0).astype(BF16)
            ctx_grad = ctx_grad + dot(spread, grad)
        prob_sum[...] = prob_grad
        ctx_sum[...] = ctx_grad

    wait_group(0, back, back_recv)
    add_points(0)

    late = pairs // GROUP - 2
    lax.fori_loop(1, late, point_grads, 0)

    @pl.when(share < half)
    def _():
        pltpu.make_async_copy(gathered.at[others], gathered.at[others], sum_send).wait()
        pltpu.make_async_copy(chip_sums.at[rest], chip_sums.at[rest], part_send).wait()
        pltpu.make_async_copy(chip_sums.at[rest], chip_sums.at[rest], sum_recv).wait()

    @pl.when(share >= half)
    def _():
        pltpu.make_async_copy(chip_sums, chip_sums, part_send).wait()
        pltpu.make_async_copy(chip_sums, chip_sums, sum_recv).wait()

    half_to_sibling.start()
    lax.fori_loop(late, pairs // GROUP, point_grads, 0)
    half_to_sibling.wait()
    wait_sent(returning, back_send)


def finish_kernel(
    codes, prob, prob_grad, ctx_grad, sums, ctx_weight,
    codes_out, logit_out, feature_out, conv_out, proj_out,
):
    code_dims = codes_out.shape[0]
    codes_out[...] = codes[...]
    chance, grad = prob[...], prob_grad[...]
    logit_out[...] = chance * (grad - jnp.sum(chance * grad, axis=0, keepdims=True))
    feature_out[...] = dot(ctx_grad[...].astype(BF16), ctx_weight[...], NT).astype(BF16)
    for share in range(conv_out.shape[0] // SHARE):
        conv_out[pl.ds(share * SHARE, SHARE), :] = sums[share].astype(F32)
    proj_out[...] = sums[conv_out.shape[0] // SHARE].astype(F32)[0:code_dims]


def per_device(
    features,
    depth_logits,
    ctx_weight,
    point_pixel,
    point_bin,
    segment_count,
    slot_cell,
    conv_weight,
    proj_weight,
    level_count,
    code_grad,
):
    _, count, capacity = slot_cell.shape
    code_dims, rows, cols = code_grad.shape
    bin_count, pix_count = depth_logits.shape
    feature_dims, channels = ctx_weight.shape
    pixels = point_pixel.reshape(-1, LANES)
    bins = point_bin.reshape(-1, LANES)
    all_cells = rows * cols
    owners = (9 * channels // SHARE + 2) // 2 * 2
    pairs = count // 2
    run = all_cells // FOLD
    vmem = pl.BlockSpec(memory_space=pltpu.VMEM)
    smem = pl.BlockSpec(memory_space=pltpu.SMEM)
    wide = pltpu.VMEM(((rows + 2) * cols, 3 * channels), BF16)
    blocks = pltpu.VMEM((count, capacity, channels), BF16)
    doubled = pltpu.VMEM((12 * channels, 2 * channels), BF16)
    weight = conv_weight.reshape(9 * channels, channels)
    dma = pltpu.SemaphoreType.DMA
    cells = slot_cell[0].T
    lifted, slot_code, slot_weight, prob, context = (
        pl.pallas_call(
            lift_kernel,
            out_shape=(
                jax.ShapeDtypeStruct((all_cells, channels), BF16),
                jax.ShapeDtypeStruct((pairs, LANES), I32),
                jax.ShapeDtypeStruct((pairs, LANES), F32),
                jax.ShapeDtypeStruct((bin_count, pix_count), F32),
                jax.ShapeDtypeStruct((pix_count, channels), BF16),
            ),
            in_specs=[smem] + [vmem] * 6,
            out_specs=(vmem,) * 5,
            scratch_shapes=[
                pltpu.VMEM((pairs, 2 * capacity), I32),
                pltpu.VMEM((count, capacity), I32),
                pltpu.SMEM((count,), I32),
                pltpu.VMEM(pixels.shape, I32),
                blocks,
                blocks,
                pltpu.VMEM((run, FOLD * channels), F32),
                dma,
                dma,
                dma((pairs // GROUP,)),
            ],
            compiler_params=pltpu.CompilerParams(
                collective_id=0, has_side_effects=True, vmem_limit_bytes=VMEM_LIMIT
            ),
            name="lift",
        )(
            segment_count,
            features,
            depth_logits,
            ctx_weight,
            pixels,
            bins,
            cells,
        )
    )
    codes, prob_grad, ctx_grad, sums = pl.pallas_call(
        tile_kernel,
        out_shape=(
            jax.ShapeDtypeStruct((code_dims, cols, rows), F32),
            jax.ShapeDtypeStruct((bin_count, pix_count), F32),
            jax.ShapeDtypeStruct((pix_count, channels), F32),
            jax.ShapeDtypeStruct((owners, SHARE, channels), BF16),
        ),
        in_specs=[smem] + [vmem] * 7 + [pl.BlockSpec(memory_space=pl.ANY)],
        out_specs=(vmem,) * 4,
        scratch_shapes=[
            pltpu.SMEM((capacity, count), I32),
            blocks,
            blocks,
            pltpu.VMEM(((rows + 2) * PITCH, channels), F32),
            wide,
            wide,
            pltpu.VMEM((all_cells, channels), F32),
            pltpu.VMEM((2, rows, channels), BF16),
            pltpu.VMEM((2, cols, channels), BF16),
            pltpu.VMEM((2, 8, rows, channels), BF16),
            pltpu.VMEM((2 * capacity, channels), F32),
            pltpu.VMEM((owners, SHARE, channels), F32),
            pltpu.VMEM((owners // 2, SHARE, channels), F32),
            pltpu.VMEM((owners // 2, SHARE, channels), BF16),
            pltpu.VMEM((count // 2, SHARE, channels), BF16),
            pltpu.VMEM((channels, 9 * channels), F32),
            doubled,
            doubled,
            pltpu.VMEM((16, channels), F32),
            pltpu.VMEM((8, all_cells), F32),
            pltpu.VMEM((code_dims * rows, cols), F32),
            pltpu.VMEM((8, all_cells), F32),
            dma((2,)),
            dma,
            dma((pairs // GROUP,)),
            dma((2, 8)),
            dma((2, 8)),
            dma,
            dma,
            dma,
            dma,
            dma,
            dma,
            dma,
            dma,
        ],
        compiler_params=pltpu.CompilerParams(
            collective_id=1, has_side_effects=True, vmem_limit_bytes=VMEM_LIMIT
        ),
        name="tile",
    )(
        level_count,
        lifted,
        slot_code,
        slot_weight,
        context,
        weight,
        proj_weight.T,
        code_grad.transpose(0, 2, 1),
        cells,
    )
    codes_out, grad_logits, grad_features, grad_conv, grad_proj = pl.pallas_call(
        finish_kernel,
        out_shape=(
            jax.ShapeDtypeStruct((code_dims, cols, rows), F32),
            jax.ShapeDtypeStruct((bin_count, pix_count), F32),
            jax.ShapeDtypeStruct((pix_count, feature_dims), BF16),
            jax.ShapeDtypeStruct((9 * channels, channels), F32),
            jax.ShapeDtypeStruct((code_dims, channels), F32),
        ),
        in_specs=[vmem] * 6,
        out_specs=(vmem,) * 5,
        compiler_params=pltpu.CompilerParams(vmem_limit_bytes=VMEM_LIMIT),
        name="finish",
    )(codes, prob, prob_grad, ctx_grad, sums, ctx_weight)
    return (
        codes_out.transpose(0, 2, 1),
        grad_logits,
        grad_features,
        grad_conv.reshape(conv_weight.shape),
        grad_proj.T,
    )


def solution(mesh):
    return jax.shard_map(
        per_device,
        mesh=mesh,
        in_specs=(
            P(("bx", "by"), None),
            P(None, ("bx", "by")),
            P(),
            P(("bx", "by")),
            P(("bx", "by")),
            P(("bx", "by"), None),
            P(("bx", "by"), None, None),
            P(),
            P(),
            P(),
            P(None, "bx", "by"),
        ),
        out_specs=(P(None, "bx", "by"), P(None, ("bx", "by")), P(("bx", "by"), None), P(), P()),
        check_vma=False,
    )
```

```python
import jax
import jax.numpy as jnp
from jax import lax
from jax.experimental import pallas as pl
from jax.experimental.pallas import tpu as pltpu
from jax.sharding import PartitionSpec as P

epsilon = 1e-05
MESH = pl.DeviceIdType.MESH
F32 = jnp.float32
BF16 = jnp.bfloat16
I32 = jnp.int32
VMEM_LIMIT = 60 * 2**20
NT = (((1,), (1,)), ((), ()))
TN = (((0,), (0,)), ((), ()))
LANES = 128
PITCH = 80
STRIDE = 11
AHEAD = 4
GROUP = 8
FOLD = 8
ENCODE_ROWS = 64
BACK_ROWS = 64
SPAN = 2048
SHARE = 16
DIRECTIONS = ((-1, 0), (1, 0), (0, -1), (0, 1), (-1, -1), (-1, 1), (1, -1), (1, 1))


def dot(left, right, dims=(((1,), (0,)), ((), ()))):
    return lax.dot_general(left, right, dims, preferred_element_type=F32)


def halves(value):
    high = value.astype(BF16)
    return high, (value - high.astype(F32)).astype(BF16)


def shared(index, size):
    return jnp.bitwise_and(index, size - 1)


def parted(index, size):
    return jnp.right_shift(index, size.bit_length() - 1)


def place(index):
    cols = lax.axis_size("by")
    return (parted(index, cols), shared(index, cols))


def grid_place():
    return lax.axis_index("bx"), lax.axis_index("by"), lax.axis_size("bx"), lax.axis_size("by")


def inside(dx, dy):
    bx, by, nx, ny = grid_place()
    x, y = bx + dx, by + dy
    return (x >= 0) & (x < nx) & (y >= 0) & (y < ny)


def lane_iota(rows):
    return lax.broadcasted_iota(I32, (rows, LANES), 1)


def row_iota(rows):
    return lax.broadcasted_iota(I32, (rows, LANES), 0)


def halo_copies(edges, sides, landed, send_sems, recv_sems):
    bx, by, _, _ = grid_place()
    cols = edges.shape[1]
    depth = sides.shape[1]
    first, last = pl.ds(0, 16), pl.ds(depth - 16, 16)
    pieces = (
        (edges.at[0], landed.at[0, pl.ds(0, cols)]),
        (edges.at[1], landed.at[1, pl.ds(0, cols)]),
        (sides.at[0], landed.at[2]),
        (sides.at[1], landed.at[3]),
        (sides.at[0, first], landed.at[4, first]),
        (sides.at[1, first], landed.at[5, first]),
        (sides.at[0, last], landed.at[6, first]),
        (sides.at[1, last], landed.at[7, first]),
    )
    return [
        pltpu.make_async_remote_copy(
            src_ref=source,
            dst_ref=target,
            send_sem=send_sems.at[way],
            recv_sem=recv_sems.at[way],
            device_id=(bx + dx, by + dy),
            device_id_type=MESH,
        )
        for way, ((dx, dy), (source, target)) in enumerate(zip(DIRECTIONS, pieces))
    ]


def start_halo(copies):
    for (dx, dy), copy in zip(DIRECTIONS, copies):
        pl.when(inside(dx, dy))(copy.start)


def finish_halo(copies, landed, field, rows, cols):
    low = (rows + 1) * PITCH

    def lay(way):
        if way == 0:
            field[pl.ds(low + 8, cols), :] = landed[0, 0:cols].astype(F32)
        elif way == 1:
            field[pl.ds(8, cols), :] = landed[1, 0:cols].astype(F32)
        elif way == 2:
            field[pl.ds(PITCH + 8 + cols, rows, stride=PITCH), :] = landed[2].astype(F32)
        elif way == 3:
            field[pl.ds(PITCH + 7, rows, stride=PITCH), :] = landed[3].astype(F32)
        elif way == 4:
            field[pl.ds(low + 8 + cols, 1), :] = landed[4, 0:16].astype(F32)[0:1]
        elif way == 5:
            field[pl.ds(low + 7, 1), :] = landed[5, 0:16].astype(F32)[0:1]
        elif way == 6:
            field[pl.ds(8 + cols, 1), :] = landed[6, 0:16].astype(F32)[15:16]
        else:
            field[pl.ds(7, 1), :] = landed[7, 0:16].astype(F32)[15:16]

    for way, ((dx, dy), copy) in enumerate(zip(DIRECTIONS, copies)):

        def arrive(way=way, copy=copy):
            copy.wait_recv()
            lay(way)

        pl.when(inside(-dx, -dy))(arrive)
        pl.when(inside(dx, dy))(copy.wait_send)


def clear_border(field, rows, cols):
    channels = field.shape[1]
    zeros = jnp.zeros((PITCH, channels), F32)
    field[pl.ds(0, PITCH), :] = zeros
    field[pl.ds((rows + 1) * PITCH, PITCH), :] = zeros
    for column in (7, 8 + cols):
        field[pl.ds(PITCH + column, rows, stride=PITCH), :] = jnp.zeros((rows, channels), F32)


def fill_borders(field, edges, sides, rows, cols):
    sides[0] = field[pl.ds(PITCH + 8, rows, stride=PITCH), :].astype(BF16)
    sides[1] = field[pl.ds(PITCH + 7 + cols, rows, stride=PITCH), :].astype(BF16)
    edges[0] = field[pl.ds(PITCH + 8, cols), :].astype(BF16)
    edges[1] = field[pl.ds(rows * PITCH + 8, cols), :].astype(BF16)


def spread_columns(field, wide, rows, cols):
    channels = field.shape[1]

    def row(x, carry):
        base = pl.multiple_of(x * PITCH, 8)
        at = pl.ds(pl.multiple_of(x * cols, cols), cols)
        for shift in range(3):
            wide[at, pl.ds(shift * channels, channels)] = field[
                pl.ds(base + 7 + shift, cols), :
            ].astype(BF16)
        return carry

    lax.fori_loop(0, rows + 2, row, 0, unroll=5)


def conv_rows(wide, weight, step, rows, cols):
    channels = weight.shape[1] // 2
    window = jnp.concatenate(
        [
            jnp.concatenate(
                [
                    wide[pl.ds(pl.multiple_of((step * rows + r + tap) * cols, cols), cols), :]
                    for r in range(0, rows, 2)
                ],
                axis=0,
            )
            for tap in range(4)
        ],
        axis=1,
    )
    both = dot(window, weight[...])
    return [
        both[(r // 2) * cols : (r // 2 + 1) * cols, (r % 2) * channels : (r % 2 + 1) * channels]
        for r in range(rows)
    ]


def double_weight(target, tap_weight, depth, channels):
    for tap in range(4):
        at = pl.ds(tap * depth, depth)
        for half in range(2):
            inner = tap - half
            lane = pl.ds(half * channels, channels)
            if 0 <= inner < 3:
                for third in range(3):
                    target[pl.ds(tap * depth + third * channels, channels), lane] = tap_weight(
                        inner, third
                    )
            else:
                target[at, lane] = jnp.zeros((depth, channels), BF16)


def position():
    count = lax.axis_size("bx") * lax.axis_size("by")
    return lax.axis_index("bx") * lax.axis_size("by") + lax.axis_index("by"), count


def greet_all(me, count):
    barrier = pltpu.get_barrier_semaphore()

    def greet(step, carry):
        pl.semaphore_signal(
            barrier, inc=1, device_id=place(shared(me + step, count)), device_id_type=MESH
        )
        return carry

    even = 1 + (count - 1) // 8 * 8
    lax.fori_loop(1, even, greet, 0, unroll=8)
    for step in range(even, count):
        greet(step, 0)
    return barrier


def partner(me, pairs, step):
    return shared(parted(me, 2) + step * STRIDE, pairs)


def source(me, pairs, step):
    return shared(parted(me, 2) + pairs * STRIDE - step * STRIDE, pairs)


def send_pair(me, pairs, step, leaving, landing, sent, received):
    pair = partner(me, pairs, step)
    for side in range(2):
        tile = 2 * pair + side

        @pl.when(tile != me)
        def _(side=side, tile=tile):
            pltpu.make_async_remote_copy(
                src_ref=leaving.at[2 * step + side],
                dst_ref=landing.at[2 * step + shared(me, 2)],
                send_sem=sent,
                recv_sem=received.at[parted(step, GROUP)],
                device_id=place(tile),
                device_id_type=MESH,
            ).start()


def wait_group(group, landing, received):
    alone = isinstance(group, int) and group == 0
    blocks = landing.at[pl.ds(0, 2 * GROUP - alone)]
    pltpu.make_async_copy(blocks, blocks, received.at[group]).wait()


def wait_sent(leaving, sent):
    others = pl.ds(0, leaving.shape[0] - 1)
    pltpu.make_async_copy(leaving.at[others], leaving.at[others], sent).wait()


def lift_kernel(
    counts, features, logits, ctx_weight, pixels, bins, cells_in,
    lifted, slot_code, slot_weight, prob_out, ctx_out,
    cells_two, cells_v, starts, point_code, outgoing, arrived, pooled,
    local_sem, send_sem, recv_sem,
):
    me, count = position()
    pairs = count // 2
    my_side = shared(me, 2)
    capacity = cells_in.shape[0]
    all_cells, channels = lifted.shape
    bin_count, pix_count = logits.shape
    barrier = greet_all(me, count)

    context = dot(features[...], ctx_weight[...]).astype(BF16)
    raw = logits[...]
    shifted = jnp.exp(raw - jnp.max(raw, axis=0, keepdims=True))
    prob = shifted / jnp.sum(shifted, axis=0, keepdims=True)
    prob_out[...] = prob
    ctx_out[...] = context
    prob_pair = jnp.concatenate(halves(prob), axis=1)
    ctx_pair = jnp.concatenate([context, context], axis=0)
    point_code[...] = pixels[...] * bin_count + bins[...]
    last_row = pixels.shape[0] - 1

    def start_of(tile, begin):
        starts[tile] = begin
        return begin + counts[0, tile]

    lax.fori_loop(0, count, start_of, 0, unroll=8)
    lane = lane_iota(1)
    pix_row = row_iota(pix_count)
    bin_row = row_iota(bin_count)

    def codes_of(pair):
        sides_codes = []
        for side in range(2):
            tile = 2 * pair + side
            begin = starts[tile]
            offset = jnp.bitwise_and(begin, LANES - 1)
            row = jnp.right_shift(begin, 7)
            here = point_code[pl.ds(jnp.minimum(row, last_row), 1), :]
            after = point_code[pl.ds(jnp.minimum(row + 1, last_row), 1), :]
            turned = pltpu.roll(
                jnp.where(lane >= offset, here, after),
                jnp.bitwise_and(side * capacity + LANES - offset, LANES - 1),
                axis=1,
            )
            sides_codes.append(jnp.where(lane - side * capacity < counts[0, tile], turned, -1))
        return jnp.where(lane < capacity, sides_codes[0], sides_codes[1])

    pl.semaphore_wait(barrier, count - 1)

    def lift(step, carry):
        found = [codes_of(partner(me, pairs, step * GROUP + part)) for part in range(GROUP)]
        for part in range(GROUP):
            slot_code[pl.ds(step * GROUP + part, 1), :] = found[part]
        code = jnp.concatenate(found, axis=1)
        wide_rows = lax.broadcasted_iota(I32, (pix_count, GROUP * LANES), 0)
        hot = jnp.right_shift(code, 6) == wide_rows
        hot_b = jnp.where(hot, 1.0, 0.0).astype(BF16)
        picked = dot(prob_pair, jnp.concatenate([hot_b, hot_b], axis=0))
        chosen = jnp.bitwise_and(code, bin_count - 1) == wide_rows[:bin_count]
        point_weight = jnp.sum(jnp.where(chosen, picked, 0.0), axis=0, keepdims=True)
        for part in range(GROUP):
            slot_weight[pl.ds(step * GROUP + part, 1), :] = point_weight[
                :, part * LANES : (part + 1) * LANES
            ]
        spread = jnp.concatenate(halves(jnp.where(hot, point_weight, 0.0)), axis=0)
        value = dot(spread, ctx_pair, TN).astype(BF16)
        outgoing[pl.ds(2 * GROUP * step, 2 * GROUP)] = value.reshape(
            2 * GROUP, capacity, channels
        )
        pl.when(step < AHEAD)(lambda: send_group(step))
        return carry

    def send_group(step):
        def send(turn, carry):
            send_pair(me, pairs, turn, outgoing, arrived, send_sem, recv_sem)
            return carry

        lax.fori_loop(step * GROUP, (step + 1) * GROUP, send, 0)

    lax.fori_loop(0, pairs // GROUP, lift, 0)
    own = pltpu.make_async_copy(outgoing.at[my_side], arrived.at[my_side], local_sem)
    own.start()

    cells_v[...] = cells_in[...].T
    cells_two[...] = jnp.concatenate(
        [cells_v[pl.ds(side, pairs, stride=2), :] for side in range(2)], axis=1
    )
    run = all_cells // FOLD
    run_shift = run.bit_length() - 1
    run_row = row_iota(run)
    own.wait()

    pooled[...] = jnp.zeros(pooled.shape, F32)
    wait_group(0, arrived, recv_sem)

    def pool(group, carry):
        pl.when(group + AHEAD < pairs // GROUP)(lambda: send_group(group + AHEAD))
        pl.when(group > 0)(lambda: wait_group(group, arrived, recv_sem))
        hot_cells, folded = [], []
        for part in range(GROUP):
            turn = group * GROUP + part
            cell = cells_two[pl.ds(source(me, pairs, turn), 1), :]
            hot_cells.append(
                jnp.where(jnp.bitwise_and(cell, run - 1) == run_row, 1.0, 0.0).astype(BF16)
            )
            which = jnp.broadcast_to(jnp.right_shift(cell, run_shift), (LANES, LANES)).T
            value = arrived[pl.ds(2 * turn, 2)].reshape(2 * capacity, channels).astype(F32)
            folded.append(
                jnp.concatenate(
                    [jnp.where(which == fold, value, 0.0).astype(BF16) for fold in range(FOLD)],
                    axis=1,
                )
            )
        pooled[...] += dot(
            jnp.concatenate(hot_cells, axis=1), jnp.concatenate(folded, axis=0)
        )
        return carry

    lax.fori_loop(0, pairs // GROUP, pool, 0)
    for fold in range(FOLD):
        lifted[pl.ds(fold * run, run), :] = pooled[:, pl.ds(fold * channels, channels)].astype(BF16)
    wait_sent(outgoing, send_sem)


def tile_kernel(
    levels, lifted_in, slot_code, slot_weight, ctx_in, weight, proj, code_grad, cells_in,
    codes_out, prob_sum, ctx_sum, sums,
    cells, lifted, returning, back, field, wide, wide_grad, lift_grad, sides, edges, landed, stage,
    parts, paired, chip_sums, gathered, flipped, weight_two, back_two, proj_two, slopes_in,
    by_row, codes,
    local_sem, back_send, back_recv, halo_send, halo_recv,
    pair_send, pair_recv, part_send, part_recv, sum_send, sum_recv, half_send, half_recv,
):
    me, count = position()
    pairs = count // 2
    my_side = shared(me, 2)
    capacity = cells.shape[0]
    channels = lifted.shape[1]
    fetch = pltpu.make_async_copy(lifted_in, lifted, local_sem.at[2])
    fetch.start()
    bin_count, pix_count = prob_sum.shape
    cols = edges.shape[1]
    rows = sides.shape[1]
    code_dims = levels.shape[0]
    depth = 3 * channels
    owners = parts.shape[0]
    full_shares = 9 * channels // SHARE
    all_cells = rows * cols
    barrier = greet_all(me, count)
    to_smem = pltpu.make_async_copy(cells_in, cells, local_sem.at[0])
    to_smem.start()
    pix_row = row_iota(pix_count)
    bin_row = row_iota(bin_count)
    clear_border(field, rows, cols)
    fetch.wait()

    def load_row(x, carry):
        field[pl.ds(pl.multiple_of((x + 1) * PITCH + 8, 8), cols), :] = lifted[
            pl.ds(pl.multiple_of(x * cols, cols), cols), :
        ].astype(F32)
        return carry

    lax.fori_loop(0, rows, load_row, 0, unroll=4)
    fill_borders(field, edges, sides, rows, cols)
    pl.semaphore_wait(barrier, count - 1)
    first = halo_copies(edges, sides, landed.at[0], halo_send.at[0], halo_recv.at[0])
    start_halo(first)
    double_weight(
        weight_two,
        lambda tap, third: weight[pl.ds(tap * depth + third * channels, channels), :],
        depth,
        channels,
    )
    double_weight(
        back_two,
        lambda tap, third: weight[pl.ds((2 - tap) * depth + (2 - third) * channels, channels), :]
        .astype(F32)
        .T.astype(BF16),
        depth,
        channels,
    )
    proj_rows = proj[...].astype(F32)
    proj_two[...] = jnp.zeros(proj_two.shape, F32)
    proj_two[0:code_dims] = proj_rows
    proj_two[8 : 8 + code_dims] = proj_rows
    slopes_in[...] = jnp.zeros(slopes_in.shape, F32)
    for q in range(code_dims):
        by_row[pl.ds(q * rows, rows), :] = code_grad[q].T

    def take_slopes(step, carry):
        two = [by_row[pl.ds(2 * step + r, code_dims, stride=rows), :] for r in range(2)]
        at = pl.ds(pl.multiple_of(step * 2 * cols, 2 * cols), 2 * cols)
        slopes_in[0:code_dims, at] = jnp.concatenate(two, axis=1)
        return carry

    lax.fori_loop(0, rows // 2, take_slopes, 0, unroll=4)
    finish_halo(first, landed.at[0], field, rows, cols)
    spread_columns(field, wide, rows, cols)

    half_levels = jnp.zeros((8, 1), F32)
    for q in range(code_dims):
        half_levels = half_levels + jnp.where(
            lax.broadcasted_iota(I32, (8, 1), 0) == q, (levels[q].astype(F32) - 1.0) * 0.5, 0.0
        )
    proj_both_rows = proj_two[...].astype(BF16)
    block = ENCODE_ROWS * cols

    def encode(step, proj_sum):
        origin = pl.multiple_of(step * block, block)
        conv_out = jnp.concatenate(conv_rows(wide, weight_two, step, ENCODE_ROWS, cols), axis=0)
        inv_rms = lax.rsqrt(jnp.mean(conv_out * conv_out, axis=-1, keepdims=True) + epsilon)
        normed = conv_out * inv_rms
        gate = 0.5 + 0.5 * jnp.tanh(0.5 * normed)
        active = normed * gate
        hidden = active.astype(BF16)
        squash = jnp.tanh(dot(proj_both_rows, hidden, NT)[:8])
        codes[:, pl.ds(origin, block)] = half_levels * squash
        slope = slopes_in[:, pl.ds(origin, block)] * half_levels * (1.0 - squash * squash)
        slope_high = slope.astype(BF16).astype(F32)
        slope_pair = jnp.concatenate([slope_high, slope - slope_high], axis=0).astype(BF16)
        proj_both = dot(slope_pair, hidden)
        hidden_grad = dot(slope_pair, proj_both_rows, TN)
        norm_grad = hidden_grad * (gate + active * (1.0 - gate))
        mixed = jnp.mean(norm_grad * normed, axis=-1, keepdims=True)
        conv_grad = inv_rms * (norm_grad - normed * mixed)
        for r in range(ENCODE_ROWS):
            at = pl.multiple_of((step * ENCODE_ROWS + r + 1) * PITCH + 8, 8)
            field[pl.ds(at, cols), :] = conv_grad[r * cols : (r + 1) * cols]
        wide_grad[pl.ds(origin + cols, block), pl.ds(channels, channels)] = conv_grad.astype(BF16)
        return proj_sum + proj_both[:8] + proj_both[8:]

    proj_sum = lax.fori_loop(0, rows // ENCODE_ROWS, encode, jnp.zeros((8, channels), F32))
    fill_borders(field, edges, sides, rows, cols)
    second = halo_copies(edges, sides, landed.at[1], halo_send.at[1], halo_recv.at[1])
    start_halo(second)

    flipped[...] = jnp.zeros(flipped.shape, F32)

    def weight_grad(step, carry):
        origin = pl.multiple_of(step * SPAN, SPAN)
        grad_t = wide_grad[pl.ds(origin + cols, SPAN), pl.ds(channels, channels)].T
        for tap in range(3):
            flipped[:, pl.ds(tap * depth, depth)] += dot(
                grad_t, wide[pl.ds(origin + tap * cols, SPAN), :]
            )
        return carry

    lax.fori_loop(0, all_cells // SPAN, weight_grad, 0)
    for tap in range(9):
        parts[pl.ds(tap * (channels // SHARE), channels // SHARE)] = flipped[
            :, pl.ds(tap * channels, channels)
        ].T.reshape(channels // SHARE, SHARE, channels)
    parts[full_shares] = jnp.concatenate(
        [proj_sum, jnp.zeros((SHARE - 8, channels), F32)], axis=0
    )
    for spare in range(full_shares + 1, owners):
        parts[spare] = jnp.zeros((SHARE, channels), F32)

    chips, half = count // 2, owners // 2
    bx, by, _, row_devices = grid_place()
    core = shared(bx, 2)
    chip = parted(bx, 2) * row_devices + by
    to_sibling = pltpu.make_async_remote_copy(
        src_ref=parts.at[pl.ds((1 - core) * half, half)],
        dst_ref=paired,
        send_sem=pair_send,
        recv_sem=pair_recv,
        device_id=(bx + 1 - 2 * core, by),
        device_id_type=MESH,
    )
    to_sibling.start()
    my_half = sums.at[pl.ds(core * half, half)]
    half_to_sibling = pltpu.make_async_remote_copy(
        src_ref=my_half,
        dst_ref=my_half,
        send_sem=half_send,
        recv_sem=half_recv,
        device_id=(bx + 1 - 2 * core, by),
        device_id_type=MESH,
    )

    def same_core(one):
        return (2 * parted(one, row_devices) + core, shared(one, row_devices))

    def share_of(one):
        return shared(one * STRIDE, chips)

    def send_part(step, carry):
        target = shared(chip + step, chips)
        share = share_of(target)

        @pl.when(share < half)
        def _():
            pltpu.make_async_remote_copy(
                src_ref=chip_sums.at[share],
                dst_ref=gathered.at[chip],
                send_sem=part_send,
                recv_sem=part_recv,
                device_id=same_core(target),
                device_id_type=MESH,
            ).start()

        return carry

    finish_halo(second, landed.at[1], field, rows, cols)
    spread_columns(field, wide_grad, rows, cols)
    to_sibling.wait()
    chip_sums[...] = (parts[pl.ds(core * half, half)] + paired[...]).astype(BF16)
    lax.fori_loop(1, chips, send_part, 0)

    def conv_back(step, carry):
        for r, row in enumerate(conv_rows(wide_grad, back_two, step, BACK_ROWS, cols)):
            at = pl.multiple_of((step * BACK_ROWS + r) * cols, cols)
            lift_grad[pl.ds(at, cols), :] = row
        return carry

    lax.fori_loop(0, rows // BACK_ROWS, conv_back, 0)

    to_smem.wait()

    def send_back(turn, carry):
        pair = partner(me, pairs, turn)
        for side in range(2):
            for slot in range(capacity):
                stage[pl.ds(side * capacity + slot, 1), :] = lift_grad[
                    pl.ds(cells[slot, 2 * pair + side], 1), :
                ]
        returning[pl.ds(2 * turn, 2)] = stage[...].astype(BF16).reshape(2, capacity, channels)
        send_pair(me, pairs, turn, returning, back, back_send, back_recv)
        return carry

    share = share_of(chip)
    mine = core * half + share
    others = pl.ds(0, chips - 1)
    rest = pl.ds(0, half - 1)

    def sum_parts():
        @pl.when(share < half)
        def _():
            pltpu.make_async_copy(gathered.at[others], gathered.at[others], part_recv).wait()
            gathered[chip] = chip_sums[share]

            def add(sender, total):
                return total + gathered[sender].astype(F32)

            sums[mine] = lax.fori_loop(0, chips, add, jnp.zeros((SHARE, channels), F32), unroll=8).astype(
                BF16
            )

            def send_sum(step, carry):
                pltpu.make_async_remote_copy(
                    src_ref=sums.at[mine],
                    dst_ref=sums.at[mine],
                    send_sem=sum_send,
                    recv_sem=sum_recv,
                    device_id=same_core(shared(chip + step, chips)),
                    device_id_type=MESH,
                ).start()
                return carry

            lax.fori_loop(1, chips, send_sum, 0)

    early = pairs // 8
    lax.fori_loop(0, early, send_back, 0)
    sum_parts()
    lax.fori_loop(early, pairs, send_back, 0)
    own_back = pltpu.make_async_copy(returning.at[my_side], back.at[my_side], local_sem.at[1])
    own_back.start()
    own_back.wait()

    def put_codes(step, carry):
        two = codes[0:code_dims, pl.ds(pl.multiple_of(step * 2 * cols, 2 * cols), 2 * cols)]
        for r in range(2):
            by_row[pl.ds(2 * step + r, code_dims, stride=rows), :] = two[
                :, r * cols : (r + 1) * cols
            ]
        return carry

    lax.fori_loop(0, rows // 2, put_codes, 0, unroll=4)
    for q in range(code_dims):
        codes_out[q] = by_row[pl.ds(q * rows, rows), :].T

    context = ctx_in[...]
    prob_sum[...] = jnp.zeros(prob_sum.shape, F32)
    ctx_sum[...] = jnp.zeros(ctx_sum.shape, F32)

    def point_grads(group, carry):
        wait_group(group, back, back_recv)
        add_points(group)
        return carry

    def add_points(group):
        prob_grad, ctx_grad = prob_sum[...], ctx_sum[...]
        for part in range(GROUP):
            turn = group * GROUP + part
            met = shared(pairs - turn, pairs)
            code = slot_code[pl.ds(met, 1), :]
            grad = back[pl.ds(2 * turn, 2)].reshape(2 * capacity, channels)
            hot = jnp.right_shift(code, 6) == pix_row
            hot_b = jnp.where(hot, 1.0, 0.0).astype(BF16)
            chosen = jnp.bitwise_and(code, bin_count - 1) == bin_row
            dots = jnp.sum(jnp.where(hot, dot(context, grad, NT), 0.0), axis=0, keepdims=True)
            by_bin = jnp.concatenate(halves(jnp.where(chosen, dots, 0.0)), axis=1)
            prob_grad = prob_grad + dot(by_bin, jnp.concatenate([hot_b, hot_b], axis=1), NT)
            spread = jnp.where(hot, slot_weight[pl.ds(met, 1), :], 0.0).astype(BF16)
            ctx_grad = ctx_grad + dot(spread, grad)
        prob_sum[...] = prob_grad
        ctx_sum[...] = ctx_grad

    wait_group(0, back, back_recv)
    add_points(0)

    late = pairs // GROUP - 2
    lax.fori_loop(1, late, point_grads, 0)

    @pl.when(share < half)
    def _():
        pltpu.make_async_copy(gathered.at[others], gathered.at[others], sum_send).wait()
        pltpu.make_async_copy(chip_sums.at[rest], chip_sums.at[rest], part_send).wait()
        pltpu.make_async_copy(chip_sums.at[rest], chip_sums.at[rest], sum_recv).wait()

    @pl.when(share >= half)
    def _():
        pltpu.make_async_copy(chip_sums, chip_sums, part_send).wait()
        pltpu.make_async_copy(chip_sums, chip_sums, sum_recv).wait()

    half_to_sibling.start()
    lax.fori_loop(late, pairs // GROUP, point_grads, 0)
    half_to_sibling.wait()
    wait_sent(returning, back_send)


def finish_kernel(
    codes, prob, prob_grad, ctx_grad, sums, ctx_weight,
    codes_out, logit_out, feature_out, conv_out, proj_out,
):
    code_dims = codes_out.shape[0]
    codes_out[...] = codes[...]
    chance, grad = prob[...], prob_grad[...]
    logit_out[...] = chance * (grad - jnp.sum(chance * grad, axis=0, keepdims=True))
    feature_out[...] = dot(ctx_grad[...].astype(BF16), ctx_weight[...], NT).astype(BF16)
    for share in range(conv_out.shape[0] // SHARE):
        conv_out[pl.ds(share * SHARE, SHARE), :] = sums[share].astype(F32)
    proj_out[...] = sums[conv_out.shape[0] // SHARE].astype(F32)[0:code_dims]


def per_device(
    features,
    depth_logits,
    ctx_weight,
    point_pixel,
    point_bin,
    segment_count,
    slot_cell,
    conv_weight,
    proj_weight,
    level_count,
    code_grad,
):
    _, count, capacity = slot_cell.shape
    code_dims, rows, cols = code_grad.shape
    bin_count, pix_count = depth_logits.shape
    feature_dims, channels = ctx_weight.shape
    pixels = point_pixel.reshape(-1, LANES)
    bins = point_bin.reshape(-1, LANES)
    all_cells = rows * cols
    owners = (9 * channels // SHARE + 2) // 2 * 2
    pairs = count // 2
    run = all_cells // FOLD
    vmem = pl.BlockSpec(memory_space=pltpu.VMEM)
    smem = pl.BlockSpec(memory_space=pltpu.SMEM)
    anywhere = pl.BlockSpec(memory_space=pl.ANY)
    wide = pltpu.VMEM(((rows + 2) * cols, 3 * channels), BF16)
    blocks = pltpu.VMEM((count, capacity, channels), BF16)
    doubled = pltpu.VMEM((12 * channels, 2 * channels), BF16)
    weight = conv_weight.reshape(9 * channels, channels)
    dma = pltpu.SemaphoreType.DMA
    cells = slot_cell[0].T
    lifted, slot_code, slot_weight, prob, context = (
        pl.pallas_call(
            lift_kernel,
            out_shape=(
                jax.ShapeDtypeStruct((all_cells, channels), BF16),
                jax.ShapeDtypeStruct((pairs, LANES), I32),
                jax.ShapeDtypeStruct((pairs, LANES), F32),
                jax.ShapeDtypeStruct((bin_count, pix_count), F32),
                jax.ShapeDtypeStruct((pix_count, channels), BF16),
            ),
            in_specs=[smem] + [vmem] * 6,
            out_specs=(vmem,) * 5,
            scratch_shapes=[
                pltpu.VMEM((pairs, 2 * capacity), I32),
                pltpu.VMEM((count, capacity), I32),
                pltpu.SMEM((count,), I32),
                pltpu.VMEM(pixels.shape, I32),
                blocks,
                blocks,
                pltpu.VMEM((run, FOLD * channels), F32),
                dma,
                dma,
                dma((pairs // GROUP,)),
            ],
            compiler_params=pltpu.CompilerParams(
                collective_id=0, has_side_effects=True, vmem_limit_bytes=VMEM_LIMIT
            ),
            name="lift",
        )(
            segment_count,
            features,
            depth_logits,
            ctx_weight,
            pixels,
            bins,
            cells,
        )
    )
    codes, prob_grad, ctx_grad, sums = pl.pallas_call(
        tile_kernel,
        out_shape=(
            jax.ShapeDtypeStruct((code_dims, cols, rows), F32),
            jax.ShapeDtypeStruct((bin_count, pix_count), F32),
            jax.ShapeDtypeStruct((pix_count, channels), F32),
            jax.ShapeDtypeStruct((owners, SHARE, channels), BF16),
        ),
        in_specs=[smem, anywhere] + [vmem] * 6 + [anywhere],
        out_specs=(vmem,) * 4,
        scratch_shapes=[
            pltpu.SMEM((capacity, count), I32),
            pltpu.VMEM((all_cells, channels), BF16),
            blocks,
            blocks,
            pltpu.VMEM(((rows + 2) * PITCH, channels), F32),
            wide,
            wide,
            pltpu.VMEM((all_cells, channels), F32),
            pltpu.VMEM((2, rows, channels), BF16),
            pltpu.VMEM((2, cols, channels), BF16),
            pltpu.VMEM((2, 8, rows, channels), BF16),
            pltpu.VMEM((2 * capacity, channels), F32),
            pltpu.VMEM((owners, SHARE, channels), F32),
            pltpu.VMEM((owners // 2, SHARE, channels), F32),
            pltpu.VMEM((owners // 2, SHARE, channels), BF16),
            pltpu.VMEM((count // 2, SHARE, channels), BF16),
            pltpu.VMEM((channels, 9 * channels), F32),
            doubled,
            doubled,
            pltpu.VMEM((16, channels), F32),
            pltpu.VMEM((8, all_cells), F32),
            pltpu.VMEM((code_dims * rows, cols), F32),
            pltpu.VMEM((8, all_cells), F32),
            dma((3,)),
            dma,
            dma((pairs // GROUP,)),
            dma((2, 8)),
            dma((2, 8)),
            dma,
            dma,
            dma,
            dma,
            dma,
            dma,
            dma,
            dma,
        ],
        compiler_params=pltpu.CompilerParams(
            collective_id=1, has_side_effects=True, vmem_limit_bytes=VMEM_LIMIT
        ),
        name="tile",
    )(
        level_count,
        lifted,
        slot_code,
        slot_weight,
        context,
        weight,
        proj_weight.T,
        code_grad.transpose(0, 2, 1),
        cells,
    )
    codes_out, grad_logits, grad_features, grad_conv, grad_proj = pl.pallas_call(
        finish_kernel,
        out_shape=(
            jax.ShapeDtypeStruct((code_dims, cols, rows), F32),
            jax.ShapeDtypeStruct((bin_count, pix_count), F32),
            jax.ShapeDtypeStruct((pix_count, feature_dims), BF16),
            jax.ShapeDtypeStruct((9 * channels, channels), F32),
            jax.ShapeDtypeStruct((code_dims, channels), F32),
        ),
        in_specs=[vmem] * 6,
        out_specs=(vmem,) * 5,
        compiler_params=pltpu.CompilerParams(vmem_limit_bytes=VMEM_LIMIT),
        name="finish",
    )(codes, prob, prob_grad, ctx_grad, sums, ctx_weight)
    return (
        codes_out.transpose(0, 2, 1),
        grad_logits,
        grad_features,
        grad_conv.reshape(conv_weight.shape),
        grad_proj.T,
    )


def solution(mesh):
    return jax.shard_map(
        per_device,
        mesh=mesh,
        in_specs=(
            P(("bx", "by"), None),
            P(None, ("bx", "by")),
            P(),
            P(("bx", "by")),
            P(("bx", "by")),
            P(("bx", "by"), None),
            P(("bx", "by"), None, None),
            P(),
            P(),
            P(),
            P(None, "bx", "by"),
        ),
        out_specs=(P(None, "bx", "by"), P(None, ("bx", "by")), P(("bx", "by"), None), P(), P()),
        check_vma=False,
    )
```

```python
import jax
import jax.numpy as jnp
from jax import lax
from jax.experimental import pallas as pl
from jax.experimental.pallas import tpu as pltpu
from jax.sharding import PartitionSpec as P

epsilon = 1e-05
MESH = pl.DeviceIdType.MESH
F32 = jnp.float32
BF16 = jnp.bfloat16
I32 = jnp.int32
VMEM_LIMIT = 60 * 2**20
NT = (((1,), (1,)), ((), ()))
TN = (((0,), (0,)), ((), ()))
LANES = 128
PITCH = 80
STRIDE = 11
AHEAD = 4
GROUP = 8
FOLD = 8
ENCODE_ROWS = 64
BACK_ROWS = 64
SPAN = 2048
SHARE = 16
DIRECTIONS = ((-1, 0), (1, 0), (0, -1), (0, 1), (-1, -1), (-1, 1), (1, -1), (1, 1))


def dot(left, right, dims=(((1,), (0,)), ((), ()))):
    return lax.dot_general(left, right, dims, preferred_element_type=F32)


def halves(value):
    high = value.astype(BF16)
    return high, (value - high.astype(F32)).astype(BF16)


def shared(index, size):
    return jnp.bitwise_and(index, size - 1)


def parted(index, size):
    return jnp.right_shift(index, size.bit_length() - 1)


def place(index):
    cols = lax.axis_size("by")
    return (parted(index, cols), shared(index, cols))


def grid_place():
    return lax.axis_index("bx"), lax.axis_index("by"), lax.axis_size("bx"), lax.axis_size("by")


def inside(dx, dy):
    bx, by, nx, ny = grid_place()
    x, y = bx + dx, by + dy
    return (x >= 0) & (x < nx) & (y >= 0) & (y < ny)


def lane_iota(rows):
    return lax.broadcasted_iota(I32, (rows, LANES), 1)


def row_iota(rows):
    return lax.broadcasted_iota(I32, (rows, LANES), 0)


def halo_copies(edges, sides, landed, send_sems, recv_sems):
    bx, by, _, _ = grid_place()
    cols = edges.shape[1]
    depth = sides.shape[1]
    first, last = pl.ds(0, 16), pl.ds(depth - 16, 16)
    pieces = (
        (edges.at[0], landed.at[0, pl.ds(0, cols)]),
        (edges.at[1], landed.at[1, pl.ds(0, cols)]),
        (sides.at[0], landed.at[2]),
        (sides.at[1], landed.at[3]),
        (sides.at[0, first], landed.at[4, first]),
        (sides.at[1, first], landed.at[5, first]),
        (sides.at[0, last], landed.at[6, first]),
        (sides.at[1, last], landed.at[7, first]),
    )
    return [
        pltpu.make_async_remote_copy(
            src_ref=source,
            dst_ref=target,
            send_sem=send_sems.at[way],
            recv_sem=recv_sems.at[way],
            device_id=(bx + dx, by + dy),
            device_id_type=MESH,
        )
        for way, ((dx, dy), (source, target)) in enumerate(zip(DIRECTIONS, pieces))
    ]


def start_halo(copies):
    for (dx, dy), copy in zip(DIRECTIONS, copies):
        pl.when(inside(dx, dy))(copy.start)


def finish_halo(copies, landed, field, rows, cols):
    low = (rows + 1) * PITCH

    def lay(way):
        if way == 0:
            field[pl.ds(low + 8, cols), :] = landed[0, 0:cols].astype(F32)
        elif way == 1:
            field[pl.ds(8, cols), :] = landed[1, 0:cols].astype(F32)
        elif way == 2:
            field[pl.ds(PITCH + 8 + cols, rows, stride=PITCH), :] = landed[2].astype(F32)
        elif way == 3:
            field[pl.ds(PITCH + 7, rows, stride=PITCH), :] = landed[3].astype(F32)
        elif way == 4:
            field[pl.ds(low + 8 + cols, 1), :] = landed[4, 0:16].astype(F32)[0:1]
        elif way == 5:
            field[pl.ds(low + 7, 1), :] = landed[5, 0:16].astype(F32)[0:1]
        elif way == 6:
            field[pl.ds(8 + cols, 1), :] = landed[6, 0:16].astype(F32)[15:16]
        else:
            field[pl.ds(7, 1), :] = landed[7, 0:16].astype(F32)[15:16]

    for way, ((dx, dy), copy) in enumerate(zip(DIRECTIONS, copies)):

        def arrive(way=way, copy=copy):
            copy.wait_recv()
            lay(way)

        pl.when(inside(-dx, -dy))(arrive)
        pl.when(inside(dx, dy))(copy.wait_send)


def clear_border(field, rows, cols):
    channels = field.shape[1]
    zeros = jnp.zeros((PITCH, channels), F32)
    field[pl.ds(0, PITCH), :] = zeros
    field[pl.ds((rows + 1) * PITCH, PITCH), :] = zeros
    for column in (7, 8 + cols):
        field[pl.ds(PITCH + column, rows, stride=PITCH), :] = jnp.zeros((rows, channels), F32)


def fill_borders(field, edges, sides, rows, cols):
    sides[0] = field[pl.ds(PITCH + 8, rows, stride=PITCH), :].astype(BF16)
    sides[1] = field[pl.ds(PITCH + 7 + cols, rows, stride=PITCH), :].astype(BF16)
    edges[0] = field[pl.ds(PITCH + 8, cols), :].astype(BF16)
    edges[1] = field[pl.ds(rows * PITCH + 8, cols), :].astype(BF16)


def spread_columns(field, wide, rows, cols):
    channels = field.shape[1]

    def row(x, carry):
        base = pl.multiple_of(x * PITCH, 8)
        at = pl.ds(pl.multiple_of(x * cols, cols), cols)
        for shift in range(3):
            wide[at, pl.ds(shift * channels, channels)] = field[
                pl.ds(base + 7 + shift, cols), :
            ].astype(BF16)
        return carry

    lax.fori_loop(0, rows + 2, row, 0, unroll=5)


def conv_rows(wide, weight, step, rows, cols):
    channels = weight.shape[1] // 2
    window = jnp.concatenate(
        [
            jnp.concatenate(
                [
                    wide[pl.ds(pl.multiple_of((step * rows + r + tap) * cols, cols), cols), :]
                    for r in range(0, rows, 2)
                ],
                axis=0,
            )
            for tap in range(4)
        ],
        axis=1,
    )
    both = dot(window, weight[...])
    return [
        both[(r // 2) * cols : (r // 2 + 1) * cols, (r % 2) * channels : (r % 2 + 1) * channels]
        for r in range(rows)
    ]


def double_weight(target, tap_weight, depth, channels):
    for tap in range(4):
        at = pl.ds(tap * depth, depth)
        for half in range(2):
            inner = tap - half
            lane = pl.ds(half * channels, channels)
            if 0 <= inner < 3:
                for third in range(3):
                    target[pl.ds(tap * depth + third * channels, channels), lane] = tap_weight(
                        inner, third
                    )
            else:
                target[at, lane] = jnp.zeros((depth, channels), BF16)


def position():
    count = lax.axis_size("bx") * lax.axis_size("by")
    return lax.axis_index("bx") * lax.axis_size("by") + lax.axis_index("by"), count


def greet_all(me, count):
    barrier = pltpu.get_barrier_semaphore()

    def greet(step, carry):
        pl.semaphore_signal(
            barrier, inc=1, device_id=place(shared(me + step, count)), device_id_type=MESH
        )
        return carry

    even = 1 + (count - 1) // 8 * 8
    lax.fori_loop(1, even, greet, 0, unroll=8)
    for step in range(even, count):
        greet(step, 0)
    return barrier


def partner(me, pairs, step):
    return shared(parted(me, 2) + step * STRIDE, pairs)


def source(me, pairs, step):
    return shared(parted(me, 2) + pairs * STRIDE - step * STRIDE, pairs)


def send_pair(me, pairs, step, leaving, landing, sent, received):
    pair = partner(me, pairs, step)
    for side in range(2):
        tile = 2 * pair + side

        @pl.when(tile != me)
        def _(side=side, tile=tile):
            pltpu.make_async_remote_copy(
                src_ref=leaving.at[2 * step + side],
                dst_ref=landing.at[2 * step + shared(me, 2)],
                send_sem=sent,
                recv_sem=received.at[parted(step, GROUP)],
                device_id=place(tile),
                device_id_type=MESH,
            ).start()


def wait_group(group, landing, received):
    alone = isinstance(group, int) and group == 0
    blocks = landing.at[pl.ds(0, 2 * GROUP - alone)]
    pltpu.make_async_copy(blocks, blocks, received.at[group]).wait()


def wait_sent(leaving, sent):
    others = pl.ds(0, leaving.shape[0] - 1)
    pltpu.make_async_copy(leaving.at[others], leaving.at[others], sent).wait()


def lift_kernel(
    counts, features, logits, ctx_weight, pixels, bins, cells_in,
    lifted, slot_code, slot_weight, prob_out, ctx_out,
    cells_two, cells_v, starts, point_code, outgoing, arrived, pooled,
    local_sem, send_sem, recv_sem,
):
    me, count = position()
    pairs = count // 2
    my_side = shared(me, 2)
    capacity = cells_in.shape[0]
    all_cells, channels = lifted.shape
    bin_count, pix_count = logits.shape
    barrier = greet_all(me, count)

    context = dot(features[...], ctx_weight[...]).astype(BF16)
    raw = logits[...]
    shifted = jnp.exp(raw - jnp.max(raw, axis=0, keepdims=True))
    prob = shifted / jnp.sum(shifted, axis=0, keepdims=True)
    prob_out[...] = prob
    ctx_out[...] = context
    prob_pair = jnp.concatenate(halves(prob), axis=1)
    ctx_pair = jnp.concatenate([context, context], axis=0)
    point_code[...] = pixels[...] * bin_count + bins[...]
    last_row = pixels.shape[0] - 1

    def start_of(tile, begin):
        starts[tile] = begin
        return begin + counts[0, tile]

    lax.fori_loop(0, count, start_of, 0, unroll=8)
    lane = lane_iota(1)
    pix_row = row_iota(pix_count)
    bin_row = row_iota(bin_count)

    def codes_of(pair):
        sides_codes = []
        for side in range(2):
            tile = 2 * pair + side
            begin = starts[tile]
            offset = jnp.bitwise_and(begin, LANES - 1)
            row = jnp.right_shift(begin, 7)
            here = point_code[pl.ds(jnp.minimum(row, last_row), 1), :]
            after = point_code[pl.ds(jnp.minimum(row + 1, last_row), 1), :]
            turned = pltpu.roll(
                jnp.where(lane >= offset, here, after),
                jnp.bitwise_and(side * capacity + LANES - offset, LANES - 1),
                axis=1,
            )
            sides_codes.append(jnp.where(lane - side * capacity < counts[0, tile], turned, -1))
        return jnp.where(lane < capacity, sides_codes[0], sides_codes[1])

    pl.semaphore_wait(barrier, count - 1)

    def lift(step, carry):
        found = [codes_of(partner(me, pairs, step * GROUP + part)) for part in range(GROUP)]
        for part in range(GROUP):
            slot_code[pl.ds(step * GROUP + part, 1), :] = found[part]
        code = jnp.concatenate(found, axis=1)
        wide_rows = lax.broadcasted_iota(I32, (pix_count, GROUP * LANES), 0)
        hot = jnp.right_shift(code, 6) == wide_rows
        hot_b = jnp.where(hot, 1.0, 0.0).astype(BF16)
        picked = dot(prob_pair, jnp.concatenate([hot_b, hot_b], axis=0))
        chosen = jnp.bitwise_and(code, bin_count - 1) == wide_rows[:bin_count]
        point_weight = jnp.sum(jnp.where(chosen, picked, 0.0), axis=0, keepdims=True)
        for part in range(GROUP):
            slot_weight[pl.ds(step * GROUP + part, 1), :] = point_weight[
                :, part * LANES : (part + 1) * LANES
            ]
        spread = jnp.concatenate(halves(jnp.where(hot, point_weight, 0.0)), axis=0)
        value = dot(spread, ctx_pair, TN).astype(BF16)
        outgoing[pl.ds(2 * GROUP * step, 2 * GROUP)] = value.reshape(
            2 * GROUP, capacity, channels
        )
        pl.when(step < AHEAD)(lambda: send_group(step))
        return carry

    def send_group(step):
        def send(turn, carry):
            send_pair(me, pairs, turn, outgoing, arrived, send_sem, recv_sem)
            return carry

        lax.fori_loop(step * GROUP, (step + 1) * GROUP, send, 0)

    lax.fori_loop(0, pairs // GROUP, lift, 0)
    own = pltpu.make_async_copy(outgoing.at[my_side], arrived.at[my_side], local_sem)
    own.start()

    cells_v[0:count] = cells_in[...].T
    cells_two[...] = jnp.concatenate(
        [cells_v[pl.ds(side, pairs, stride=2), :] for side in range(2)], axis=1
    )
    run = all_cells // FOLD
    run_shift = run.bit_length() - 1
    run_row = row_iota(run)
    own.wait()

    pooled[...] = jnp.zeros(pooled.shape, F32)
    wait_group(0, arrived, recv_sem)

    def pool(group, carry):
        pl.when(group + AHEAD < pairs // GROUP)(lambda: send_group(group + AHEAD))
        pl.when(group > 0)(lambda: wait_group(group, arrived, recv_sem))
        hot_cells, folded = [], []
        for part in range(GROUP):
            turn = group * GROUP + part
            cell = cells_two[pl.ds(source(me, pairs, turn), 1), :]
            hot_cells.append(
                jnp.where(jnp.bitwise_and(cell, run - 1) == run_row, 1.0, 0.0).astype(BF16)
            )
            which = jnp.broadcast_to(jnp.right_shift(cell, run_shift), (LANES, LANES)).T
            value = arrived[pl.ds(2 * turn, 2)].reshape(2 * capacity, channels).astype(F32)
            folded.append(
                jnp.concatenate(
                    [jnp.where(which == fold, value, 0.0).astype(BF16) for fold in range(FOLD)],
                    axis=1,
                )
            )
        pooled[...] += dot(
            jnp.concatenate(hot_cells, axis=1), jnp.concatenate(folded, axis=0)
        )
        return carry

    lax.fori_loop(0, pairs // GROUP, pool, 0)
    for fold in range(FOLD):
        lifted[pl.ds(fold * run, run), :] = pooled[:, pl.ds(fold * channels, channels)].astype(BF16)
    wait_sent(outgoing, send_sem)


def tile_kernel(
    levels, lifted_in, slot_code, slot_weight, ctx_in, weight, proj, code_grad, cells_in,
    codes_out, prob_sum, ctx_sum, sums,
    cells, lifted, returning, back, field, wide, wide_grad, lift_grad, sides, edges, landed, stage,
    parts, paired, chip_sums, gathered, flipped, weight_two, back_two, proj_two, slopes_in,
    by_row, codes,
    local_sem, back_send, back_recv, halo_send, halo_recv,
    pair_send, pair_recv, part_send, part_recv, sum_send, sum_recv, half_send, half_recv,
):
    me, count = position()
    pairs = count // 2
    my_side = shared(me, 2)
    capacity = cells.shape[0]
    channels = lifted.shape[1]
    fetch = pltpu.make_async_copy(lifted_in, lifted, local_sem.at[2])
    fetch.start()
    bin_count, pix_count = prob_sum.shape
    cols = edges.shape[1]
    rows = sides.shape[1]
    code_dims = levels.shape[0]
    depth = 3 * channels
    owners = parts.shape[0]
    full_shares = 9 * channels // SHARE
    all_cells = rows * cols
    barrier = greet_all(me, count)
    to_smem = pltpu.make_async_copy(cells_in, cells, local_sem.at[0])
    to_smem.start()
    pix_row = row_iota(pix_count)
    bin_row = row_iota(bin_count)
    clear_border(field, rows, cols)
    fetch.wait()

    def load_row(x, carry):
        field[pl.ds(pl.multiple_of((x + 1) * PITCH + 8, 8), cols), :] = lifted[
            pl.ds(pl.multiple_of(x * cols, cols), cols), :
        ].astype(F32)
        return carry

    lax.fori_loop(0, rows, load_row, 0, unroll=4)
    fill_borders(field, edges, sides, rows, cols)
    pl.semaphore_wait(barrier, count - 1)
    first = halo_copies(edges, sides, landed.at[0], halo_send.at[0], halo_recv.at[0])
    start_halo(first)
    double_weight(
        weight_two,
        lambda tap, third: weight[pl.ds(tap * depth + third * channels, channels), :],
        depth,
        channels,
    )
    double_weight(
        back_two,
        lambda tap, third: weight[pl.ds((2 - tap) * depth + (2 - third) * channels, channels), :]
        .astype(F32)
        .T.astype(BF16),
        depth,
        channels,
    )
    proj_rows = proj[...].astype(F32)
    proj_two[...] = jnp.zeros(proj_two.shape, F32)
    proj_two[0:code_dims] = proj_rows
    proj_two[8 : 8 + code_dims] = proj_rows
    slopes_in[...] = jnp.zeros(slopes_in.shape, F32)
    for q in range(code_dims):
        by_row[pl.ds(q * rows, rows), :] = code_grad[q].T

    def take_slopes(step, carry):
        two = [by_row[pl.ds(2 * step + r, code_dims, stride=rows), :] for r in range(2)]
        at = pl.ds(pl.multiple_of(step * 2 * cols, 2 * cols), 2 * cols)
        slopes_in[0:code_dims, at] = jnp.concatenate(two, axis=1)
        return carry

    lax.fori_loop(0, rows // 2, take_slopes, 0, unroll=4)
    finish_halo(first, landed.at[0], field, rows, cols)
    spread_columns(field, wide, rows, cols)

    half_levels = jnp.zeros((8, 1), F32)
    for q in range(code_dims):
        half_levels = half_levels + jnp.where(
            lax.broadcasted_iota(I32, (8, 1), 0) == q, (levels[q].astype(F32) - 1.0) * 0.5, 0.0
        )
    proj_both_rows = proj_two[...].astype(BF16)
    block = ENCODE_ROWS * cols

    def encode(step, proj_sum):
        origin = pl.multiple_of(step * block, block)
        conv_out = jnp.concatenate(conv_rows(wide, weight_two, step, ENCODE_ROWS, cols), axis=0)
        inv_rms = lax.rsqrt(jnp.mean(conv_out * conv_out, axis=-1, keepdims=True) + epsilon)
        normed = conv_out * inv_rms
        gate = 0.5 + 0.5 * jnp.tanh(0.5 * normed)
        active = normed * gate
        hidden = active.astype(BF16)
        squash = jnp.tanh(dot(proj_both_rows, hidden, NT)[:8])
        codes[:, pl.ds(origin, block)] = half_levels * squash
        slope = slopes_in[:, pl.ds(origin, block)] * half_levels * (1.0 - squash * squash)
        slope_high = slope.astype(BF16).astype(F32)
        slope_pair = jnp.concatenate([slope_high, slope - slope_high], axis=0).astype(BF16)
        proj_both = dot(slope_pair, hidden)
        hidden_grad = dot(slope_pair, proj_both_rows, TN)
        norm_grad = hidden_grad * (gate + active * (1.0 - gate))
        mixed = jnp.mean(norm_grad * normed, axis=-1, keepdims=True)
        conv_grad = inv_rms * (norm_grad - normed * mixed)
        for r in range(ENCODE_ROWS):
            at = pl.multiple_of((step * ENCODE_ROWS + r + 1) * PITCH + 8, 8)
            field[pl.ds(at, cols), :] = conv_grad[r * cols : (r + 1) * cols]
        wide_grad[pl.ds(origin + cols, block), pl.ds(channels, channels)] = conv_grad.astype(BF16)
        return proj_sum + proj_both[:8] + proj_both[8:]

    proj_sum = lax.fori_loop(0, rows // ENCODE_ROWS, encode, jnp.zeros((8, channels), F32))
    fill_borders(field, edges, sides, rows, cols)
    second = halo_copies(edges, sides, landed.at[1], halo_send.at[1], halo_recv.at[1])
    start_halo(second)

    flipped[...] = jnp.zeros(flipped.shape, F32)

    def weight_grad(step, carry):
        origin = pl.multiple_of(step * SPAN, SPAN)
        grad_t = wide_grad[pl.ds(origin + cols, SPAN), pl.ds(channels, channels)].T
        for tap in range(3):
            flipped[:, pl.ds(tap * depth, depth)] += dot(
                grad_t, wide[pl.ds(origin + tap * cols, SPAN), :]
            )
        return carry

    lax.fori_loop(0, all_cells // SPAN, weight_grad, 0)
    for tap in range(9):
        parts[pl.ds(tap * (channels // SHARE), channels // SHARE)] = flipped[
            :, pl.ds(tap * channels, channels)
        ].T.reshape(channels // SHARE, SHARE, channels)
    parts[full_shares] = jnp.concatenate(
        [proj_sum, jnp.zeros((SHARE - 8, channels), F32)], axis=0
    )
    for spare in range(full_shares + 1, owners):
        parts[spare] = jnp.zeros((SHARE, channels), F32)

    chips, half = count // 2, owners // 2
    bx, by, _, row_devices = grid_place()
    core = shared(bx, 2)
    chip = parted(bx, 2) * row_devices + by
    to_sibling = pltpu.make_async_remote_copy(
        src_ref=parts.at[pl.ds((1 - core) * half, half)],
        dst_ref=paired,
        send_sem=pair_send,
        recv_sem=pair_recv,
        device_id=(bx + 1 - 2 * core, by),
        device_id_type=MESH,
    )
    to_sibling.start()
    my_half = sums.at[pl.ds(core * half, half)]
    half_to_sibling = pltpu.make_async_remote_copy(
        src_ref=my_half,
        dst_ref=my_half,
        send_sem=half_send,
        recv_sem=half_recv,
        device_id=(bx + 1 - 2 * core, by),
        device_id_type=MESH,
    )

    def same_core(one):
        return (2 * parted(one, row_devices) + core, shared(one, row_devices))

    def share_of(one):
        return shared(one * STRIDE, chips)

    def send_part(step, carry):
        target = shared(chip + step, chips)
        share = share_of(target)

        @pl.when(share < half)
        def _():
            pltpu.make_async_remote_copy(
                src_ref=chip_sums.at[share],
                dst_ref=gathered.at[chip],
                send_sem=part_send,
                recv_sem=part_recv,
                device_id=same_core(target),
                device_id_type=MESH,
            ).start()

        return carry

    finish_halo(second, landed.at[1], field, rows, cols)
    spread_columns(field, wide_grad, rows, cols)
    to_sibling.wait()
    chip_sums[...] = (parts[pl.ds(core * half, half)] + paired[...]).astype(BF16)
    lax.fori_loop(1, chips, send_part, 0)

    def conv_back(step, carry):
        for r, row in enumerate(conv_rows(wide_grad, back_two, step, BACK_ROWS, cols)):
            at = pl.multiple_of((step * BACK_ROWS + r) * cols, cols)
            lift_grad[pl.ds(at, cols), :] = row
        return carry

    lax.fori_loop(0, rows // BACK_ROWS, conv_back, 0)

    to_smem.wait()

    def send_back(turn, carry):
        pair = partner(me, pairs, turn)
        for side in range(2):
            for slot in range(capacity):
                stage[pl.ds(side * capacity + slot, 1), :] = lift_grad[
                    pl.ds(cells[slot, 2 * pair + side], 1), :
                ]
        returning[pl.ds(2 * turn, 2)] = stage[...].astype(BF16).reshape(2, capacity, channels)
        send_pair(me, pairs, turn, returning, back, back_send, back_recv)
        return carry

    share = share_of(chip)
    mine = core * half + share
    others = pl.ds(0, chips - 1)
    rest = pl.ds(0, half - 1)

    def sum_parts():
        @pl.when(share < half)
        def _():
            pltpu.make_async_copy(gathered.at[others], gathered.at[others], part_recv).wait()
            gathered[chip] = chip_sums[share]

            def add(sender, total):
                return total + gathered[sender].astype(F32)

            sums[mine] = lax.fori_loop(0, chips, add, jnp.zeros((SHARE, channels), F32), unroll=8).astype(
                BF16
            )

            def send_sum(step, carry):
                pltpu.make_async_remote_copy(
                    src_ref=sums.at[mine],
                    dst_ref=sums.at[mine],
                    send_sem=sum_send,
                    recv_sem=sum_recv,
                    device_id=same_core(shared(chip + step, chips)),
                    device_id_type=MESH,
                ).start()
                return carry

            lax.fori_loop(1, chips, send_sum, 0)

    early = pairs // 8
    lax.fori_loop(0, early, send_back, 0)
    sum_parts()
    lax.fori_loop(early, pairs, send_back, 0)
    own_back = pltpu.make_async_copy(returning.at[my_side], back.at[my_side], local_sem.at[1])
    own_back.start()
    own_back.wait()

    def put_codes(step, carry):
        two = codes[0:code_dims, pl.ds(pl.multiple_of(step * 2 * cols, 2 * cols), 2 * cols)]
        for r in range(2):
            by_row[pl.ds(2 * step + r, code_dims, stride=rows), :] = two[
                :, r * cols : (r + 1) * cols
            ]
        return carry

    lax.fori_loop(0, rows // 2, put_codes, 0, unroll=4)
    for q in range(code_dims):
        codes_out[q] = by_row[pl.ds(q * rows, rows), :].T

    context = ctx_in[...]
    prob_sum[...] = jnp.zeros(prob_sum.shape, F32)
    ctx_sum[...] = jnp.zeros(ctx_sum.shape, F32)

    def point_grads(group, carry):
        wait_group(group, back, back_recv)
        add_points(group)
        return carry

    def add_points(group):
        prob_grad, ctx_grad = prob_sum[...], ctx_sum[...]
        for part in range(GROUP):
            turn = group * GROUP + part
            met = shared(pairs - turn, pairs)
            code = slot_code[pl.ds(met, 1), :]
            grad = back[pl.ds(2 * turn, 2)].reshape(2 * capacity, channels)
            hot = jnp.right_shift(code, 6) == pix_row
            hot_b = jnp.where(hot, 1.0, 0.0).astype(BF16)
            chosen = jnp.bitwise_and(code, bin_count - 1) == bin_row
            dots = jnp.sum(jnp.where(hot, dot(context, grad, NT), 0.0), axis=0, keepdims=True)
            by_bin = jnp.concatenate(halves(jnp.where(chosen, dots, 0.0)), axis=1)
            prob_grad = prob_grad + dot(by_bin, jnp.concatenate([hot_b, hot_b], axis=1), NT)
            spread = jnp.where(hot, slot_weight[pl.ds(met, 1), :], 0.0).astype(BF16)
            ctx_grad = ctx_grad + dot(spread, grad)
        prob_sum[...] = prob_grad
        ctx_sum[...] = ctx_grad

    wait_group(0, back, back_recv)
    add_points(0)

    late = pairs // GROUP - 2
    lax.fori_loop(1, late, point_grads, 0)

    @pl.when(share < half)
    def _():
        pltpu.make_async_copy(gathered.at[others], gathered.at[others], sum_send).wait()
        pltpu.make_async_copy(chip_sums.at[rest], chip_sums.at[rest], part_send).wait()
        pltpu.make_async_copy(chip_sums.at[rest], chip_sums.at[rest], sum_recv).wait()

    @pl.when(share >= half)
    def _():
        pltpu.make_async_copy(chip_sums, chip_sums, part_send).wait()
        pltpu.make_async_copy(chip_sums, chip_sums, sum_recv).wait()

    half_to_sibling.start()
    lax.fori_loop(late, pairs // GROUP, point_grads, 0)
    half_to_sibling.wait()
    wait_sent(returning, back_send)


def finish_kernel(
    codes, prob, prob_grad, ctx_grad, sums, ctx_weight,
    codes_out, logit_out, feature_out, conv_out, proj_out,
):
    code_dims = codes_out.shape[0]
    codes_out[...] = codes[...]
    chance, grad = prob[...], prob_grad[...]
    logit_out[...] = chance * (grad - jnp.sum(chance * grad, axis=0, keepdims=True))
    feature_out[...] = dot(ctx_grad[...].astype(BF16), ctx_weight[...], NT).astype(BF16)
    for share in range(conv_out.shape[0] // SHARE):
        conv_out[pl.ds(share * SHARE, SHARE), :] = sums[share].astype(F32)
    proj_out[...] = sums[conv_out.shape[0] // SHARE].astype(F32)[0:code_dims]


def per_device(
    features,
    depth_logits,
    ctx_weight,
    point_pixel,
    point_bin,
    segment_count,
    slot_cell,
    conv_weight,
    proj_weight,
    level_count,
    code_grad,
):
    _, count, capacity = slot_cell.shape
    code_dims, rows, cols = code_grad.shape
    bin_count, pix_count = depth_logits.shape
    feature_dims, channels = ctx_weight.shape
    pixels = point_pixel.reshape(-1, LANES)
    bins = point_bin.reshape(-1, LANES)
    all_cells = rows * cols
    owners = (9 * channels // SHARE + 2) // 2 * 2
    pairs = count // 2
    run = all_cells // FOLD
    vmem = pl.BlockSpec(memory_space=pltpu.VMEM)
    smem = pl.BlockSpec(memory_space=pltpu.SMEM)
    anywhere = pl.BlockSpec(memory_space=pl.ANY)
    wide = pltpu.VMEM(((rows + 2) * cols, 3 * channels), BF16)
    blocks = pltpu.VMEM((count, capacity, channels), BF16)
    doubled = pltpu.VMEM((12 * channels, 2 * channels), BF16)
    weight = conv_weight.reshape(9 * channels, channels)
    dma = pltpu.SemaphoreType.DMA
    cells = slot_cell[0].T
    lifted, slot_code, slot_weight, prob, context = (
        pl.pallas_call(
            lift_kernel,
            out_shape=(
                jax.ShapeDtypeStruct((all_cells, channels), BF16),
                jax.ShapeDtypeStruct((pairs, LANES), I32),
                jax.ShapeDtypeStruct((pairs, LANES), F32),
                jax.ShapeDtypeStruct((bin_count, pix_count), F32),
                jax.ShapeDtypeStruct((pix_count, channels), BF16),
            ),
            in_specs=[smem] + [vmem] * 6,
            out_specs=(vmem,) * 5,
            scratch_shapes=[
                pltpu.VMEM((pairs, 2 * capacity), I32),
                pltpu.VMEM((count + 8, capacity), I32),
                pltpu.SMEM((count,), I32),
                pltpu.VMEM(pixels.shape, I32),
                blocks,
                blocks,
                pltpu.VMEM((run, FOLD * channels), F32),
                dma,
                dma,
                dma((pairs // GROUP,)),
            ],
            compiler_params=pltpu.CompilerParams(
                collective_id=0, has_side_effects=True, vmem_limit_bytes=VMEM_LIMIT
            ),
            name="lift",
        )(
            segment_count,
            features,
            depth_logits,
            ctx_weight,
            pixels,
            bins,
            cells,
        )
    )
    codes, prob_grad, ctx_grad, sums = pl.pallas_call(
        tile_kernel,
        out_shape=(
            jax.ShapeDtypeStruct((code_dims, cols, rows), F32),
            jax.ShapeDtypeStruct((bin_count, pix_count), F32),
            jax.ShapeDtypeStruct((pix_count, channels), F32),
            jax.ShapeDtypeStruct((owners, SHARE, channels), BF16),
        ),
        in_specs=[smem, anywhere] + [vmem] * 6 + [anywhere],
        out_specs=(vmem,) * 4,
        scratch_shapes=[
            pltpu.SMEM((capacity, count), I32),
            pltpu.VMEM((all_cells, channels), BF16),
            blocks,
            blocks,
            pltpu.VMEM(((rows + 2) * PITCH, channels), F32),
            wide,
            wide,
            pltpu.VMEM((all_cells, channels), F32),
            pltpu.VMEM((2, rows, channels), BF16),
            pltpu.VMEM((2, cols, channels), BF16),
            pltpu.VMEM((2, 8, rows, channels), BF16),
            pltpu.VMEM((2 * capacity, channels), F32),
            pltpu.VMEM((owners, SHARE, channels), F32),
            pltpu.VMEM((owners // 2, SHARE, channels), F32),
            pltpu.VMEM((owners // 2, SHARE, channels), BF16),
            pltpu.VMEM((count // 2, SHARE, channels), BF16),
            pltpu.VMEM((channels, 9 * channels), F32),
            doubled,
            doubled,
            pltpu.VMEM((16, channels), F32),
            pltpu.VMEM((8, all_cells), F32),
            pltpu.VMEM(((code_dims + 1) * rows, cols), F32),
            pltpu.VMEM((8, all_cells), F32),
            dma((3,)),
            dma,
            dma((pairs // GROUP,)),
            dma((2, 8)),
            dma((2, 8)),
            dma,
            dma,
            dma,
            dma,
            dma,
            dma,
            dma,
            dma,
        ],
        compiler_params=pltpu.CompilerParams(
            collective_id=1, has_side_effects=True, vmem_limit_bytes=VMEM_LIMIT
        ),
        name="tile",
    )(
        level_count,
        lifted,
        slot_code,
        slot_weight,
        context,
        weight,
        proj_weight.T,
        code_grad.transpose(0, 2, 1),
        cells,
    )
    codes_out, grad_logits, grad_features, grad_conv, grad_proj = pl.pallas_call(
        finish_kernel,
        out_shape=(
            jax.ShapeDtypeStruct((code_dims, cols, rows), F32),
            jax.ShapeDtypeStruct((bin_count, pix_count), F32),
            jax.ShapeDtypeStruct((pix_count, feature_dims), BF16),
            jax.ShapeDtypeStruct((9 * channels, channels), F32),
            jax.ShapeDtypeStruct((code_dims, channels), F32),
        ),
        in_specs=[vmem] * 6,
        out_specs=(vmem,) * 5,
        compiler_params=pltpu.CompilerParams(vmem_limit_bytes=VMEM_LIMIT),
        name="finish",
    )(codes, prob, prob_grad, ctx_grad, sums, ctx_weight)
    return (
        codes_out.transpose(0, 2, 1),
        grad_logits,
        grad_features,
        grad_conv.reshape(conv_weight.shape),
        grad_proj.T,
    )


def solution(mesh):
    return jax.shard_map(
        per_device,
        mesh=mesh,
        in_specs=(
            P(("bx", "by"), None),
            P(None, ("bx", "by")),
            P(),
            P(("bx", "by")),
            P(("bx", "by")),
            P(("bx", "by"), None),
            P(("bx", "by"), None, None),
            P(),
            P(),
            P(),
            P(None, "bx", "by"),
        ),
        out_specs=(P(None, "bx", "by"), P(None, ("bx", "by")), P(("bx", "by"), None), P(), P()),
        check_vma=False,
    )
```
